256 devices in a mesh: dp: 8 (over y_lo, x), space: 32 (over y_hi, z, core).
Axes of the slice: x: 4, y: 4 (y_hi: 2, y_lo: 2; y = y_hi * 2 + y_lo), z: 8, core: 2. Of those that a mesh axis runs over, the one named last changes fastest.
Arguments:
- fields: bfloat16 [8, 128, 48, 48, 128], P('dp', 'space'), may hold values from -6 to 6
- cotangent: bfloat16 [8, 128, 48, 48, 128], P('dp', 'space')
- neighbours: int32 [128, 4], replicated, may hold values from 0 to 127, as said below
- rotations: int32 [128, 4], replicated, may hold values from 0 to 3
- tile_counts: int32 [32], replicated, may hold values from 1 to 4, as said below
- depth_kernel: float32 [3, 3, 128], replicated, may hold values from -2 to 2
- depth_bias: float32 [128], replicated, may hold values from -3 to 3
- norm_gain: float32 [128], replicated, may hold values from 0.5 to 1.5
- norm_bias: float32 [128], replicated, may hold values from -3 to 3
- weight_in: bfloat16 [128, 512], replicated, may hold values from -0.5 to 0.5
- bias_in: float32 [512], replicated, may hold values from -3 to 3
- weight_out: bfloat16 [512, 128], replicated, may hold values from -0.25 to 0.25
- bias_out: float32 [128], replicated, may hold values from -3 to 3
- layer_scale: float32 [128], replicated, may hold values from 0.5 to 1.5
Outputs:
- blocks_out: bfloat16 [8, 128, 48, 48, 128], P('dp', 'space')
- grad_weight_in: float32 [128, 512], replicated
- grad_weight_out: float32 [512, 128], replicated
- grad_bias_in: float32 [512], replicated
- grad_channel: float32 [14, 128], replicated
The draws below stay inside these ranges and needn't reach their ends.
Inputs may be any that keep to these rules, and one draw needn't show every extreme that they name: `neighbours`: every entry names a live slot. The 16 entries of the slots of one index of space name slots held by 16 different indices of space, so at most one line goes from one device to another. `tile_counts`: some index of space holds exactly 4 live tiles.
All inputs are finite; a program needn't handle non-finite values.
Results may differ from the reference program's by a relative error of at most 0.0065.
Values may be sent and summed in bfloat16 or wider, within the bound.
A program may use at most 128 MiB of HBM per device.

```python
import math
import jax
import jax.numpy as jnp
import numpy as np
from jax import lax

C = 128
HID = 512
P_SIZE = 48
SLOTS = 4
SAMPLES = 8
SLOTS_ALL = 128
N_SPACE = 32


def device_loads(key):
    first, second = jax.random.split(key)
    counts = jax.random.randint(first, (N_SPACE,), 1, SLOTS + 1)
    chosen = jax.random.randint(second, (), 0, N_SPACE)
    return jnp.where(jnp.arange(N_SPACE) == chosen, SLOTS, counts).astype(jnp.int32)


def draw_tile_counts(key, part):
    counts = device_loads(key)
    return counts


def draw_neighbours(key, part):
    counts = device_loads(key)
    key = jax.random.fold_in(key, 7)
    first, second = jax.random.split(key)
    device_keys = jax.random.split(first, N_SPACE)
    orders = jax.vmap(lambda single: jax.random.permutation(single, N_SPACE))(device_keys)[:, :4 * SLOTS]
    owners = (jnp.arange(N_SPACE)[:, None] + orders) % N_SPACE
    picks = jax.random.randint(second, (N_SPACE, 4 * SLOTS), 0, 1 << 20)
    slots = picks % counts[owners]
    return (owners * SLOTS + slots).reshape(SLOTS_ALL, 4).astype(jnp.int32)


def draw_cotangent(key, part):
    key = jax.random.fold_in(key, 5)
    first = jax.random.fold_in(key, 0)
    ramp = 1.0 + 2.0 * jnp.arange(SLOTS_ALL, dtype=jnp.float32) / max(SLOTS_ALL - 1, 1)
    ramp = ramp.reshape(1, SLOTS_ALL, 1, 1, 1)
    values = jax.random.normal(first, (SAMPLES, SLOTS_ALL, P_SIZE, P_SIZE, C), jnp.float32) * ramp
    return jnp.clip(values, -12.0, 12.0).astype(jnp.bfloat16)


def with_ends(entries, key, least, largest):
    extent = entries.shape
    spot = [jax.random.randint(jax.random.fold_in(key, axis), (), 0, extent[axis]) for axis in range(len(extent))]
    entries = entries.at[tuple(spot)].set(least)
    longest = extent.index(max(extent))
    spot[longest] = (spot[longest] + 1) % extent[longest]
    return entries.at[tuple(spot)].set(largest)


def steps_of(rng, extent, shards, smallest, high):
    loudness = 1.0
    for position, blocks in shards:
        steps = jax.random.uniform(jax.random.fold_in(jax.random.fold_in(rng, 6), position), (blocks,), jnp.float32, smallest / len(shards), high / len(shards))
        loudness = loudness * jnp.repeat(jnp.exp(steps), extent[position] // blocks).reshape((-1,) + (1,) * (len(extent) - 1 - position))
    return loudness


def scatter_about(own_key, extent, deviation, most, pieces=(), held_as=jnp.bfloat16):
    array = jax.random.normal(own_key, extent, jnp.float32) * deviation
    if len(pieces) > 0:
        array = steps_of(own_key, extent, pieces, -0.22, 0.18) * array
    return jnp.clip(array, min=-most, max=most).astype(held_as)


def setup_inputs(seed: int = 0) -> dict:
    splits = jax.random.split(jax.random.key(seed), 15)
    fields = scatter_about(splits[0], (SAMPLES, SLOTS_ALL, P_SIZE, P_SIZE, C), 1.0, 6.0, ((0, 8), (1, 32)))
    cotangent = draw_cotangent(jax.random.fold_in(splits[14], 71), 0)
    neighbours = draw_neighbours(jax.random.fold_in(splits[14], 71), 0)
    rotations = with_ends(jax.random.randint(splits[3], (SLOTS_ALL, 4), 0, 4), jax.random.fold_in(splits[3], 1), 0, 3).astype(jnp.int32)
    tile_counts = draw_tile_counts(jax.random.fold_in(splits[14], 71), 0)
    depth_kernel = scatter_about(splits[5], (3, 3, C), 9 ** -0.5, 2.0, (), jnp.float32)
    depth_bias = scatter_about(splits[6], (C,), 0.5, 3.0, (), jnp.float32)
    norm_gain = jnp.clip(jax.random.uniform(splits[7], (C,), jnp.float32, 0.5, 1.5), 0.5, 1.5)
    norm_bias = scatter_about(splits[8], (C,), 0.5, 3.0, (), jnp.float32)
    weight_in = scatter_about(splits[9], (C, HID), C ** -0.5, 0.5)
    bias_in = scatter_about(splits[10], (HID,), 0.5, 3.0, (), jnp.float32)
    weight_out = scatter_about(splits[11], (HID, C), HID ** -0.5, 0.25)
    bias_out = scatter_about(splits[12], (C,), 0.5, 3.0, (), jnp.float32)
    layer_scale = jnp.clip(jax.random.uniform(splits[13], (C,), jnp.float32, 0.5, 1.5), 0.5, 1.5)
    return dict(fields=fields, cotangent=cotangent, neighbours=neighbours, rotations=rotations, tile_counts=tile_counts, depth_kernel=depth_kernel, depth_bias=depth_bias, norm_gain=norm_gain, norm_bias=norm_bias, weight_in=weight_in, bias_in=bias_in, weight_out=weight_out, bias_out=bias_out, layer_scale=layer_scale)


def side_pixels(width):
    grid = np.arange(width * width).reshape(width, width)
    table = np.zeros((4, 4, width), np.int32)
    turned = grid
    for turns in range(4):
        table[turns, 0] = turned[-1, :]
        table[turns, 1] = turned[:, 0]
        table[turns, 2] = turned[0, :]
        table[turns, 3] = turned[:, -1]
        turned = turned.T[::-1]
    return table

def framed_tiles(tiles, lines):
    lead = [(0, 0)] * (tiles.ndim - 3)
    padded = jnp.pad(tiles, lead + [(1, 1), (1, 1), (0, 0)])
    padded = padded.at[..., 0, 1:-1, :].set(lines[..., 0, :, :])
    padded = padded.at[..., 1:-1, -1, :].set(lines[..., 1, :, :])
    padded = padded.at[..., -1, 1:-1, :].set(lines[..., 2, :, :])
    padded = padded.at[..., 1:-1, 0, :].set(lines[..., 3, :, :])
    return padded

def tile_block(tiles, padded, live, cotan, depth_kernel, depth_bias, norm_gain, norm_bias, weight_in, bias_in, weight_out, bias_out, layer_scale):
    width = tiles.shape[-2]
    chans = tiles.shape[-1]
    conv = jnp.zeros(tiles.shape, jnp.float32) + depth_bias
    for row_off in range(3):
        for col_off in range(3):
            conv = conv + padded[..., row_off:row_off + width, col_off:col_off + width, :].astype(jnp.float32) * depth_kernel[row_off, col_off]
    rows = conv.reshape(-1, chans)
    centre = rows - lax.optimization_barrier(jnp.mean(rows, axis=-1, keepdims=True))
    inv_std = lax.rsqrt(lax.optimization_barrier(jnp.mean(centre * centre, axis=-1, keepdims=True)) + 1e-06)
    nhat = centre * inv_std
    normed = (nhat * norm_gain + norm_bias).astype(jnp.bfloat16)
    pre = jnp.dot(normed, weight_in, preferred_element_type=jnp.float32) + bias_in
    erf_part = jax.scipy.special.erf(pre * (1.0 / math.sqrt(2.0)))
    act = (0.5 * pre * (1.0 + erf_part)).astype(jnp.bfloat16)
    proj = jnp.dot(act, weight_out, preferred_element_type=jnp.float32) + bias_out
    keep = jnp.broadcast_to(live, tiles.shape[:-1] + (1,)).reshape(-1, 1)
    inputs = tiles.reshape(-1, chans).astype(jnp.float32)
    result = ((inputs + layer_scale * proj) * keep).astype(jnp.bfloat16).reshape(tiles.shape)
    grad_rows = cotan.reshape(-1, chans).astype(jnp.float32) * keep
    grad_scale = lax.optimization_barrier(jnp.sum(grad_rows * proj, axis=0))
    branch_f = grad_rows * layer_scale
    grad_bout = lax.optimization_barrier(jnp.sum(branch_f, axis=0))
    branch = branch_f.astype(jnp.bfloat16)
    contract_rows = (((0,), (0,)), ((), ()))
    contract_cols = (((1,), (1,)), ((), ()))
    grad_wout = lax.dot_general(act, branch, contract_rows, preferred_element_type=jnp.float32)
    dact = lax.dot_general(branch, weight_out, contract_cols, preferred_element_type=jnp.float32)
    slope = 0.5 * (1.0 + erf_part) + pre * jnp.exp(-0.5 * pre * pre) * (1.0 / math.sqrt(2.0 * math.pi))
    dpre_f = dact * slope
    grad_bin = lax.optimization_barrier(jnp.sum(dpre_f, axis=0))
    dpre = dpre_f.astype(jnp.bfloat16)
    grad_win = lax.dot_general(normed, dpre, contract_rows, preferred_element_type=jnp.float32)
    dnorm = lax.dot_general(dpre, weight_in, contract_cols, preferred_element_type=jnp.float32)
    grad_gain = lax.optimization_barrier(jnp.sum(dnorm * nhat, axis=0))
    grad_nbias = lax.optimization_barrier(jnp.sum(dnorm, axis=0))
    scaled = dnorm * norm_gain
    dconv = inv_std * (scaled - lax.optimization_barrier(jnp.mean(scaled, axis=-1, keepdims=True)) - nhat * lax.optimization_barrier(jnp.mean(scaled * nhat, axis=-1, keepdims=True)))
    grad_dbias = lax.optimization_barrier(jnp.sum(dconv, axis=0))
    dconv_tiles = dconv.reshape(tiles.shape)
    taps = []
    for row_off in range(3):
        for col_off in range(3):
            window = padded[..., row_off:row_off + width, col_off:col_off + width, :].astype(jnp.float32)
            taps.append(lax.optimization_barrier(jnp.sum((dconv_tiles * window).reshape(-1, chans), axis=0)))
    channel = jnp.stack(taps + [grad_dbias, grad_gain, grad_nbias, grad_bout, grad_scale], axis=0)
    return (result, grad_win, grad_wout, grad_bin, channel)

def reference(fields, cotangent, neighbours, rotations, tile_counts, depth_kernel, depth_bias, norm_gain, norm_bias, weight_in, bias_in, weight_out, bias_out, layer_scale):
    pixels = jnp.asarray(side_pixels(P_SIZE))
    slot_ids = jnp.arange(SLOTS_ALL, dtype=jnp.int32)
    live = (slot_ids % SLOTS < tile_counts[slot_ids // SLOTS]).astype(jnp.float32).reshape(SLOTS_ALL, 1, 1, 1)
    index = pixels[rotations, jnp.arange(4, dtype=jnp.int32)[None, :]]

    def one_sample(pair):
        tiles, cotan = pair
        flat = tiles.reshape(SLOTS_ALL, P_SIZE * P_SIZE, C)
        lines = flat[neighbours[:, :, None], index]
        padded = framed_tiles(tiles, lines)
        return tile_block(tiles, padded, live, cotan, depth_kernel, depth_bias, norm_gain, norm_bias, weight_in, bias_in, weight_out, bias_out, layer_scale)
    result, grad_win, grad_wout, grad_bin, channel = lax.map(one_sample, (fields, cotangent))
    return (result, lax.optimization_barrier(jnp.sum(grad_win, axis=0)), lax.optimization_barrier(jnp.sum(grad_wout, axis=0)), lax.optimization_barrier(jnp.sum(grad_bin, axis=0)), lax.optimization_barrier(jnp.sum(channel, axis=0)))
```

```python
import functools
import math

import jax
import jax.numpy as jnp
from jax import lax
from jax.experimental import pallas as pl
from jax.experimental.pallas import tpu as pltpu
from jax.sharding import PartitionSpec as P

F32, BF16 = jnp.float32, jnp.bfloat16
PITCH = 64
ROWS = 16
GROUP = 64
HALF = 256
def over_rows(a):
    return jnp.sum(a.reshape(-1, 8, a.shape[-1]), axis=0)

def contract_rows(a, b):
    return lax.dot_general(a, b, (((0,), (0,)), ((), ())), preferred_element_type=F32)

def block_kernel(count, tile, cotan, lines, taps_w, dbias, gain, nbias, win, bin_, wout, bout, scale,
                 out, grads, small, frame, win_t, wout_t, nhat_s, normed_s, branch_s, act_s, dpre_s, dconv_s, sums, bsum):
    t = pl.program_id(0)
    width, chans = tile.shape[1], tile.shape[2]
    hid = win.shape[1]

    @pl.when(t == 0)
    def _():
        win_t[...] = win[...].T
        wout_t[...] = wout[...].T
        grads[...] = jnp.zeros_like(grads)
        sums[...] = jnp.zeros_like(sums)
        bsum[...] = jnp.zeros_like(bsum)
        frame[...] = jnp.zeros_like(frame)

    @pl.when(t >= count[0])
    def _():
        out[...] = jnp.zeros_like(out)

    @pl.when(t < count[0])
    def _():
        def fill(r, c):
            frame[pl.ds(pl.multiple_of((r + 1) * PITCH + 8, 8), width), :] = tile[r].astype(F32)
            return c
        lax.fori_loop(0, width, fill, 0, unroll=4)
        frame[pl.ds(8, width), :] = lines[0].astype(F32)
        frame[pl.ds((width + 1) * PITCH + 8, width), :] = lines[2].astype(F32)
        frame[pl.ds(PITCH + 8 + width, width, stride=PITCH), :] = lines[1].astype(F32)
        frame[pl.ds(PITCH + 7, width, stride=PITCH), :] = lines[3].astype(F32)

        def chunk(c, carry):
            top = c * ROWS
            rows = ROWS * width
            kern = [[taps_w[3 * a + b] for b in range(3)] for a in range(3)]
            bias = dbias[...]
            inv = []
            conv = {}
            for fr in range(ROWS + 2):
                base = (top + fr) * PITCH + 7
                win3 = [frame[pl.ds(base + b, width), :] for b in range(3)]
                for a in range(3):
                    r = fr - a
                    if 0 <= r < ROWS:
                        acc = conv.get(r, bias)
                        for b in range(3):
                            acc = acc + win3[b] * kern[a][b]
                        conv[r] = acc
                r = fr - 2
                if r >= 0:
                    x = conv.pop(r)
                    x = x - jnp.mean(x, axis=-1, keepdims=True)
                    iv = lax.rsqrt(jnp.mean(x * x, axis=-1, keepdims=True) + 1e-06)
                    nhat = x * iv
                    inv.append(iv)
                    sl = pl.ds(r * width, width)
                    nhat_s[sl, :] = nhat
                    normed_s[sl, :] = (nhat * gain[...] + nbias[...]).astype(BF16)
                    g = cotan[top + r].astype(F32)
                    branch_s[sl, :] = (g * scale[...]).astype(BF16)
            normed = normed_s[...]
            branch = branch_s[...]
            for h in range(0, hid, HALF):
                hs = pl.ds(h, HALF)
                pre_h = jnp.dot(normed, win[:, hs], preferred_element_type=F32)
                dact_h = jnp.dot(branch, wout_t[:, hs], preferred_element_type=F32)
                bs = jnp.zeros((8, HALF), F32)
                for q in range(0, rows, GROUP):
                    pre = pre_h[q:q + GROUP] + bin_[:, hs]
                    ph = 0.5 * lax.erf(pre * (1.0 / math.sqrt(2.0))) + 0.5
                    act_s[pl.ds(q, GROUP), hs] = (pre * ph).astype(BF16)
                    slope = ph + pre * (jnp.exp(-0.5 * pre * pre) * (1.0 / math.sqrt(2.0 * math.pi)))
                    dpre = dact_h[q:q + GROUP] * slope
                    bs = bs + over_rows(dpre)
                    dpre_s[pl.ds(q, GROUP), hs] = dpre.astype(BF16)
                bsum[:, hs] += bs
            act = act_s[...]
            dpre = dpre_s[...]
            grads[0:chans, :] += contract_rows(normed, dpre)
            grads[chans:2 * chans, :] += contract_rows(branch, act)
            proj_a = jnp.dot(act, wout[...], preferred_element_type=F32)
            dnorm_a = jnp.dot(dpre, win_t[...], preferred_element_type=F32)
            s_g = s_gp = s_dn = s_dnh = s_dc = jnp.zeros((8, chans), F32)
            for r in range(ROWS):
                sl = slice(r * width, (r + 1) * width)
                proj = proj_a[sl]
                x = tile[top + r].astype(F32)
                out[top + r] = (x + scale[...] * (proj + bout[...])).astype(BF16)
                g = cotan[top + r].astype(F32)
                s_g = s_g + over_rows(g)
                s_gp = s_gp + over_rows(g * proj)
                dnorm = dnorm_a[sl]
                nhat = nhat_s[pl.ds(r * width, width), :]
                dnh = dnorm * nhat
                s_dn = s_dn + over_rows(dnorm)
                s_dnh = s_dnh + over_rows(dnh)
                m1 = jnp.mean(dnorm * gain[...], axis=-1, keepdims=True)
                m2 = jnp.mean(dnh * gain[...], axis=-1, keepdims=True)
                dconv = inv[r] * (dnorm * gain[...] - m1 - nhat * m2)
                s_dc = s_dc + over_rows(dconv)
                dconv_s[pl.ds(r * width, width), :] = dconv
            taps = [[jnp.zeros((8, chans), F32)] * 3 for _ in range(3)]
            for fr in range(ROWS + 2):
                base = (top + fr) * PITCH + 7
                win3 = [frame[pl.ds(base + b, width), :] for b in range(3)]
                for a in range(3):
                    r = fr - a
                    if 0 <= r < ROWS:
                        d = dconv_s[pl.ds(r * width, width), :]
                        for b in range(3):
                            taps[a][b] = taps[a][b] + over_rows(d * win3[b])
            for i, s in enumerate([taps[a][b] for a in range(3) for b in range(3)] + [s_dc, s_dnh, s_dn, s_g, s_gp]):
                sums[i] += s
            return carry
        lax.fori_loop(0, width // ROWS, chunk, 0)

    @pl.when(t == pl.num_programs(0) - 1)
    def _():
        tot = jnp.sum(sums[...], axis=1)
        small[...] = jnp.zeros_like(small)
        small[0:12, :] = tot[0:12]
        small[12:13, :] = tot[12:13] * scale[...]
        small[13:14, :] = tot[13:14] + tot[12:13] * bout[...]
        b = jnp.sum(bsum[...], axis=0, keepdims=True)
        for i in range(hid // chans):
            small[14 + i:15 + i, :] = b[:, i * chans:(i + 1) * chans]

def block(count, fields, cotan, lines, kern, dbias, gain, nbias, win, bin_, wout, bout, scale):
    slots, width, _, chans = fields.shape
    hid = win.shape[1]
    m = ROWS * width
    row = lambda v: v.reshape(1, -1)
    full = lambda *s: pl.BlockSpec(s, lambda t: (0,) * len(s))
    tiles = pl.BlockSpec((None, width, width, chans), lambda t: (t, 0, 0, 0))
    vec = full(1, chans)
    return pl.pallas_call(
        block_kernel,
        grid=(slots,),
        in_specs=[pl.BlockSpec(memory_space=pltpu.SMEM), tiles, tiles,
                  pl.BlockSpec((None, 4, width, chans), lambda t: (t, 0, 0, 0)),
                  full(9, 1, chans), vec, vec, vec, full(chans, hid), full(1, hid), full(hid, chans), vec, vec],
        out_specs=[tiles, full(2 * chans, hid), full(24, chans)],
        out_shape=[jax.ShapeDtypeStruct(fields.shape, BF16), jax.ShapeDtypeStruct((2 * chans, hid), F32),
                   jax.ShapeDtypeStruct((24, chans), F32)],
        scratch_shapes=[
            pltpu.VMEM(((width + 2) * PITCH + 8, chans), F32),
            pltpu.VMEM((hid, chans), BF16), pltpu.VMEM((chans, hid), BF16),
            pltpu.VMEM((m, chans), F32), pltpu.VMEM((m, chans), BF16), pltpu.VMEM((m, chans), BF16),
            pltpu.VMEM((m, hid), BF16), pltpu.VMEM((m, hid), BF16), pltpu.VMEM((m, chans), F32),
            pltpu.VMEM((14, 8, chans), F32), pltpu.VMEM((8, hid), F32)],
        compiler_params=pltpu.CompilerParams(vmem_limit_bytes=56 * 2**20),
    )(count, fields, cotan, lines, kern.reshape(9, 1, chans), row(dbias), row(gain), row(nbias), win, row(bin_), wout, row(bout), row(scale))


MESH = pl.DeviceIdType.MESH


def remote(src, dst, send_sem, recv_sem, device):
    return pltpu.make_async_remote_copy(
        src_ref=src, dst_ref=dst, send_sem=send_sem, recv_sem=recv_sem, device_id=device, device_id_type=MESH
    )


def halo_kernel(space, nbrs, turns, edges, lines, cand, outgo, income, send_sem, recv_sem):
    dp, me = lax.axis_index("dp"), lax.axis_index("space")
    slots, width = edges.shape[1], edges.shape[2]
    picks = 4 * slots
    barrier = pltpu.get_barrier_semaphore()

    def greet(o, c):
        pl.semaphore_signal(barrier, inc=1, device_id=(dp, lax.rem(me + o, space)), device_id_type=MESH)
        return c

    lax.fori_loop(1, space, greet, 0)
    i = lax.broadcasted_iota(jnp.int32, (width, width), 0)
    j = lax.broadcasted_iota(jnp.int32, (width, width), 1)
    mirror = (i + j == width - 1).astype(BF16)

    def candidates(k, c):
        for q in range(4):
            line = edges[q, k]
            cand[4 * k + q] = line
            cand[picks + 4 * k + q] = jnp.dot(mirror, line, preferred_element_type=F32).astype(BF16)
        return c

    lax.fori_loop(0, slots, candidates, 0)

    def pick(o, c):
        peer = lax.rem(me + o, space)
        code = jnp.int32(0)
        for k in range(picks):
            slot, side = peer * slots + k // 4, k % 4
            nbr, turn = nbrs[slot, side], turns[slot, side]
            edge = (turn + (side + 2)) & 3
            flip = ((turn + (side & 1)) >> 1) & 1
            mine = flip * picks + 4 * (nbr & (slots - 1)) + edge
            code = jnp.where(nbr // slots == me, mine, code)
        outgo[o] = cand[code]
        return c

    lax.fori_loop(0, space, pick, 0)
    income[me] = outgo[0]
    pl.semaphore_wait(barrier, space - 1)

    def send(o, c):
        remote(outgo.at[o], income.at[me], send_sem.at[o], recv_sem.at[me], (dp, lax.rem(me + o, space))).start()
        return c

    def settle(o, c):
        src = lax.rem(me + space - o, space)
        remote(outgo.at[o], income.at[src], send_sem.at[o], recv_sem.at[src], (dp, src)).wait()
        return c

    lax.fori_loop(1, space, send, 0)
    lax.fori_loop(1, space, settle, 0)
    for k in range(picks):
        lines[k // 4, k % 4] = income[nbrs[me * slots + k // 4, k % 4] // slots]


def halo(space, nbrs, turns, edges):
    _, slots, width, chans = edges.shape
    line = (width, chans)
    smem, vmem = pl.BlockSpec(memory_space=pltpu.SMEM), pl.BlockSpec(memory_space=pltpu.VMEM)
    return pl.pallas_call(
        functools.partial(halo_kernel, space),
        in_specs=[smem, smem, vmem],
        out_specs=vmem,
        out_shape=jax.ShapeDtypeStruct((slots, 4) + line, BF16),
        scratch_shapes=[
            pltpu.VMEM((8 * slots,) + line, BF16),
            pltpu.VMEM((space,) + line, BF16),
            pltpu.VMEM((space,) + line, BF16),
            pltpu.SemaphoreType.DMA((space,)),
            pltpu.SemaphoreType.DMA((space,)),
        ],
        compiler_params=pltpu.CompilerParams(collective_id=0, has_side_effects=True, vmem_limit_bytes=32 * 2**20),
    )(nbrs, turns, edges)


def reduce_kernel(near, far, ring, grads, small, whole, small_out, halves, got, small_got, tiles, small_mid,
                  far_got, small_far, final, spread, sems_a, sems_b, sems_c, sems_d, sems_e, sems_f):
    dp, space = lax.axis_index("dp"), lax.axis_index("space")
    core, plane = lax.rem(space, 2), space // 2
    a, b = dp * 2 + core, plane
    z, base = lax.rem(plane, ring), (plane // ring) * ring
    rows, cols = whole.shape[1], whole.shape[2]

    def near_id(o):
        p = lax.rem(a + o, near)
        return p, (p // 2, plane * 2 + lax.rem(p, 2))

    def far_id(o):
        p = lax.rem(b + o, far)
        return p, (dp, p * 2 + core)

    def ring_id(o):
        p = lax.rem(z + o, ring)
        return p, (dp, (base + p) * 2 + core)

    barrier = pltpu.get_barrier_semaphore()

    def greet_near(o, c):
        pl.semaphore_signal(barrier, inc=1, device_id=near_id(o)[1], device_id_type=MESH)
        return c

    def greet_far(o, c):
        pl.semaphore_signal(barrier, inc=1, device_id=far_id(o)[1], device_id_type=MESH)
        return c

    lax.fori_loop(1, near, greet_near, 0)
    lax.fori_loop(1, far, greet_far, 0)
    for p in range(near):
        halves[p] = grads[pl.ds(p * rows, rows), :].astype(BF16)
    pl.semaphore_wait(barrier, near + far - 2)

    def send_near(o, c):
        p, device = near_id(o)
        remote(halves.at[p], got.at[a], sems_a.at[0, o], sems_a.at[1, a], device).start()
        remote(small, small_got.at[a], sems_b.at[0, o], sems_b.at[1, a], device).start()
        return c

    def settle_near(o, c):
        p, device = near_id(near - o)
        remote(halves.at[p], got.at[p], sems_a.at[0, o], sems_a.at[1, p], device).wait()
        remote(small, small_got.at[p], sems_b.at[0, o], sems_b.at[1, p], device).wait()
        return c

    lax.fori_loop(1, near, send_near, 0)
    got[a] = halves[a]
    small_got[a] = small[...]
    lax.fori_loop(1, near, settle_near, 0)
    tot = got[0].astype(F32)
    s = small_got[0]
    for p in range(1, near):
        tot = tot + got[p].astype(F32)
        s = s + small_got[p]
    per = cols // 128
    for p in range(ring):
        r, q = p // per, p % per
        tiles[p] = tot[r * 8:r * 8 + 8, q * 128:q * 128 + 128]
    small_mid[...] = s

    def send_far(o, c):
        p, device = far_id(o)
        remote(tiles.at[lax.rem(p, ring)], far_got.at[b], sems_c.at[0, o], sems_c.at[1, b], device).start()
        remote(small_mid, small_far.at[b], sems_d.at[0, o], sems_d.at[1, b], device).start()
        return c

    def settle_far(o, c):
        p, device = far_id(far - o)
        remote(tiles.at[lax.rem(p, ring)], far_got.at[p], sems_c.at[0, o], sems_c.at[1, p], device).wait()
        remote(small_mid, small_far.at[p], sems_d.at[0, o], sems_d.at[1, p], device).wait()
        return c

    lax.fori_loop(1, far, send_far, 0)
    far_got[b] = tiles[z]
    small_far[b] = s
    lax.fori_loop(1, far, settle_far, 0)
    t = far_got[0]
    s = small_far[0]
    for p in range(1, far):
        t = t + far_got[p]
        s = s + small_far[p]
    small_out[...] = s
    final[z] = t

    def send_ring(o, c):
        p, device = ring_id(o)
        remote(final.at[z], final.at[z], sems_e.at[0, o], sems_e.at[1, z], device).start()
        return c

    def settle_ring(o, c):
        p, device = ring_id(ring - o)
        remote(final.at[z], final.at[p], sems_e.at[0, o], sems_e.at[1, p], device).wait()
        return c

    lax.fori_loop(1, ring, send_ring, 0)
    lax.fori_loop(1, ring, settle_ring, 0)
    for q in range(per):
        spread[:, q * 128:(q + 1) * 128] = jnp.concatenate([final[q], final[per + q]], axis=0).astype(BF16)

    def send_back(o, c):
        p, device = near_id(o)
        remote(spread, whole.at[a], sems_f.at[0, o], sems_f.at[1, a], device).start()
        return c

    def settle_back(o, c):
        p, device = near_id(near - o)
        remote(spread, whole.at[p], sems_f.at[0, o], sems_f.at[1, p], device).wait()
        return c

    lax.fori_loop(1, near, send_back, 0)
    whole[a] = spread[...]
    lax.fori_loop(1, near, settle_back, 0)


def reduce_all(near, far, ring, grads, small):
    rows, cols = grads.shape[0] // near, grads.shape[1]
    vmem = pl.BlockSpec(memory_space=pltpu.VMEM)
    sems = lambda n: pltpu.SemaphoreType.DMA((2, n))
    return pl.pallas_call(
        functools.partial(reduce_kernel, near, far, ring),
        in_specs=[vmem, vmem],
        out_specs=[vmem, vmem],
        out_shape=[jax.ShapeDtypeStruct((near, rows, cols), BF16), jax.ShapeDtypeStruct(small.shape, F32)],
        scratch_shapes=[
            pltpu.VMEM((near, rows, cols), BF16),
            pltpu.VMEM((near, rows, cols), BF16),
            pltpu.VMEM((near,) + small.shape, F32),
            pltpu.VMEM((ring, 8, 128), F32),
            pltpu.VMEM(small.shape, F32),
            pltpu.VMEM((far, 8, 128), F32),
            pltpu.VMEM((far,) + small.shape, F32),
            pltpu.VMEM((ring, 8, 128), F32),
            pltpu.VMEM((rows, cols), BF16),
            sems(near), sems(near), sems(far), sems(far), sems(ring), sems(near),
        ],
        compiler_params=pltpu.CompilerParams(collective_id=1, has_side_effects=True, vmem_limit_bytes=32 * 2**20),
    )(grads, small)


def local(fields, cotangent, neighbours, rotations, tile_counts, depth_kernel, depth_bias, norm_gain, norm_bias,
          weight_in, bias_in, weight_out, bias_out, layer_scale, shape):
    tiles, cotan = fields[0], cotangent[0]
    width = tiles.shape[1]
    chans, hid = weight_in.shape
    space, near = shape["space"], 2 * shape["dp"]
    far = space // 2
    edges = jnp.stack([tiles[:, 0], tiles[:, :, width - 1], tiles[:, width - 1], tiles[:, :, 0]], axis=0)
    lines = halo(space, neighbours, rotations, edges)
    count = lax.dynamic_slice_in_dim(tile_counts, lax.axis_index("space"), 1, 0)
    result, grads, small = block(count, tiles, cotan, lines, depth_kernel, depth_bias, norm_gain, norm_bias,
                                 weight_in, bias_in, weight_out, bias_out, layer_scale)
    whole, small = reduce_all(near, far, far // 2, grads, small)
    whole = whole.reshape(2 * chans, hid)
    grad_win = whole[:chans].astype(F32)
    grad_wout = whole[chans:].T.astype(F32)
    return result[None], grad_win, grad_wout, small[14:14 + hid // chans].reshape(hid), small[:14]


def solution(mesh):
    placed = P("dp", "space", None, None, None)
    return jax.shard_map(
        functools.partial(local, shape=dict(mesh.shape)),
        mesh=mesh,
        in_specs=(placed, placed) + (P(),) * 12,
        out_specs=(placed, P(), P(), P(), P()),
        check_vma=False,
    )
```

```python
import functools
import math

import jax
import jax.numpy as jnp
from jax import lax
from jax.experimental import pallas as pl
from jax.experimental.pallas import tpu as pltpu
from jax.sharding import PartitionSpec as P

F32, BF16 = jnp.float32, jnp.bfloat16
MESH = pl.DeviceIdType.MESH
PITCH = 64
CONV_ROWS = 8
LAST_ROWS = 8
GROUP = 64
COMM = True


def over_rows(a):
    return jnp.sum(a.reshape(-1, 8, a.shape[-1]), axis=0)


def contract_rows(a, b):
    return lax.dot_general(a, b, (((0,), (0,)), ((), ())), preferred_element_type=F32)


def remote(src, dst, send_sem, recv_sem, device):
    return pltpu.make_async_remote_copy(
        src_ref=src, dst_ref=dst, send_sem=send_sem, recv_sem=recv_sem, device_id=device, device_id_type=MESH
    )


def loop(lo, hi, body, unroll=1):
    def step(i, c):
        body(i)
        return c

    lax.fori_loop(lo, hi, step, 0, unroll=unroll)


def block_kernel(space, near, nbrs, turns, counts, fields, cotangent, taps_w, dbias, gain, nbias, win, bin_, wout,
                 bout, scale, out, grad_win, grad_wout, small_out,
                 tile, cotan, frame, win_t, wout_t, nhat_s, inv_s, normed_s, branch_s, proj_s, dnorm_s, act_s, dpre_s,
                 cot_s, grads, sums, bsum, small, cand, outgo, income, halves, got, mid, far_got, spread, whole,
                 small_got, small_mid, small_far,
                 load_sem, halo_send, halo_recv, near_sem, far_sem, back_sem, sn_sem, sf_sem):
    slots, width, _, chans = tile.shape
    hid = win.shape[1]
    hh = hid // 2
    area = width * width
    main = slots * area
    m = act_s.shape[0]
    picks = 4 * slots
    far = space // 2
    if COMM:
        dp, me = lax.axis_index("dp"), lax.axis_index("space")
        core, plane = lax.rem(me, 2), me // 2
        a = dp * 2 + core
    else:
        me = 0
    loads = []
    for t in range(slots):
        loads.append((pltpu.make_async_copy(fields.at[t], tile.at[t], load_sem.at[0, t]),
                      pltpu.make_async_copy(cotangent.at[t], cotan.at[t], load_sem.at[1, t])))
    for t in range(slots):
        loads[t][0].start()
    for t in range(slots):
        loads[t][1].start()

    def near_id(o):
        p = lax.rem(a + o, near)
        return p, (p // 2, plane * 2 + lax.rem(p, 2))

    def far_id(o):
        p = lax.rem(plane + o, far)
        return p, (dp, p * 2 + core)

    if COMM:
        barrier = pltpu.get_barrier_semaphore()
        loop(1, space, lambda o: pl.semaphore_signal(
            barrier, inc=1, device_id=(dp, lax.rem(me + o, space)), device_id_type=MESH))
        loop(1, near, lambda o: pl.semaphore_signal(barrier, inc=1, device_id=near_id(o)[1], device_id_type=MESH))

    win_t[...] = win[...].T
    for h in range(2):
        wout_t[h] = wout[h * hh:(h + 1) * hh, :].T
    grads[...] = jnp.zeros_like(grads)
    sums[...] = jnp.zeros_like(sums)
    bsum[...] = jnp.zeros_like(bsum)

    def clear(t):
        frame[t, 0:PITCH, :] = jnp.zeros((PITCH, chans), F32)
        frame[t, pl.ds((width + 1) * PITCH, PITCH + 8), :] = jnp.zeros((PITCH + 8, chans), F32)

        def side(r):
            frame[t, pl.ds(pl.multiple_of((r + 1) * PITCH, 8), 8), :] = jnp.zeros((8, chans), F32)
            frame[t, pl.ds(pl.multiple_of((r + 1) * PITCH + 8 + width, 8), 8), :] = jnp.zeros((8, chans), F32)
            frame[t, pl.ds(pl.multiple_of((r + 1) * PITCH + 8, 8), width), :] = tile[t, r].astype(F32)

        loop(0, width, side, 4)

    def edge_of(k, q):
        t = k
        if q == 0:
            return frame[t, pl.ds(PITCH + 8, width), :]
        if q == 1:
            return frame[t, pl.ds(PITCH + 7 + width, width, stride=PITCH), :]
        if q == 2:
            return frame[t, pl.ds(width * PITCH + 8, width), :]
        return frame[t, pl.ds(PITCH + 8, width, stride=PITCH), :]

    def pick_code(nbr, turn, side):
        edge = (turn + (side + 2)) & 3
        flip = ((turn + (side & 1)) >> 1) & 1
        return flip * picks + 4 * (nbr & (slots - 1)) + edge

    for t in range(slots):
        loads[t][0].wait()
    loop(0, slots, clear)
    i = lax.broadcasted_iota(jnp.int32, (width, width), 0)
    j = lax.broadcasted_iota(jnp.int32, (width, width), 1)
    mirror = (i + j == width - 1).astype(BF16)

    def candidates(t):
        for q in range(4):
            line = edge_of(t, q).astype(BF16)
            cand[4 * t + q] = line
            cand[picks + 4 * t + q] = jnp.dot(mirror, line, preferred_element_type=F32).astype(BF16)

    loop(0, slots, candidates)

    if COMM:
        def pick(o):
            peer = lax.rem(me + o, space)
            code = jnp.int32(0)
            for k in range(picks):
                slot, side = peer * slots + k // 4, k % 4
                nbr = nbrs[side, slot]
                code = jnp.where(nbr // slots == me, pick_code(nbr, turns[side, slot], side), code)
            outgo[o] = cand[code]

        loop(0, space, pick)
        income[me] = outgo[0]
        pl.semaphore_wait(barrier, space + near - 2)

        loop(1, space, lambda o: remote(
            outgo.at[o], income.at[me], halo_send.at[o], halo_recv.at[me], (dp, lax.rem(me + o, space))).start())

    for t in range(slots):
        loads[t][1].wait()

    count = counts[me]
    px = lax.broadcasted_iota(jnp.int32, (width, chans), 0)
    inner = ((px > 0) & (px < width - 1)).astype(F32)

    def norm_rows(conv, at):
        x = conv - jnp.mean(conv, axis=-1, keepdims=True)
        iv = lax.rsqrt(jnp.mean(x * x, axis=-1, keepdims=True) + 1e-06)
        nhat = x * iv
        sl = pl.ds(pl.multiple_of(at, 16), width)
        inv_s[sl, :] = jnp.broadcast_to(iv, (width, chans))
        nhat_s[sl, :] = nhat
        normed_s[sl, :] = (nhat * gain[...] + nbias[...]).astype(BF16)

    per = width // CONV_ROWS

    def conv_chunk(step):
        t = step // per
        top = (step - t * per) * CONV_ROWS
        live = jnp.where(t < count, 1.0, 0.0)
        kern = [[taps_w[x, y:y + 1, :] for y in range(3)] for x in range(3)]
        bias = dbias[...]
        conv = {}
        for fr in range(CONV_ROWS + 2):
            base = (top + fr) * PITCH + 7
            win3 = [frame[t, pl.ds(base + b, width), :] for b in range(3)]
            for x in range(3):
                r = fr - x
                if 0 <= r < CONV_ROWS:
                    acc = conv.get(r, bias)
                    for b in range(3):
                        acc = acc + win3[b] * kern[x][b]
                    conv[r] = acc
            r = fr - 2
            if r >= 0:
                at = t * area + (top + r) * width
                norm_rows(conv.pop(r), at)
                inside = jnp.where((top + r > 0) & (top + r < width - 1), live, 0.0)
                g = cotan[t, top + r].astype(F32) * inside
                branch_s[pl.ds(pl.multiple_of(at, 16), width), :] = (g * (scale[...] * inner)).astype(BF16)

    loop(0, slots * per, conv_chunk)

    def border(t):
        live = jnp.where(t < count, 1.0, 0.0)
        kern = [[taps_w[x, y:y + 1, :] for y in range(3)] for x in range(3)]
        for s in range(4):
            if COMM:
                line = income[nbrs[s, me * slots + t] // slots]
            else:
                line = cand[pick_code(nbrs[s, t], turns[s, t], s)]
            line = line.astype(F32)
            if s == 0:
                frame[t, pl.ds(8, width), :] = line
            elif s == 1:
                frame[t, pl.ds(PITCH + 8 + width, width, stride=PITCH), :] = line
            elif s == 2:
                frame[t, pl.ds((width + 1) * PITCH + 8, width), :] = line
            else:
                frame[t, pl.ds(PITCH + 7, width, stride=PITCH), :] = line

        def cots(r):
            cot_s[pl.ds(pl.multiple_of(r * 16, 8), 8), :] = cotan[t, r, 0:16, :].astype(F32)[0:8]
            cot_s[pl.ds(pl.multiple_of(r * 16 + 8, 8), 8), :] = cotan[t, r, width - 16:width, :].astype(F32)[8:16]

        loop(0, width, cots, 4)
        for s in range(4):
            acc = dbias[...]
            for x in range(3):
                for b in range(3):
                    if s == 0:
                        w = frame[t, pl.ds(x * PITCH + 7 + b, width), :]
                    elif s == 1:
                        w = frame[t, pl.ds(x * PITCH + 6 + width + b, width, stride=PITCH), :]
                    elif s == 2:
                        w = frame[t, pl.ds((width - 1 + x) * PITCH + 7 + b, width), :]
                    else:
                        w = frame[t, pl.ds(x * PITCH + 7 + b, width, stride=PITCH), :]
                    acc = acc + w * taps_w[x, b:b + 1, :]
            at = main + (t * 4 + s) * width
            norm_rows(acc, at)
            if s == 0:
                g = cotan[t, 0].astype(F32)
            elif s == 1:
                g = cot_s[pl.ds(15, width, stride=16), :] * inner
            elif s == 2:
                g = cotan[t, width - 1].astype(F32)
            else:
                g = cot_s[pl.ds(0, width, stride=16), :] * inner
            branch_s[pl.ds(pl.multiple_of(at, 16), width), :] = (g * live * scale[...]).astype(BF16)

    def hidden(h, step):
        base = pl.multiple_of(step * m, 16)
        normed = normed_s[pl.ds(base, m), :]
        branch = branch_s[pl.ds(base, m), :]
        hs = pl.ds(h * hh, hh)
        pre_h = jnp.dot(normed, win[:, hs], preferred_element_type=F32)
        dact_h = jnp.dot(branch, wout_t[h], preferred_element_type=F32)
        bs = jnp.zeros((8, hh), F32)
        for q in range(0, m, GROUP):
            pre = pre_h[q:q + GROUP] + bin_[:, hs]
            ph = 0.5 * lax.erf(pre * (1.0 / math.sqrt(2.0))) + 0.5
            act_s[pl.ds(q, GROUP), :] = (pre * ph).astype(BF16)
            slope = ph + pre * (jnp.exp(-0.5 * pre * pre) * (1.0 / math.sqrt(2.0 * math.pi)))
            dpre = dact_h[q:q + GROUP] * slope
            bs = bs + over_rows(dpre)
            dpre_s[pl.ds(q, GROUP), :] = dpre.astype(BF16)
        bsum[h] += bs
        act = act_s[...]
        dpre = dpre_s[...]
        grads[h, 0:chans, :] += contract_rows(normed, dpre)
        grads[h, chans:2 * chans, :] += contract_rows(branch, act)
        proj = jnp.dot(act, wout[hs, :], preferred_element_type=F32)
        dnorm = jnp.dot(dpre, win_t[hs, :], preferred_element_type=F32)
        rows = pl.ds(base, m)
        if h == 0:
            proj_s[rows, :] = proj
            dnorm_s[rows, :] = dnorm
        else:
            proj_s[rows, :] += proj
            dnorm_s[rows, :] += dnorm

    def send_near(h):
        prows = 2 * chans // near
        for p in range(near):
            halves[h, p] = grads[h, p * prows:(p + 1) * prows, :].astype(BF16)
        got[h, a] = halves[h, a]

        def go(o):
            p, device = near_id(o)
            remote(halves.at[h, p], got.at[h, a], near_sem.at[h, 0, o], near_sem.at[h, 1, a], device).start()

        loop(1, near, go)

    def pass_far(h):
        def wait(o):
            p, device = near_id(near - o)
            remote(halves.at[h, p], got.at[h, p], near_sem.at[h, 0, o], near_sem.at[h, 1, p], device).wait()

        loop(1, near, wait)
        tot = got[h, 0].astype(F32)
        for p in range(1, near):
            tot = tot + got[h, p].astype(F32)
        mid[h] = tot.astype(BF16)
        far_got[h, plane] = mid[h]

        def go(o):
            p, device = far_id(o)
            remote(mid.at[h], far_got.at[h, plane], far_sem.at[h, 0, o], far_sem.at[h, 1, plane], device).start()

        loop(1, far, go)

    def pass_back(h):
        def wait(o):
            p, device = far_id(far - o)
            remote(mid.at[h], far_got.at[h, p], far_sem.at[h, 0, o], far_sem.at[h, 1, p], device).wait()

        loop(1, far, wait)
        tot = far_got[h, 0].astype(F32)
        for p in range(1, far):
            tot = tot + far_got[h, p].astype(F32)
        spread[h] = tot.astype(BF16)
        whole[h, a] = spread[h]

        def go(o):
            p, device = near_id(o)
            remote(spread.at[h], whole.at[h, a], back_sem.at[h, 0, o], back_sem.at[h, 1, a], device).start()

        loop(1, near, go)

    def finish(h):
        def wait(o):
            p, device = near_id(near - o)
            remote(spread.at[h], whole.at[h, p], back_sem.at[h, 0, o], back_sem.at[h, 1, p], device).wait()

        loop(1, near, wait)
        prows = 2 * chans // near
        hs = slice(h * hh, (h + 1) * hh)
        full = whole[h].reshape(2 * chans, hh).astype(F32)
        grad_win[:, hs] = full[:chans]
        grad_wout[hs, :] = full[chans:].T

    steps = (main + slots * 4 * width) // m
    loop(0, steps - 1, lambda s: hidden(0, s))
    if COMM:
        def halo_wait(o):
            src = lax.rem(me + space - o, space)
            remote(outgo.at[o], income.at[src], halo_send.at[o], halo_recv.at[src], (dp, src)).wait()

        loop(1, space, halo_wait)
    loop(0, slots, border)
    hidden(0, steps - 1)
    if COMM:
        send_near(0)

    def second(s):
        hidden(1, s)
        if COMM:
            @pl.when(s == 4)
            def _():
                pass_far(0)

            @pl.when(s == 9)
            def _():
                pass_back(0)

    loop(0, steps, second)
    if COMM:
        send_near(1)
        finish(0)

    def merge(t):
        for ref in (proj_s, dnorm_s, nhat_s, inv_s):
            for s in (1, 3, 0, 2):
                v = ref[pl.ds(pl.multiple_of(main + (t * 4 + s) * width, 8), width), :]
                if s == 1:
                    ref[pl.ds(t * area + width - 1, width, stride=width), :] = v
                elif s == 3:
                    ref[pl.ds(t * area, width, stride=width), :] = v
                elif s == 0:
                    ref[pl.ds(pl.multiple_of(t * area, 8), width), :] = v
                else:
                    ref[pl.ds(pl.multiple_of(t * area + area - width, 8), width), :] = v

    loop(0, slots, merge)

    lper = width // LAST_ROWS

    def last(step):
        t = step // lper
        top = (step - t * lper) * LAST_ROWS
        live = jnp.where(t < count, 1.0, 0.0)
        taps = [[jnp.zeros((8, chans), F32)] * 3 for _ in range(3)]
        s_g = s_gp = s_dn = s_dnh = s_dc = jnp.zeros((8, chans), F32)
        dconv = {}
        for fr in range(LAST_ROWS + 2):
            r = fr
            if r < LAST_ROWS:
                sl = pl.ds(pl.multiple_of(t * area + (top + r) * width, 16), width)
                proj = proj_s[sl, :]
                x = tile[t, top + r].astype(F32)
                out[t, top + r] = ((x + scale[...] * (proj + bout[...])) * live).astype(BF16)
                g = cotan[t, top + r].astype(F32)
                s_g = s_g + over_rows(g)
                s_gp = s_gp + over_rows(g * proj)
                dnorm = dnorm_s[sl, :]
                nhat = nhat_s[sl, :]
                dnh = dnorm * nhat
                s_dn = s_dn + over_rows(dnorm)
                s_dnh = s_dnh + over_rows(dnh)
                m1 = jnp.mean(dnorm * gain[...], axis=-1, keepdims=True)
                m2 = jnp.mean(dnh * gain[...], axis=-1, keepdims=True)
                dc = inv_s[sl, :] * (dnorm * gain[...] - m1 - nhat * m2)
                s_dc = s_dc + over_rows(dc)
                dconv[r] = dc
            base = (top + fr) * PITCH + 7
            win3 = [frame[t, pl.ds(base + b, width), :] for b in range(3)]
            for x in range(3):
                r = fr - x
                if 0 <= r < LAST_ROWS:
                    for b in range(3):
                        taps[x][b] = taps[x][b] + over_rows(dconv[r] * win3[b])
            dconv.pop(fr - 2, None)
        for n, s in enumerate([taps[x][b] for x in range(3) for b in range(3)]
                              + [s_dc, s_dnh, s_dn, s_g * live, s_gp * live]):
            sums[n] += s
        if COMM:
            @pl.when(step == slots * lper // 2)
            def _():
                pass_far(1)

    loop(0, slots * lper, last)

    tot = jnp.sum(sums[...], axis=1)
    small[...] = jnp.zeros_like(small)
    small[0:12, :] = tot[0:12]
    small[12:13, :] = tot[12:13] * scale[...]
    small[13:14, :] = tot[13:14] + tot[12:13] * bout[...]
    b = jnp.sum(bsum[...], axis=1)
    per_h = hh // chans
    for h in range(2):
        for n in range(per_h):
            k = 14 + h * per_h + n
            small[k:k + 1, :] = b[h:h + 1, n * chans:(n + 1) * chans]
    if not COMM:
        small_out[...] = small[...]
        for h in range(2):
            grad_win[:, h * hh:(h + 1) * hh] = grads[h, 0:chans, :]
            grad_wout[h * hh:(h + 1) * hh, :] = grads[h, chans:2 * chans, :].T
        return

    small_got[a] = small[...]

    def small_near(o):
        p, device = near_id(o)
        remote(small, small_got.at[a], sn_sem.at[0, o], sn_sem.at[1, a], device).start()

    def small_near_wait(o):
        p, device = near_id(near - o)
        remote(small, small_got.at[p], sn_sem.at[0, o], sn_sem.at[1, p], device).wait()

    def small_far_go(o):
        p, device = far_id(o)
        remote(small_mid, small_far.at[plane], sf_sem.at[0, o], sf_sem.at[1, plane], device).start()

    def small_far_wait(o):
        p, device = far_id(far - o)
        remote(small_mid, small_far.at[p], sf_sem.at[0, o], sf_sem.at[1, p], device).wait()

    loop(1, near, small_near)
    pass_back(1)
    loop(1, near, small_near_wait)
    s = small_got[0]
    for p in range(1, near):
        s = s + small_got[p]
    small_mid[...] = s
    small_far[plane] = s
    loop(1, far, small_far_go)
    finish(1)
    loop(1, far, small_far_wait)
    s = small_far[0]
    for p in range(1, far):
        s = s + small_far[p]
    small_out[...] = s


def block(space, near, nbrs, turns, counts, fields, cotan, kern, dbias, gain, nbias, win, bin_, wout, bout, scale):
    slots, width, _, chans = fields.shape
    hid = win.shape[1]
    hh = hid // 2
    far = space // 2
    main, edge = slots * width * width, slots * 4 * width
    row = lambda v: v.reshape(1, -1)
    smem, vmem, anyw = (pl.BlockSpec(memory_space=s) for s in (pltpu.SMEM, pltpu.VMEM, pl.ANY))
    dma = lambda *s: pltpu.SemaphoreType.DMA(s)
    v = lambda dt, *s: pltpu.VMEM(s, dt)
    piece = (2 * chans // near, hh)
    line = (width, chans)
    return pl.pallas_call(
        functools.partial(block_kernel, space, near),
        in_specs=[smem, smem, smem, anyw, anyw] + [vmem] * 9,
        out_specs=[vmem] * 4,
        out_shape=[jax.ShapeDtypeStruct(fields.shape, BF16), jax.ShapeDtypeStruct((chans, hid), F32),
                   jax.ShapeDtypeStruct((hid, chans), F32), jax.ShapeDtypeStruct((24, chans), F32)],
        scratch_shapes=[
            v(BF16, *fields.shape), v(BF16, *fields.shape), v(F32, slots, (width + 2) * PITCH + 8, chans),
            v(BF16, hid, chans), v(BF16, 2, chans, hh),
            v(F32, main + edge, chans), v(F32, main + edge, chans),
            v(BF16, main + edge, chans), v(BF16, main + edge, chans),
            v(F32, main + edge, chans), v(F32, main + edge, chans),
            v(BF16, edge, hh), v(BF16, edge, hh), v(F32, width * 16, chans),
            v(F32, 2, 2 * chans, hh), v(F32, 14, 8, chans), v(F32, 2, 8, hh), v(F32, 24, chans),
            v(BF16, 8 * slots, *line), v(BF16, space, *line), v(BF16, space, *line),
            v(BF16, 2, near, *piece), v(BF16, 2, near, *piece), v(BF16, 2, *piece), v(BF16, 2, far, *piece),
            v(BF16, 2, *piece), v(BF16, 2, near, *piece),
            v(F32, near, 24, chans), v(F32, 24, chans), v(F32, far, 24, chans),
            dma(2, slots), dma(space), dma(space), dma(2, 2, near), dma(2, 2, far), dma(2, 2, near),
            dma(2, near), dma(2, far)],
        compiler_params=pltpu.CompilerParams(
            vmem_limit_bytes=60 * 2**20, **(dict(collective_id=0, has_side_effects=True) if COMM else {})),
    )(nbrs, turns, counts, fields, cotan, kern, row(dbias), row(gain), row(nbias), win, row(bin_), wout, row(bout),
      row(scale))


def local(fields, cotangent, neighbours, rotations, tile_counts, depth_kernel, depth_bias, norm_gain, norm_bias,
          weight_in, bias_in, weight_out, bias_out, layer_scale, shape):
    chans, hid = weight_in.shape
    result, grad_win, grad_wout, small = block(
        shape["space"], 2 * shape["dp"], neighbours.T, rotations.T, tile_counts, fields[0], cotangent[0], depth_kernel,
        depth_bias, norm_gain, norm_bias, weight_in, bias_in, weight_out, bias_out, layer_scale)
    return result[None], grad_win, grad_wout, small[14:14 + hid // chans].reshape(hid), small[:14]


def solution(mesh):
    placed = P("dp", "space", None, None, None)
    return jax.shard_map(
        functools.partial(local, shape=dict(mesh.shape)),
        mesh=mesh,
        in_specs=(placed, placed) + (P(),) * 12,
        out_specs=(placed, P(), P(), P(), P()),
        check_vma=False,
    )
```

```python
import functools
import math

import jax
import jax.numpy as jnp
from jax import lax
from jax.experimental import pallas as pl
from jax.experimental.pallas import tpu as pltpu
from jax.sharding import PartitionSpec as P

F32, BF16 = jnp.float32, jnp.bfloat16
MESH = pl.DeviceIdType.MESH
PITCH = 64
CONV_ROWS = 16
LAST_ROWS = 16
GROUP = 64
COMM = True


def over_rows(a):
    return jnp.sum(a.reshape(-1, 8, a.shape[-1]), axis=0)


def contract_rows(a, b):
    return lax.dot_general(a, b, (((0,), (0,)), ((), ())), preferred_element_type=F32)


def remote(src, dst, send_sem, recv_sem, device):
    return pltpu.make_async_remote_copy(
        src_ref=src, dst_ref=dst, send_sem=send_sem, recv_sem=recv_sem, device_id=device, device_id_type=MESH
    )


def loop(lo, hi, body, unroll=1):
    def step(i, c):
        body(i)
        return c

    lax.fori_loop(lo, hi, step, 0, unroll=unroll)


def block_kernel(space, near, fields, cotangent, *refs):
    slots, width, _, chans = fields.shape
    held, outs, scratch = refs[:12], refs[12:17], refs[17:]
    kept, made, rest = scratch[:12], scratch[12:16], scratch[16:]
    in_sem, out_sem = rest[:2]
    first = [pltpu.make_async_copy(held[n], kept[n], in_sem.at[n]) for n in range(12)]
    for n in (9, 11, 0, 1, 2, 3, 4, 5, 6, 7, 8, 10):
        first[n].start()
    last = [pltpu.make_async_copy(made[n], outs[n + 1], out_sem.at[n]) for n in range(4)]
    body(space, near, fields, cotangent, *kept, outs[0], *made, first, last, *rest[2:])


def body(space, near, fields, cotangent, nbrs, turns, counts, taps_w, dbias, gain, nbias, bin_, scale, win, bout, wout,
         out, grad_win, grad_wout, channel_out, bias_out, first, final_copies,
                 tile, cotan, frame, win_t, wout_t, win_h, nhat_s, inv_s, normed_s, branch_s, act_all, dpre_all,
                 pre_a, pre_b, dact_a, dact_b, act_a, act_b, dpre_a, dpre_b, proj_b, dnorm_b, rows_a, rows_b, result,
                 cot_s, codes, grads, sums, bsum, small, cand, outgo, income, halves, got, mid, far_got, spread, whole,
                 small_got, small_mid, small_far,
                 load_sem, out_sem, halo_send, halo_recv, near_sem, far_sem, back_sem, sn_sem, sf_sem):
    slots, width, _, chans = tile.shape
    hid = win.shape[1]
    hh = hid // 2
    area = width * width
    main = slots * area
    m = act_a.shape[0]
    shift = slots.bit_length() - 1
    picks = 4 * slots
    far = space // 2
    if COMM:
        dp, me = lax.axis_index("dp"), lax.axis_index("space")
        core, plane = lax.rem(me, 2), me // 2
        a = dp * 2 + core
    else:
        me = 0
    loads = []
    for t in range(slots):
        loads.append((pltpu.make_async_copy(fields.at[t], tile.at[t], load_sem.at[0, t]),
                      pltpu.make_async_copy(cotangent.at[t], cotan.at[t], load_sem.at[1, t])))
    for t in range(slots):
        loads[t][0].start()
    for t in range(slots):
        loads[t][1].start()

    def near_id(o):
        p = lax.rem(a + o, near)
        return p, (p // 2, plane * 2 + lax.rem(p, 2))

    def far_id(o):
        p = lax.rem(plane + o, far)
        return p, (dp, p * 2 + core)

    for c in first:
        c.wait()
    if COMM:
        barrier = pltpu.get_barrier_semaphore()
        loop(1, space, lambda o: pl.semaphore_signal(
            barrier, inc=1, device_id=(dp, lax.rem(me + o, space)), device_id_type=MESH))
        loop(1, near, lambda o: pl.semaphore_signal(barrier, inc=1, device_id=near_id(o)[1], device_id_type=MESH))

    win_t[...] = win[...].T
    for h in range(2):
        win_h[h] = win[:, h * hh:(h + 1) * hh]
        wout_t[h] = wout[h * hh:(h + 1) * hh, :].T
    grads[...] = jnp.zeros_like(grads)
    sums[...] = jnp.zeros_like(sums)
    bsum[...] = jnp.zeros_like(bsum)
    act_b[...] = jnp.zeros_like(act_b)
    dpre_b[...] = jnp.zeros_like(dpre_b)

    def pick_code(k, nbr, turn):
        side = k & 3
        edge = (turn + (side + 2)) & 3
        flip = ((turn + (side & 1)) >> 1) & 1
        return flip * picks + 4 * (nbr & (slots - 1)) + edge

    if COMM:
        def scan(o):
            peer = lax.rem(me + o, space)
            hit = jnp.int32(0)
            for k in range(picks):
                nbr = nbrs[k & 3, peer * slots + (k >> 2)]
                hit = jnp.where((nbr >> shift) == me, k, hit)
            slot = peer * slots + (hit >> 2)
            codes[o] = pick_code(hit, nbrs[hit & 3, slot], turns[hit & 3, slot])

        loop(0, space, scan)

    def clear(t):
        frame[t, 0:PITCH, :] = jnp.zeros((PITCH, chans), F32)
        frame[t, pl.ds((width + 1) * PITCH, PITCH + 8), :] = jnp.zeros((PITCH + 8, chans), F32)

        def side(r):
            frame[t, pl.ds(pl.multiple_of((r + 1) * PITCH, 8), 8), :] = jnp.zeros((8, chans), F32)
            frame[t, pl.ds(pl.multiple_of((r + 1) * PITCH + 8 + width, 8), 8), :] = jnp.zeros((8, chans), F32)
            frame[t, pl.ds(pl.multiple_of((r + 1) * PITCH + 8, 8), width), :] = tile[t, r].astype(F32)

        loop(0, width, side, 4)

    def edge_of(k, q):
        t = k
        if q == 0:
            return frame[t, pl.ds(PITCH + 8, width), :]
        if q == 1:
            return frame[t, pl.ds(PITCH + 7 + width, width, stride=PITCH), :]
        if q == 2:
            return frame[t, pl.ds(width * PITCH + 8, width), :]
        return frame[t, pl.ds(PITCH + 8, width, stride=PITCH), :]

    for t in range(slots):
        loads[t][0].wait()
        clear(t)
    i = lax.broadcasted_iota(jnp.int32, (width, width), 0)
    j = lax.broadcasted_iota(jnp.int32, (width, width), 1)
    mirror = (i + j == width - 1).astype(BF16)

    def candidates(t):
        for q in range(4):
            line = edge_of(t, q).astype(BF16)
            cand[4 * t + q] = line
            cand[picks + 4 * t + q] = jnp.dot(mirror, line, preferred_element_type=F32).astype(BF16)

    loop(0, slots, candidates)

    if COMM:
        def gather(o):
            outgo[o] = cand[codes[o]]

        loop(0, space, gather, 4)
        income[me] = outgo[0]
        pl.semaphore_wait(barrier, space + near - 2)

        loop(1, space, lambda o: remote(
            outgo.at[o], income.at[me], halo_send.at[o], halo_recv.at[me], (dp, lax.rem(me + o, space))).start())

    for t in range(slots):
        loads[t][1].wait()

    count = counts[me]
    px = lax.broadcasted_iota(jnp.int32, (width, chans), 0)
    inner = ((px > 0) & (px < width - 1)).astype(F32)

    def norm_rows(conv, at):
        x = conv - jnp.mean(conv, axis=-1, keepdims=True)
        iv = lax.rsqrt(jnp.mean(x * x, axis=-1, keepdims=True) + 1e-06)
        nhat = x * iv
        sl = pl.ds(pl.multiple_of(at, 16), width)
        inv_s[sl, :] = jnp.broadcast_to(iv, (width, chans))
        nhat_s[sl, :] = nhat
        normed_s[sl, :] = (nhat * gain[...] + nbias[...]).astype(BF16)

    per = width // CONV_ROWS

    def conv_chunk(step):
        t = step // per
        top = (step - t * per) * CONV_ROWS
        live = jnp.where(t < count, 1.0, 0.0)
        kern = [[taps_w[x, y:y + 1, :] for y in range(3)] for x in range(3)]
        bias = dbias[...]
        conv = {}
        for fr in range(CONV_ROWS + 2):
            base = (top + fr) * PITCH + 7
            win3 = [frame[t, pl.ds(base + b, width), :] for b in range(3)]
            for x in range(3):
                r = fr - x
                if 0 <= r < CONV_ROWS:
                    acc = conv.get(r, bias)
                    for b in range(3):
                        acc = acc + win3[b] * kern[x][b]
                    conv[r] = acc
            r = fr - 2
            if r >= 0:
                at = t * area + (top + r) * width
                norm_rows(conv.pop(r), at)
                inside = jnp.where((top + r > 0) & (top + r < width - 1), live, 0.0)
                g = cotan[t, top + r].astype(F32) * inside
                branch_s[pl.ds(pl.multiple_of(at, 16), width), :] = (g * (scale[...] * inner)).astype(BF16)

    loop(0, slots * per, conv_chunk)

    def border(t):
        live = jnp.where(t < count, 1.0, 0.0)
        kern = [[taps_w[x, y:y + 1, :] for y in range(3)] for x in range(3)]
        for s in range(4):
            if COMM:
                line = income[nbrs[s, me * slots + t] >> shift]
            else:
                line = cand[pick_code(s, nbrs[s, t], turns[s, t])]
            line = line.astype(F32)
            if s == 0:
                frame[t, pl.ds(8, width), :] = line
            elif s == 1:
                frame[t, pl.ds(PITCH + 8 + width, width, stride=PITCH), :] = line
            elif s == 2:
                frame[t, pl.ds((width + 1) * PITCH + 8, width), :] = line
            else:
                frame[t, pl.ds(PITCH + 7, width, stride=PITCH), :] = line

        def cots(r):
            cot_s[pl.ds(pl.multiple_of(r * 16, 8), 8), :] = cotan[t, r, 0:16, :].astype(F32)[0:8]
            cot_s[pl.ds(pl.multiple_of(r * 16 + 8, 8), 8), :] = cotan[t, r, width - 16:width, :].astype(F32)[8:16]

        loop(0, width, cots, 4)
        for s in range(4):
            acc = dbias[...]
            for x in range(3):
                for b in range(3):
                    if s == 0:
                        w = frame[t, pl.ds(x * PITCH + 7 + b, width), :]
                    elif s == 1:
                        w = frame[t, pl.ds(x * PITCH + 6 + width + b, width, stride=PITCH), :]
                    elif s == 2:
                        w = frame[t, pl.ds((width - 1 + x) * PITCH + 7 + b, width), :]
                    else:
                        w = frame[t, pl.ds(x * PITCH + 7 + b, width, stride=PITCH), :]
                    acc = acc + w * taps_w[x, b:b + 1, :]
            at = main + (t * 4 + s) * width
            norm_rows(acc, at)
            if s == 0:
                g = cotan[t, 0].astype(F32)
            elif s == 1:
                g = cot_s[pl.ds(15, width, stride=16), :] * inner
            elif s == 2:
                g = cotan[t, width - 1].astype(F32)
            else:
                g = cot_s[pl.ds(0, width, stride=16), :] * inner
            branch_s[pl.ds(pl.multiple_of(at, 16), width), :] = (g * live * scale[...]).astype(BF16)

    steps = (main + slots * 4 * width) // m
    total = 2 * steps

    def place(k):
        h = k // steps
        return h, pl.ds(pl.multiple_of((k - h * steps) * m, 16), m)

    def ahead(k, pre_s, dact_s):
        h, rows = place(k)
        pre_s[...] = jnp.dot(normed_s[rows, :], win_h[h], preferred_element_type=F32)
        dact_s[...] = jnp.dot(branch_s[rows, :], wout_t[h], preferred_element_type=F32)

    def behind(k, act_s, dpre_s):
        h, rows = place(k)
        act = act_s[...]
        dpre = dpre_s[...]
        act_all[h, rows, :] = act
        dpre_all[h, rows, :] = dpre
        grads[h, 0:chans, :] += contract_rows(normed_s[rows, :], dpre)
        grads[h, chans:2 * chans, :] += contract_rows(branch_s[rows, :], act)

    def hidden(k, pre_s, dact_s, act_s, dpre_s):
        h, _ = place(k)
        bias = bin_[h]
        bs = jnp.zeros((8, hh), F32)
        for q in range(0, m, GROUP):
            sl = pl.ds(q, GROUP)
            pre = pre_s[sl, :] + bias
            ph = 0.5 * lax.erf(pre * (1.0 / math.sqrt(2.0))) + 0.5
            act_s[sl, :] = (pre * ph).astype(BF16)
            slope = ph + pre * (jnp.exp(-0.5 * pre * pre) * (1.0 / math.sqrt(2.0 * math.pi)))
            dpre = dact_s[sl, :] * slope
            bs = bs + over_rows(dpre)
            dpre_s[sl, :] = dpre.astype(BF16)
        bsum[h] += bs

    def send_near(h):
        prows = 2 * chans // near
        for p in range(near):
            halves[h, p] = grads[h, p * prows:(p + 1) * prows, :].astype(BF16)
        got[h, a] = halves[h, a]

        def go(o):
            p, device = near_id(o)
            remote(halves.at[h, p], got.at[h, a], near_sem.at[h, 0, o], near_sem.at[h, 1, a], device).start()

        loop(1, near, go)

    def pass_far(h):
        def wait(o):
            p, device = near_id(near - o)
            remote(halves.at[h, p], got.at[h, p], near_sem.at[h, 0, o], near_sem.at[h, 1, p], device).wait()

        loop(1, near, wait)
        tot = got[h, 0].astype(F32)
        for p in range(1, near):
            tot = tot + got[h, p].astype(F32)
        mid[h] = tot.astype(BF16)
        far_got[h, plane] = mid[h]

        def go(o):
            p, device = far_id(o)
            remote(mid.at[h], far_got.at[h, plane], far_sem.at[h, 0, o], far_sem.at[h, 1, plane], device).start()

        loop(1, far, go)

    def pass_back(h):
        def wait(o):
            p, device = far_id(far - o)
            remote(mid.at[h], far_got.at[h, p], far_sem.at[h, 0, o], far_sem.at[h, 1, p], device).wait()

        loop(1, far, wait)
        tot = far_got[h, 0].astype(F32)
        for p in range(1, far):
            tot = tot + far_got[h, p].astype(F32)
        spread[h] = tot.astype(BF16)
        whole[h, a] = spread[h]

        def go(o):
            p, device = near_id(o)
            remote(spread.at[h], whole.at[h, a], back_sem.at[h, 0, o], back_sem.at[h, 1, a], device).start()

        loop(1, near, go)

    def finish(h):
        def wait(o):
            p, device = near_id(near - o)
            remote(spread.at[h], whole.at[h, p], back_sem.at[h, 0, o], back_sem.at[h, 1, p], device).wait()

        loop(1, near, wait)
        prows = 2 * chans // near
        hs = slice(h * hh, (h + 1) * hh)
        full = whole[h].reshape(2 * chans, hh).astype(F32)
        grad_win[:, hs] = full[:chans]
        grad_wout[hs, :] = full[chans:].T

    def halo_wait(o):
        src = lax.rem(me + space - o, space)
        remote(outgo.at[o], income.at[src], halo_send.at[o], halo_recv.at[src], (dp, src)).wait()

    def stage(j):
        k = 2 * j

        @pl.when(j == (steps - 2) // 2)
        def _():
            if COMM:
                loop(1, space, halo_wait)
            loop(0, slots, border)

        if COMM:
            @pl.when(j == (steps + 2) // 2)
            def _():
                send_near(0)

        behind(jnp.maximum(k - 1, 0), act_b, dpre_b)
        ahead(k + 1, pre_b, dact_b)
        hidden(k, pre_a, dact_a, act_a, dpre_a)
        behind(k, act_a, dpre_a)
        ahead(jnp.minimum(k + 2, total - 1), pre_a, dact_a)
        hidden(k + 1, pre_b, dact_b, act_b, dpre_b)

    ahead(0, pre_a, dact_a)
    loop(0, steps, stage)
    behind(total - 1, act_b, dpre_b)
    if COMM:
        pass_far(0)
        send_near(1)
    edge_rows = pl.ds(main, m)
    dnorm_b[...] = jnp.dot(jnp.concatenate([dpre_all[0, edge_rows, :], dpre_all[1, edge_rows, :]], axis=1), win_t[...],
                           preferred_element_type=F32)

    def merge(t):
        for ref in (nhat_s, inv_s):
            for s in (1, 3, 0, 2):
                v = ref[pl.ds(pl.multiple_of(main + (t * 4 + s) * width, 8), width), :]
                if s == 1:
                    ref[pl.ds(t * area + width - 1, width, stride=width), :] = v
                elif s == 3:
                    ref[pl.ds(t * area, width, stride=width), :] = v
                elif s == 0:
                    ref[pl.ds(pl.multiple_of(t * area, 8), width), :] = v
                else:
                    ref[pl.ds(pl.multiple_of(t * area + area - width, 8), width), :] = v

    loop(0, slots, merge)

    lper = width // LAST_ROWS
    lrows = LAST_ROWS * width

    def product(step, both, weight, rows_s):
        rows = pl.ds(pl.multiple_of(step * lrows, 16), lrows)
        rows_s[...] = jnp.dot(jnp.concatenate([both[0, rows, :], both[1, rows, :]], axis=1), weight[...],
                              preferred_element_type=F32)

    def piped(lo, hi, both, weight, use):
        product(lo, both, weight, rows_a)

        def pair(j):
            k = lo + 2 * j
            product(k + 1, both, weight, rows_b)
            use(k, rows_a)
            product(jnp.minimum(k + 2, hi - 1), both, weight, rows_a)
            use(k + 1, rows_b)

        loop(0, (hi - lo) // 2, pair)

    def with_border(t, top, rows_s, edges):
        at = t * 4 * width
        rows_s[pl.ds(width - 1, LAST_ROWS, stride=width), :] = edges[pl.ds(pl.multiple_of(at + width + top, 8), LAST_ROWS), :]
        rows_s[pl.ds(0, LAST_ROWS, stride=width), :] = edges[pl.ds(pl.multiple_of(at + 3 * width + top, 8), LAST_ROWS), :]
        out = []
        for r in range(LAST_ROWS):
            v = rows_s[pl.ds(r * width, width), :]
            if r == 0:
                v = jnp.where(top == 0, edges[pl.ds(pl.multiple_of(at, 8), width), :], v)
            if r == LAST_ROWS - 1:
                v = jnp.where(top == width - LAST_ROWS, edges[pl.ds(pl.multiple_of(at + 2 * width, 8), width), :], v)
            out.append(v)
        return out

    def last(step, rows_s):
        t = step // lper
        top = pl.multiple_of((step - t * lper) * LAST_ROWS, 8)
        live = jnp.where(t < count, 1.0, 0.0)
        start = pl.multiple_of(t * area + top * width, 16)
        dn = with_border(t, top, rows_s, dnorm_b)
        taps = [[jnp.zeros((8, chans), F32)] * 3 for _ in range(3)]
        s_g = s_dn = s_dnh = s_dc = jnp.zeros((8, chans), F32)
        dconv = {}
        for fr in range(LAST_ROWS + 2):
            r = fr
            if r < LAST_ROWS:
                sl = pl.ds(pl.multiple_of(start + r * width, 16), width)
                s_g = s_g + over_rows(cotan[t, top + r].astype(F32))
                dnorm = dn[r]
                nhat = nhat_s[sl, :]
                dnh = dnorm * nhat
                s_dn = s_dn + over_rows(dnorm)
                s_dnh = s_dnh + over_rows(dnh)
                m1 = jnp.mean(dnorm * gain[...], axis=-1, keepdims=True)
                m2 = jnp.mean(dnh * gain[...], axis=-1, keepdims=True)
                dc = inv_s[sl, :] * (dnorm * gain[...] - m1 - nhat * m2)
                s_dc = s_dc + over_rows(dc)
                dconv[r] = dc
            base = (top + fr) * PITCH + 7
            win3 = [frame[t, pl.ds(base + b, width), :] for b in range(3)]
            for x in range(3):
                r = fr - x
                if 0 <= r < LAST_ROWS:
                    for b in range(3):
                        taps[x][b] = taps[x][b] + over_rows(dconv[r] * win3[b])
            dconv.pop(fr - 2, None)
        for n, s in enumerate([taps[x][b] for x in range(3) for b in range(3)] + [s_dc, s_dnh, s_dn, s_g * live]):
            sums[n] += s
        if COMM:
            @pl.when(step == slots * lper * 3 // 4)
            def _():
                pass_far(1)

    def finalize(step, rows_s):
        t = step // lper
        top = pl.multiple_of((step - t * lper) * LAST_ROWS, 8)
        live = jnp.where(t < count, 1.0, 0.0)
        start = pl.multiple_of(t * area + top * width, 16)
        proj = with_border(t, top, rows_s, proj_b)
        for r in range(LAST_ROWS):
            x = tile[t, top + r].astype(F32)
            result[t, top + r] = ((x + scale[...] * (proj[r] + bout[...])) * live).astype(BF16)

        @pl.when(top == width - LAST_ROWS)
        def _():
            pltpu.make_async_copy(result.at[t], out.at[t], out_sem.at[t]).start()

    def finalize_all(lo, hi):
        piped(lo, hi, act_all, wout, finalize)

    piped(0, slots * lper, dpre_all, win_t, last)

    tot = jnp.sum(sums[...], axis=1)
    small[...] = jnp.zeros_like(small)
    g_proj = jnp.zeros((8, chans), F32)
    for h in range(2):
        g_proj = g_proj + over_rows(grads[h, chans:2 * chans, :].T * wout[h * hh:(h + 1) * hh, :].astype(F32))
    small[0:12, :] = tot[0:12]
    small[12:13, :] = tot[12:13] * scale[...]
    small[13:14, :] = jnp.sum(g_proj, axis=0, keepdims=True) / scale[...] + tot[12:13] * bout[...]
    b = jnp.sum(bsum[...], axis=1)
    per_h = hh // chans
    for h in range(2):
        for n in range(per_h):
            k = 14 + h * per_h + n
            small[k:k + 1, :] = b[h:h + 1, n * chans:(n + 1) * chans]
    def write_small(v):
        channel_out[...] = v[0:14]
        for n in range(hid // chans):
            bias_out[:, n * chans:(n + 1) * chans] = v[14 + n:15 + n]

    proj_b[...] = jnp.dot(jnp.concatenate([act_all[0, edge_rows, :], act_all[1, edge_rows, :]], axis=1), wout[...],
                          preferred_element_type=F32)
    if not COMM:
        write_small(small[...])
        for h in range(2):
            grad_win[:, h * hh:(h + 1) * hh] = grads[h, 0:chans, :]
            grad_wout[h * hh:(h + 1) * hh, :] = grads[h, chans:2 * chans, :].T
        finalize_all(0, slots * lper)
        for c in final_copies:
            c.start()
        for t in range(slots):
            pltpu.make_async_copy(result.at[t], out.at[t], out_sem.at[t]).wait()
        for c in final_copies:
            c.wait()
        return

    small_got[a] = small[...]

    def small_near(o):
        p, device = near_id(o)
        remote(small, small_got.at[a], sn_sem.at[0, o], sn_sem.at[1, a], device).start()

    def small_near_wait(o):
        p, device = near_id(near - o)
        remote(small, small_got.at[p], sn_sem.at[0, o], sn_sem.at[1, p], device).wait()

    def small_far_go(o):
        p, device = far_id(o)
        remote(small_mid, small_far.at[plane], sf_sem.at[0, o], sf_sem.at[1, plane], device).start()

    def small_far_wait(o):
        p, device = far_id(far - o)
        remote(small_mid, small_far.at[p], sf_sem.at[0, o], sf_sem.at[1, p], device).wait()

    loop(1, near, small_near)
    pass_back(0)
    finalize_all(0, slots * lper // 2)
    loop(1, near, small_near_wait)
    s = small_got[0]
    for p in range(1, near):
        s = s + small_got[p]
    small_mid[...] = s
    small_far[plane] = s
    loop(1, far, small_far_go)
    pass_back(1)
    finalize_all(slots * lper // 2, slots * lper)
    finish(0)
    for t in range(slots):
        pltpu.make_async_copy(result.at[t], out.at[t], out_sem.at[t]).wait()
    finish(1)
    for c in final_copies[:2]:
        c.start()
    loop(1, far, small_far_wait)
    s = small_far[0]
    for p in range(1, far):
        s = s + small_far[p]
    write_small(s)
    for c in final_copies[2:]:
        c.start()
    for c in final_copies:
        c.wait()


def publish_kernel(*refs):
    n = len(refs) // 2
    srcs, dsts, sems = refs[:n], refs[n:2 * n], refs[2 * n]
    copies = []
    for t in range(srcs[0].shape[0]):
        copies.append(pltpu.make_async_copy(srcs[0].at[t], dsts[0].at[t], sems.at[len(copies)]))
    for src, dst in zip(srcs[1:], dsts[1:]):
        copies.append(pltpu.make_async_copy(src, dst, sems.at[len(copies)]))
    for c in copies:
        c.start()
    for c in copies:
        c.wait()


def publish(*arrays):
    anyw = pl.BlockSpec(memory_space=pl.ANY)
    return pl.pallas_call(
        publish_kernel,
        in_specs=[anyw] * len(arrays),
        out_specs=[anyw] * len(arrays),
        out_shape=[jax.ShapeDtypeStruct(v.shape, v.dtype) for v in arrays],
        scratch_shapes=[pltpu.SemaphoreType.DMA((arrays[0].shape[0] + len(arrays) - 1,))],
        compiler_params=pltpu.CompilerParams(vmem_limit_bytes=60 * 2**20),
    )(*arrays)


def block(space, near, nbrs, turns, counts, fields, cotan, kern, dbias, gain, nbias, win, bin_, wout, bout, scale):
    slots, width, _, chans = fields.shape
    hid = win.shape[1]
    hh = hid // 2
    far = space // 2
    main, edge = slots * width * width, slots * 4 * width
    row = lambda v: v.reshape(1, -1)
    anyw = pl.BlockSpec(memory_space=pl.ANY)
    ints = lambda *s: pltpu.SMEM(s, jnp.int32)
    dma = lambda *s: pltpu.SemaphoreType.DMA(s)
    v = lambda dt, *s: pltpu.VMEM(s, dt)
    piece = (2 * chans // near, hh)
    line = (width, chans)
    return pl.pallas_call(
        functools.partial(block_kernel, space, near),
        in_specs=[anyw] * 14,
        out_specs=[anyw] * 5,
        out_shape=[jax.ShapeDtypeStruct(fields.shape, BF16), jax.ShapeDtypeStruct((chans, hid), F32),
                   jax.ShapeDtypeStruct((hid, chans), F32), jax.ShapeDtypeStruct((14, chans), F32),
                   jax.ShapeDtypeStruct((1, hid), F32)],
        scratch_shapes=[
            ints(*nbrs.shape), ints(*turns.shape), ints(*counts.shape), v(F32, 3, 3, chans), v(F32, 1, chans),
            v(F32, 1, chans), v(F32, 1, chans), v(F32, 2, 1, hh), v(F32, 1, chans), v(BF16, chans, hid),
            v(F32, 1, chans), v(BF16, hid, chans),
            v(F32, chans, hid), v(F32, hid, chans), v(F32, 14, chans), v(F32, 1, hid), dma(12), dma(4),
            v(BF16, *fields.shape), v(BF16, *fields.shape), v(F32, slots, (width + 2) * PITCH + 8, chans),
            v(BF16, hid, chans), v(BF16, 2, chans, hh), v(BF16, 2, chans, hh),
            v(F32, main + edge, chans), v(F32, main + edge, chans),
            v(BF16, main + edge, chans), v(BF16, main + edge, chans),
            v(BF16, 2, main + edge, hh), v(BF16, 2, main + edge, hh),
            v(F32, edge, hh), v(F32, edge, hh), v(F32, edge, hh), v(F32, edge, hh),
            v(BF16, edge, hh), v(BF16, edge, hh), v(BF16, edge, hh), v(BF16, edge, hh),
            v(F32, edge, chans), v(F32, edge, chans), v(F32, LAST_ROWS * width, chans), v(F32, LAST_ROWS * width, chans),
            v(BF16, *fields.shape),
            v(F32, width * 16, chans), pltpu.SMEM((space,), jnp.int32),
            v(F32, 2, 2 * chans, hh), v(F32, 13, 8, chans), v(F32, 2, 8, hh), v(F32, 24, chans),
            v(BF16, 8 * slots, *line), v(BF16, space, *line), v(BF16, space, *line),
            v(BF16, 2, near, *piece), v(BF16, 2, near, *piece), v(BF16, 2, *piece), v(BF16, 2, far, *piece),
            v(BF16, 2, *piece), v(BF16, 2, near, *piece),
            v(F32, near, 24, chans), v(F32, 24, chans), v(F32, far, 24, chans),
            dma(2, slots), dma(slots), dma(space), dma(space), dma(2, 2, near), dma(2, 2, far), dma(2, 2, near),
            dma(2, near), dma(2, far)],
        compiler_params=pltpu.CompilerParams(
            vmem_limit_bytes=60 * 2**20, **(dict(collective_id=0, has_side_effects=True) if COMM else {})),
    )(fields, cotan, nbrs, turns, counts, kern, row(dbias), row(gain), row(nbias), bin_.reshape(2, 1, hh), row(scale),
      win, row(bout), wout)


def local(fields, cotangent, neighbours, rotations, tile_counts, depth_kernel, depth_bias, norm_gain, norm_bias,
          weight_in, bias_in, weight_out, bias_out, layer_scale, shape):
    result, grad_win, grad_wout, channel, bias = publish(*block(
        shape["space"], 2 * shape["dp"], neighbours.T, rotations.T, tile_counts, fields[0], cotangent[0], depth_kernel,
        depth_bias, norm_gain, norm_bias, weight_in, bias_in, weight_out, bias_out, layer_scale))
    return result[None], grad_win, grad_wout, bias.reshape(-1), channel


def solution(mesh):
    placed = P("dp", "space", None, None, None)
    return jax.shard_map(
        functools.partial(local, shape=dict(mesh.shape)),
        mesh=mesh,
        in_specs=(placed, placed) + (P(),) * 12,
        out_specs=(placed, P(), P(), P(), P()),
        check_vma=False,
    )
```

```python
import functools
import math

import jax
import jax.numpy as jnp
from jax import lax
from jax.experimental import pallas as pl
from jax.experimental.pallas import tpu as pltpu
from jax.sharding import PartitionSpec as P

F32, BF16 = jnp.float32, jnp.bfloat16
MESH = pl.DeviceIdType.MESH
PITCH = 64
CONV_ROWS = 16
LAST_ROWS = 16
GROUP = 64
UNROLL = 2
COMM = True


def over_rows(a):
    return jnp.sum(a.reshape(-1, 8, a.shape[-1]), axis=0)


def contract_rows(a, b):
    return lax.dot_general(a, b, (((0,), (0,)), ((), ())), preferred_element_type=F32)


def remote(src, dst, send_sem, recv_sem, device):
    return pltpu.make_async_remote_copy(
        src_ref=src, dst_ref=dst, send_sem=send_sem, recv_sem=recv_sem, device_id=device, device_id_type=MESH
    )


def loop(lo, hi, body, unroll=1):
    def step(i, c):
        body(i)
        return c

    lax.fori_loop(lo, hi, step, 0, unroll=unroll)


def block_kernel(space, near, fields, cotangent, *refs):
    slots, width, _, chans = fields.shape
    held, outs, scratch = refs[:12], refs[12:17], refs[17:]
    kept, made, rest = scratch[:12], scratch[12:16], scratch[16:]
    in_sem, out_sem = rest[:2]
    first = [pltpu.make_async_copy(held[n], kept[n], in_sem.at[n]) for n in range(12)]
    for n in (9, 11, 0, 1, 2, 3, 4, 5, 6, 7, 8, 10):
        first[n].start()
    last = [pltpu.make_async_copy(made[n], outs[n + 1], out_sem.at[n]) for n in range(4)]
    body(space, near, fields, cotangent, *kept, outs[0], *made, first, last, *rest[2:])


def body(space, near, fields, cotangent, nbrs, turns, counts, taps_w, dbias, gain, nbias, bin_, scale, win, bout, wout,
         out, grad_win, grad_wout, channel_out, bias_out, first, final_copies,
                 tile, cotan, frame, win_t, wout_t, win_h, nhat_s, inv_s, normed_s, branch_s, act_all, dpre_all,
                 pre_a, pre_b, dact_a, dact_b, act_a, act_b, dpre_a, dpre_b, proj_b, dnorm_b, rows_a, rows_b,
                 cot_s, codes, grads, sums, bsum, small, cand, outgo, income, halves, got, mid, far_got, spread, whole,
                 small_got, small_mid, small_far, parts,
                 load_sem, out_sem, halo_send, halo_recv, near_sem, far_sem, back_sem, sn_sem, sf_sem):
    slots, width, _, chans = tile.shape
    hid = win.shape[1]
    hh = hid // 2
    area = width * width
    main = slots * area
    m = act_a.shape[0]
    shift = slots.bit_length() - 1
    picks = 4 * slots
    far = space // 2
    if COMM:
        dp, me = lax.axis_index("dp"), lax.axis_index("space")
        core, plane = lax.rem(me, 2), me // 2
        a = dp * 2 + core
    else:
        me = 0
    loads = []
    for t in range(slots):
        loads.append((pltpu.make_async_copy(fields.at[t], tile.at[t], load_sem.at[0, t]),
                      pltpu.make_async_copy(cotangent.at[t], cotan.at[t], load_sem.at[1, t])))
    for t in range(slots):
        loads[t][0].start()
    for t in range(slots):
        loads[t][1].start()

    def near_id(o):
        p = lax.rem(a + o, near)
        return p, (p // 2, plane * 2 + lax.rem(p, 2))

    def far_id(o):
        p = lax.rem(plane + o, far)
        return p, (dp, p * 2 + core)

    if COMM:
        barrier = pltpu.get_barrier_semaphore()
        loop(1, space, lambda o: pl.semaphore_signal(
            barrier, inc=1, device_id=(dp, lax.rem(me + o, space)), device_id_type=MESH))
        loop(1, near, lambda o: pl.semaphore_signal(barrier, inc=1, device_id=near_id(o)[1], device_id_type=MESH))

    for c in first:
        c.wait()
    win_t[...] = win[...].T
    for h in range(2):
        win_h[h] = win[:, h * hh:(h + 1) * hh]
        wout_t[h] = wout[h * hh:(h + 1) * hh, :].T
    grads[...] = jnp.zeros_like(grads)
    sums[...] = jnp.zeros_like(sums)
    bsum[...] = jnp.zeros_like(bsum)
    act_b[...] = jnp.zeros_like(act_b)
    dpre_b[...] = jnp.zeros_like(dpre_b)

    def pick_code(k, nbr, turn):
        side = k & 3
        edge = (turn + (side + 2)) & 3
        flip = ((turn + (side & 1)) >> 1) & 1
        return flip * picks + 4 * (nbr & (slots - 1)) + edge

    if COMM:
        def scan(o):
            peer = lax.rem(me + o, space)
            hit = jnp.int32(0)
            for k in range(picks):
                nbr = nbrs[k & 3, peer * slots + (k >> 2)]
                hit = jnp.where((nbr >> shift) == me, k, hit)
            slot = peer * slots + (hit >> 2)
            codes[o] = pick_code(hit, nbrs[hit & 3, slot], turns[hit & 3, slot])

        loop(0, space, scan)

    def clear(t):
        frame[t, 0:PITCH, :] = jnp.zeros((PITCH, chans), F32)
        frame[t, pl.ds((width + 1) * PITCH, PITCH + 8), :] = jnp.zeros((PITCH + 8, chans), F32)

        def side(r):
            frame[t, pl.ds(pl.multiple_of((r + 1) * PITCH, 8), 8), :] = jnp.zeros((8, chans), F32)
            frame[t, pl.ds(pl.multiple_of((r + 1) * PITCH + 8 + width, 8), 8), :] = jnp.zeros((8, chans), F32)
            frame[t, pl.ds(pl.multiple_of((r + 1) * PITCH + 8, 8), width), :] = tile[t, r].astype(F32)

        loop(0, width, side, 4)

    def edge_of(k, q):
        t = k
        if q == 0:
            return frame[t, pl.ds(PITCH + 8, width), :]
        if q == 1:
            return frame[t, pl.ds(PITCH + 7 + width, width, stride=PITCH), :]
        if q == 2:
            return frame[t, pl.ds(width * PITCH + 8, width), :]
        return frame[t, pl.ds(PITCH + 8, width, stride=PITCH), :]

    for t in range(slots):
        loads[t][0].wait()
        clear(t)
    i = lax.broadcasted_iota(jnp.int32, (width, width), 0)
    j = lax.broadcasted_iota(jnp.int32, (width, width), 1)
    mirror = (i + j == width - 1).astype(BF16)

    def candidates(t):
        for q in range(4):
            line = edge_of(t, q).astype(BF16)
            cand[4 * t + q] = line
            cand[picks + 4 * t + q] = jnp.dot(mirror, line, preferred_element_type=F32).astype(BF16)

    loop(0, slots, candidates)

    if COMM:
        def gather(o):
            outgo[o] = cand[codes[o]]

        loop(0, space, gather, 4)
        income[me] = outgo[0]
        pl.semaphore_wait(barrier, space + near - 2)

        loop(1, space, lambda o: remote(
            outgo.at[o], income.at[me], halo_send.at[o], halo_recv.at[me], (dp, lax.rem(me + o, space))).start())

    for t in range(slots):
        loads[t][1].wait()

    count = counts[me]
    px = lax.broadcasted_iota(jnp.int32, (width, chans), 0)
    inner = ((px > 0) & (px < width - 1)).astype(F32)

    def norm_rows(conv, at):
        x = conv - jnp.mean(conv, axis=-1, keepdims=True)
        iv = lax.rsqrt(jnp.mean(x * x, axis=-1, keepdims=True) + 1e-06)
        nhat = x * iv
        sl = pl.ds(pl.multiple_of(at, 16), width)
        inv_s[sl, :] = jnp.broadcast_to(iv, (width, chans))
        nhat_s[sl, :] = nhat
        normed_s[sl, :] = (nhat * gain[...] + nbias[...]).astype(BF16)

    per = width // CONV_ROWS

    def conv_chunk(step):
        t = step // per
        top = (step - t * per) * CONV_ROWS
        live = jnp.where(t < count, 1.0, 0.0)
        kern = [[taps_w[x, y:y + 1, :] for y in range(3)] for x in range(3)]
        bias = dbias[...]
        conv = {}
        for fr in range(CONV_ROWS + 2):
            base = (top + fr) * PITCH + 7
            win3 = [frame[t, pl.ds(base + b, width), :] for b in range(3)]
            for x in range(3):
                r = fr - x
                if 0 <= r < CONV_ROWS:
                    acc = conv.get(r, bias)
                    for b in range(3):
                        acc = acc + win3[b] * kern[x][b]
                    conv[r] = acc
            r = fr - 2
            if r >= 0:
                at = t * area + (top + r) * width
                norm_rows(conv.pop(r), at)
                inside = jnp.where((top + r > 0) & (top + r < width - 1), live, 0.0)
                g = cotan[t, top + r].astype(F32) * inside
                branch_s[pl.ds(pl.multiple_of(at, 16), width), :] = (g * (scale[...] * inner)).astype(BF16)

    loop(0, slots * per, conv_chunk)

    def border(t):
        live = jnp.where(t < count, 1.0, 0.0)
        kern = [[taps_w[x, y:y + 1, :] for y in range(3)] for x in range(3)]
        for s in range(4):
            if COMM:
                line = income[nbrs[s, me * slots + t] >> shift]
            else:
                line = cand[pick_code(s, nbrs[s, t], turns[s, t])]
            line = line.astype(F32)
            if s == 0:
                frame[t, pl.ds(8, width), :] = line
            elif s == 1:
                frame[t, pl.ds(PITCH + 8 + width, width, stride=PITCH), :] = line
            elif s == 2:
                frame[t, pl.ds((width + 1) * PITCH + 8, width), :] = line
            else:
                frame[t, pl.ds(PITCH + 7, width, stride=PITCH), :] = line

        def cots(r):
            cot_s[pl.ds(pl.multiple_of(r * 16, 8), 8), :] = cotan[t, r, 0:16, :].astype(F32)[0:8]
            cot_s[pl.ds(pl.multiple_of(r * 16 + 8, 8), 8), :] = cotan[t, r, width - 16:width, :].astype(F32)[8:16]

        loop(0, width, cots, 4)
        for s in range(4):
            acc = dbias[...]
            for x in range(3):
                for b in range(3):
                    if s == 0:
                        w = frame[t, pl.ds(x * PITCH + 7 + b, width), :]
                    elif s == 1:
                        w = frame[t, pl.ds(x * PITCH + 6 + width + b, width, stride=PITCH), :]
                    elif s == 2:
                        w = frame[t, pl.ds((width - 1 + x) * PITCH + 7 + b, width), :]
                    else:
                        w = frame[t, pl.ds(x * PITCH + 7 + b, width, stride=PITCH), :]
                    acc = acc + w * taps_w[x, b:b + 1, :]
            at = main + (t * 4 + s) * width
            norm_rows(acc, at)
            if s == 0:
                g = cotan[t, 0].astype(F32)
            elif s == 1:
                g = cot_s[pl.ds(15, width, stride=16), :] * inner
            elif s == 2:
                g = cotan[t, width - 1].astype(F32)
            else:
                g = cot_s[pl.ds(0, width, stride=16), :] * inner
            branch_s[pl.ds(pl.multiple_of(at, 16), width), :] = (g * live * scale[...]).astype(BF16)

    steps = (main + slots * 4 * width) // m
    total = 2 * steps

    def place(k):
        h = k // steps
        return h, pl.ds(pl.multiple_of((k - h * steps) * m, 16), m)

    def ahead(k, pre_s, dact_s):
        h, rows = place(k)
        pre_s[...] = jnp.dot(normed_s[rows, :], win_h[h], preferred_element_type=F32)
        dact_s[...] = jnp.dot(branch_s[rows, :], wout_t[h], preferred_element_type=F32)

    def behind(k, act_s, dpre_s):
        h, rows = place(k)
        act = act_s[...]
        dpre = dpre_s[...]
        act_all[h, rows, :] = act
        dpre_all[h, rows, :] = dpre
        grads[h, 0:chans, :] += contract_rows(normed_s[rows, :], dpre)
        grads[h, chans:2 * chans, :] += contract_rows(branch_s[rows, :], act)

    def hidden(k, pre_s, dact_s, act_s, dpre_s):
        h, _ = place(k)
        bias = bin_[h]
        bs = jnp.zeros((8, hh), F32)
        for q in range(0, m, GROUP):
            sl = pl.ds(q, GROUP)
            pre = pre_s[sl, :] + bias
            ph = 0.5 * lax.erf(pre * (1.0 / math.sqrt(2.0))) + 0.5
            act_s[sl, :] = (pre * ph).astype(BF16)
            slope = ph + pre * (jnp.exp(-0.5 * pre * pre) * (1.0 / math.sqrt(2.0 * math.pi)))
            dpre = dact_s[sl, :] * slope
            bs = bs + over_rows(dpre)
            dpre_s[sl, :] = dpre.astype(BF16)
        bsum[h] += bs

    def send_near(h):
        prows = 2 * chans // near
        for p in range(near):
            halves[h, p] = grads[h, p * prows:(p + 1) * prows, :].astype(BF16)
        got[h, a] = halves[h, a]

        def go(o):
            p, device = near_id(o)
            remote(halves.at[h, p], got.at[h, a], near_sem.at[h, 0, o], near_sem.at[h, 1, a], device).start()

        loop(1, near, go)

    def pass_far(h):
        def wait(o):
            p, device = near_id(near - o)
            remote(halves.at[h, p], got.at[h, p], near_sem.at[h, 0, o], near_sem.at[h, 1, p], device).wait()

        loop(1, near, wait)
        tot = got[h, 0].astype(F32)
        for p in range(1, near):
            tot = tot + got[h, p].astype(F32)
        mid[h] = tot.astype(BF16)
        far_got[h, plane] = mid[h]

        def go(o):
            p, device = far_id(o)
            remote(mid.at[h], far_got.at[h, plane], far_sem.at[h, 0, o], far_sem.at[h, 1, plane], device).start()

        loop(1, far, go)

    def pass_back(h):
        def wait(o):
            p, device = far_id(far - o)
            remote(mid.at[h], far_got.at[h, p], far_sem.at[h, 0, o], far_sem.at[h, 1, p], device).wait()

        loop(1, far, wait)
        tot = far_got[h, 0].astype(F32)
        for p in range(1, far):
            tot = tot + far_got[h, p].astype(F32)
        spread[h] = tot.astype(BF16)
        whole[h, a] = spread[h]

        def go(o):
            p, device = near_id(o)
            remote(spread.at[h], whole.at[h, a], back_sem.at[h, 0, o], back_sem.at[h, 1, a], device).start()

        loop(1, near, go)

    def finish(h):
        def wait(o):
            p, device = near_id(near - o)
            remote(spread.at[h], whole.at[h, p], back_sem.at[h, 0, o], back_sem.at[h, 1, p], device).wait()

        loop(1, near, wait)
        prows = 2 * chans // near
        hs = slice(h * hh, (h + 1) * hh)
        full = whole[h].reshape(2 * chans, hh).astype(F32)
        grad_win[:, hs] = full[:chans]
        grad_wout[hs, :] = full[chans:].T

    def halo_wait(o):
        src = lax.rem(me + space - o, space)
        remote(outgo.at[o], income.at[src], halo_send.at[o], halo_recv.at[src], (dp, src)).wait()

    def pair(k):
        behind(jnp.maximum(k - 1, 0), act_b, dpre_b)
        ahead(k + 1, pre_b, dact_b)
        hidden(k, pre_a, dact_a, act_a, dpre_a)
        behind(k, act_a, dpre_a)
        ahead(jnp.minimum(k + 2, total - 1), pre_a, dact_a)
        hidden(k + 1, pre_b, dact_b, act_b, dpre_b)

    def stage(i):
        @pl.when(i == (steps - 3) // 4)
        def _():
            if COMM:
                loop(1, space, halo_wait)
            loop(0, slots, border)

        if COMM:
            @pl.when(i == (steps - 3) // 4 + 1)
            def _():
                send_near(0)

        for n in range(UNROLL):
            pair(2 + 2 * UNROLL * i + 2 * n)

    ahead(0, pre_a, dact_a)
    pair(0)
    loop(0, (steps - 1) // UNROLL, stage)
    behind(total - 1, act_b, dpre_b)
    if COMM:
        pass_far(0)
        send_near(1)
    edge_rows = pl.ds(main, m)
    g_proj = jnp.zeros((8, chans), F32)
    for h in range(2):
        g_proj = g_proj + over_rows(grads[h, chans:2 * chans, :].T * wout[h * hh:(h + 1) * hh, :].astype(F32))
    parts[...] = jnp.zeros_like(parts)
    parts[13:14, :] = jnp.sum(g_proj, axis=0, keepdims=True) / scale[...]
    b = jnp.sum(bsum[...], axis=1)
    per_h = hh // chans
    for h in range(2):
        for n in range(per_h):
            k = 14 + h * per_h + n
            parts[k:k + 1, :] = b[h:h + 1, n * chans:(n + 1) * chans]
    dnorm_b[...] = jnp.dot(jnp.concatenate([dpre_all[0, edge_rows, :], dpre_all[1, edge_rows, :]], axis=1), win_t[...],
                           preferred_element_type=F32)

    def merge(t):
        for ref in (nhat_s, inv_s):
            for s in (1, 3, 0, 2):
                v = ref[pl.ds(pl.multiple_of(main + (t * 4 + s) * width, 8), width), :]
                if s == 1:
                    ref[pl.ds(t * area + width - 1, width, stride=width), :] = v
                elif s == 3:
                    ref[pl.ds(t * area, width, stride=width), :] = v
                elif s == 0:
                    ref[pl.ds(pl.multiple_of(t * area, 8), width), :] = v
                else:
                    ref[pl.ds(pl.multiple_of(t * area + area - width, 8), width), :] = v

    loop(0, slots, merge)

    lper = width // LAST_ROWS
    lrows = LAST_ROWS * width

    def product(step, both, weight, rows_s):
        rows = pl.ds(pl.multiple_of(step * lrows, 16), lrows)
        rows_s[...] = jnp.dot(jnp.concatenate([both[0, rows, :], both[1, rows, :]], axis=1), weight[...],
                              preferred_element_type=F32)

    def piped(lo, hi, both, weight, use, hook=None):
        product(lo, both, weight, rows_a)

        def pair(j):
            k = lo + 2 * j
            if hook is not None:
                hook(j)
            product(k + 1, both, weight, rows_b)
            use(k, rows_a)
            product(jnp.minimum(k + 2, hi - 1), both, weight, rows_a)
            use(k + 1, rows_b)

        loop(0, (hi - lo) // 2, pair)

    def with_border(t, top, rows_s, edges):
        at = t * 4 * width
        rows_s[pl.ds(width - 1, LAST_ROWS, stride=width), :] = edges[pl.ds(pl.multiple_of(at + width + top, 8), LAST_ROWS), :]
        rows_s[pl.ds(0, LAST_ROWS, stride=width), :] = edges[pl.ds(pl.multiple_of(at + 3 * width + top, 8), LAST_ROWS), :]
        out = []
        for r in range(LAST_ROWS):
            v = rows_s[pl.ds(r * width, width), :]
            if r == 0:
                v = jnp.where(top == 0, edges[pl.ds(pl.multiple_of(at, 8), width), :], v)
            if r == LAST_ROWS - 1:
                v = jnp.where(top == width - LAST_ROWS, edges[pl.ds(pl.multiple_of(at + 2 * width, 8), width), :], v)
            out.append(v)
        return out

    def last(step, rows_s):
        t = step // lper
        top = pl.multiple_of((step - t * lper) * LAST_ROWS, 8)
        live = jnp.where(t < count, 1.0, 0.0)
        start = pl.multiple_of(t * area + top * width, 16)
        dn = with_border(t, top, rows_s, dnorm_b)
        taps = [[jnp.zeros((8, chans), F32)] * 3 for _ in range(3)]
        s_g = s_dn = s_dnh = s_dc = jnp.zeros((8, chans), F32)
        dconv = {}
        for fr in range(LAST_ROWS + 2):
            r = fr
            if r < LAST_ROWS:
                sl = pl.ds(pl.multiple_of(start + r * width, 16), width)
                s_g = s_g + over_rows(cotan[t, top + r].astype(F32))
                dnorm = dn[r]
                nhat = nhat_s[sl, :]
                dnh = dnorm * nhat
                s_dn = s_dn + over_rows(dnorm)
                s_dnh = s_dnh + over_rows(dnh)
                m1 = jnp.mean(dnorm * gain[...], axis=-1, keepdims=True)
                m2 = jnp.mean(dnh * gain[...], axis=-1, keepdims=True)
                dc = inv_s[sl, :] * (dnorm * gain[...] - m1 - nhat * m2)
                s_dc = s_dc + over_rows(dc)
                dconv[r] = dc
            base = (top + fr) * PITCH + 7
            win3 = [frame[t, pl.ds(base + b, width), :] for b in range(3)]
            for x in range(3):
                r = fr - x
                if 0 <= r < LAST_ROWS:
                    for b in range(3):
                        taps[x][b] = taps[x][b] + over_rows(dconv[r] * win3[b])
            dconv.pop(fr - 2, None)
        for n, s in enumerate([taps[x][b] for x in range(3) for b in range(3)] + [s_dc, s_dnh, s_dn, s_g * live]):
            sums[n] += s
    def finalize(step, rows_s):
        t = step // lper
        top = pl.multiple_of((step - t * lper) * LAST_ROWS, 8)
        live = jnp.where(t < count, 1.0, 0.0)
        start = pl.multiple_of(t * area + top * width, 16)
        proj = with_border(t, top, rows_s, proj_b)
        for r in range(LAST_ROWS):
            x = tile[t, top + r].astype(F32)
            tile[t, top + r] = ((x + scale[...] * (proj[r] + bout[...])) * live).astype(BF16)

        @pl.when(top == width - LAST_ROWS)
        def _():
            pltpu.make_async_copy(tile.at[t], out.at[t], out_sem.at[t]).start()

    def small_near(o):
        p, device = near_id(o)
        remote(small, small_got.at[a], sn_sem.at[0, o], sn_sem.at[1, a], device).start()

    def finalize_all(lo, hi):
        piped(lo, hi, act_all, wout, finalize)

    def between(j):
        if COMM:
            @pl.when(j == slots * lper // 2 * 2 // 3)
            def _():
                pass_far(1)

    piped(0, slots * lper, dpre_all, win_t, last, between)

    tot = jnp.sum(sums[...], axis=1)
    parts[0:12, :] = tot[0:12]
    parts[12:13, :] = tot[12:13] * scale[...]
    parts[13:14, :] += tot[12:13] * bout[...]
    small[...] = parts[...].astype(BF16)
    if COMM:
        small_got[a] = small[...]
        loop(1, near, small_near)

    def write_small(v):
        channel_out[...] = v[0:14]
        for n in range(hid // chans):
            bias_out[:, n * chans:(n + 1) * chans] = v[14 + n:15 + n]

    proj_b[...] = jnp.dot(jnp.concatenate([act_all[0, edge_rows, :], act_all[1, edge_rows, :]], axis=1), wout[...],
                          preferred_element_type=F32)
    if not COMM:
        write_small(parts[...])
        for h in range(2):
            grad_win[:, h * hh:(h + 1) * hh] = grads[h, 0:chans, :]
            grad_wout[h * hh:(h + 1) * hh, :] = grads[h, chans:2 * chans, :].T
        finalize_all(0, slots * lper)
        for c in final_copies:
            c.start()
        for t in range(slots):
            pltpu.make_async_copy(tile.at[t], out.at[t], out_sem.at[t]).wait()
        for c in final_copies:
            c.wait()
        return

    def small_near_wait(o):
        p, device = near_id(near - o)
        remote(small, small_got.at[p], sn_sem.at[0, o], sn_sem.at[1, p], device).wait()

    def small_far_go(o):
        p, device = far_id(o)
        remote(small_mid, small_far.at[plane], sf_sem.at[0, o], sf_sem.at[1, plane], device).start()

    def small_far_wait(o):
        p, device = far_id(far - o)
        remote(small_mid, small_far.at[p], sf_sem.at[0, o], sf_sem.at[1, p], device).wait()

    pass_back(0)
    finalize_all(0, slots * lper // 2)
    loop(1, near, small_near_wait)
    s = small_got[0].astype(F32)
    for p in range(1, near):
        s = s + small_got[p].astype(F32)
    small_mid[...] = s.astype(BF16)
    small_far[plane] = small_mid[...]
    loop(1, far, small_far_go)
    pass_back(1)
    finalize_all(slots * lper // 2, slots * lper)
    finish(0)
    for t in range(slots):
        pltpu.make_async_copy(tile.at[t], out.at[t], out_sem.at[t]).wait()
    finish(1)
    for c in final_copies[:2]:
        c.start()
    loop(1, far, small_far_wait)
    s = small_far[0].astype(F32)
    for p in range(1, far):
        s = s + small_far[p].astype(F32)
    write_small(s)
    for c in final_copies[2:]:
        c.start()
    for c in final_copies:
        c.wait()


def publish_kernel(*refs):
    n = (len(refs) - 1) // 3
    srcs, dsts, held, sems = refs[:n], refs[n:2 * n], refs[2 * n:3 * n], refs[3 * n]
    parts = [(srcs[0].at[t], held[0].at[t], dsts[0].at[t]) for t in range(srcs[0].shape[0])]
    parts += list(zip(srcs[1:], held[1:], dsts[1:]))
    ins = [pltpu.make_async_copy(src, mid, sems.at[0, i]) for i, (src, mid, _) in enumerate(parts)]
    outs = [pltpu.make_async_copy(mid, dst, sems.at[1, i]) for i, (_, mid, dst) in enumerate(parts)]
    for c in ins:
        c.start()
    for c, d in zip(ins, outs):
        c.wait()
        d.start()
    for d in outs:
        d.wait()


def publish(*arrays):
    anyw = pl.BlockSpec(memory_space=pl.ANY)
    return pl.pallas_call(
        publish_kernel,
        in_specs=[anyw] * len(arrays),
        out_specs=[anyw] * len(arrays),
        out_shape=[jax.ShapeDtypeStruct(v.shape, v.dtype) for v in arrays],
        scratch_shapes=[pltpu.VMEM(v.shape, v.dtype) for v in arrays]
        + [pltpu.SemaphoreType.DMA((2, arrays[0].shape[0] + len(arrays) - 1))],
        compiler_params=pltpu.CompilerParams(vmem_limit_bytes=60 * 2**20),
    )(*arrays)


def block(space, near, nbrs, turns, counts, fields, cotan, kern, dbias, gain, nbias, win, bin_, wout, bout, scale):
    slots, width, _, chans = fields.shape
    hid = win.shape[1]
    hh = hid // 2
    far = space // 2
    main, edge = slots * width * width, slots * 4 * width
    row = lambda v: v.reshape(1, -1)
    anyw = pl.BlockSpec(memory_space=pl.ANY)
    ints = lambda *s: pltpu.SMEM(s, jnp.int32)
    dma = lambda *s: pltpu.SemaphoreType.DMA(s)
    v = lambda dt, *s: pltpu.VMEM(s, dt)
    piece = (2 * chans // near, hh)
    line = (width, chans)
    return pl.pallas_call(
        functools.partial(block_kernel, space, near),
        in_specs=[anyw] * 14,
        out_specs=[anyw] * 5,
        out_shape=[jax.ShapeDtypeStruct(fields.shape, BF16), jax.ShapeDtypeStruct((chans, hid), F32),
                   jax.ShapeDtypeStruct((hid, chans), F32), jax.ShapeDtypeStruct((14, chans), F32),
                   jax.ShapeDtypeStruct((1, hid), F32)],
        scratch_shapes=[
            ints(*nbrs.shape), ints(*turns.shape), ints(*counts.shape), v(F32, 3, 3, chans), v(F32, 1, chans),
            v(F32, 1, chans), v(F32, 1, chans), v(F32, 2, 1, hh), v(F32, 1, chans), v(BF16, chans, hid),
            v(F32, 1, chans), v(BF16, hid, chans),
            v(F32, chans, hid), v(F32, hid, chans), v(F32, 14, chans), v(F32, 1, hid), dma(12), dma(4),
            v(BF16, *fields.shape), v(BF16, *fields.shape), v(F32, slots, (width + 2) * PITCH + 8, chans),
            v(BF16, hid, chans), v(BF16, 2, chans, hh), v(BF16, 2, chans, hh),
            v(F32, main + edge, chans), v(F32, main + edge, chans),
            v(BF16, main + edge, chans), v(BF16, main + edge, chans),
            v(BF16, 2, main + edge, hh), v(BF16, 2, main + edge, hh),
            v(F32, edge, hh), v(F32, edge, hh), v(F32, edge, hh), v(F32, edge, hh),
            v(BF16, edge, hh), v(BF16, edge, hh), v(BF16, edge, hh), v(BF16, edge, hh),
            v(F32, edge, chans), v(F32, edge, chans), v(F32, LAST_ROWS * width, chans), v(F32, LAST_ROWS * width, chans),
            v(F32, width * 16, chans), pltpu.SMEM((space,), jnp.int32),
            v(F32, 2, 2 * chans, hh), v(F32, 13, 8, chans), v(F32, 2, 8, hh), v(BF16, 32, chans),
            v(BF16, 8 * slots, *line), v(BF16, space, *line), v(BF16, space, *line),
            v(BF16, 2, near, *piece), v(BF16, 2, near, *piece), v(BF16, 2, *piece), v(BF16, 2, far, *piece),
            v(BF16, 2, *piece), v(BF16, 2, near, *piece),
            v(BF16, near, 32, chans), v(BF16, 32, chans), v(BF16, far, 32, chans), v(F32, 32, chans),
            dma(2, slots), dma(slots), dma(space), dma(space), dma(2, 2, near), dma(2, 2, far), dma(2, 2, near),
            dma(2, near), dma(2, far)],
        compiler_params=pltpu.CompilerParams(
            vmem_limit_bytes=60 * 2**20, **(dict(collective_id=0, has_side_effects=True) if COMM else {})),
    )(fields, cotan, nbrs, turns, counts, kern, row(dbias), row(gain), row(nbias), bin_.reshape(2, 1, hh), row(scale),
      win, row(bout), wout)


def local(fields, cotangent, neighbours, rotations, tile_counts, depth_kernel, depth_bias, norm_gain, norm_bias,
          weight_in, bias_in, weight_out, bias_out, layer_scale, shape):
    result, grad_win, grad_wout, channel, bias = publish(*block(
        shape["space"], 2 * shape["dp"], neighbours.T, rotations.T, tile_counts, fields[0], cotangent[0], depth_kernel,
        depth_bias, norm_gain, norm_bias, weight_in, bias_in, weight_out, bias_out, layer_scale))
    return result[None], grad_win, grad_wout, bias.reshape(-1), channel


def solution(mesh):
    placed = P("dp", "space", None, None, None)
    return jax.shard_map(
        functools.partial(local, shape=dict(mesh.shape)),
        mesh=mesh,
        in_specs=(placed, placed) + (P(),) * 12,
        out_specs=(placed, P(), P(), P(), P()),
        check_vma=False,
    )
```

```python
import functools
import math

import jax
import jax.numpy as jnp
from jax import lax
from jax.experimental import pallas as pl
from jax.experimental.pallas import tpu as pltpu
from jax.sharding import PartitionSpec as P

F32, BF16 = jnp.float32, jnp.bfloat16
MESH = pl.DeviceIdType.MESH
PITCH = 64
CONV_ROWS = 16
LAST_ROWS = 16
GROUP = 64
UNROLL = 2
COMM = True


def over_rows(a):
    return jnp.sum(a.reshape(-1, 8, a.shape[-1]), axis=0)


def contract_rows(a, b):
    return lax.dot_general(a, b, (((0,), (0,)), ((), ())), preferred_element_type=F32)


def remote(src, dst, send_sem, recv_sem, device):
    return pltpu.make_async_remote_copy(
        src_ref=src, dst_ref=dst, send_sem=send_sem, recv_sem=recv_sem, device_id=device, device_id_type=MESH
    )


def loop(lo, hi, body, unroll=1):
    def step(i, c):
        body(i)
        return c

    lax.fori_loop(lo, hi, step, 0, unroll=unroll)


def block_kernel(space, near, fields, cotangent, *refs):
    slots, width, _, chans = fields.shape
    held, outs, scratch = refs[:12], refs[12:17], refs[17:]
    kept, made, rest = scratch[:12], scratch[12:16], scratch[16:]
    in_sem, out_sem = rest[:2]
    first = [pltpu.make_async_copy(held[n], kept[n], in_sem.at[n]) for n in range(12)]
    for n in (9, 11, 0, 1, 2, 3, 4, 5, 6, 7, 8, 10):
        first[n].start()
    last = [pltpu.make_async_copy(made[n], outs[n + 1], out_sem.at[n]) for n in range(4)]
    body(space, near, fields, cotangent, *kept, outs[0], *made, first, last, *rest[2:])


def body(space, near, fields, cotangent, nbrs, turns, counts, taps_w, dbias, gain, nbias, bin_, scale, win, bout, wout,
         out, grad_win, grad_wout, channel_out, bias_out, first, final_copies,
                 tile, cotan, frame, win_t, half_out, wout_t, win_h, nhat_s, inv_s, normed_s, branch_s, act_all, dpre_all,
                 pre_a, pre_b, dact_a, dact_b, act_a, act_b, dpre_a, dpre_b, proj_b, dnorm_b, rows_a, rows_b,
                 cot_s, codes, grads, sums, bsum, small, cand, outgo, income, halves, got, mid, far_got, spread, whole,
                 small_got, small_mid, small_far, parts,
                 load_sem, out_sem, halo_send, halo_recv, near_sem, far_sem, back_sem, sn_sem, sf_sem):
    slots, width, _, chans = tile.shape
    hid = win.shape[1]
    hh = hid // 2
    area = width * width
    main = slots * area
    m = act_a.shape[0]
    shift = slots.bit_length() - 1
    picks = 4 * slots
    far = space // 2
    if COMM:
        dp, me = lax.axis_index("dp"), lax.axis_index("space")
        core, plane = lax.rem(me, 2), me // 2
        a = dp * 2 + core
    else:
        me = 0
    loads = []
    for t in range(slots):
        loads.append((pltpu.make_async_copy(fields.at[t], tile.at[t], load_sem.at[0, t]),
                      pltpu.make_async_copy(cotangent.at[t], cotan.at[t], load_sem.at[1, t])))
    for t in range(slots):
        loads[t][0].start()
    for t in range(slots):
        loads[t][1].start()

    def near_id(o):
        p = lax.rem(a + o, near)
        return p, (p // 2, plane * 2 + lax.rem(p, 2))

    def far_id(o):
        p = lax.rem(plane + o, far)
        return p, (dp, p * 2 + core)

    if COMM:
        barrier = pltpu.get_barrier_semaphore()
        loop(1, space, lambda o: pl.semaphore_signal(
            barrier, inc=1, device_id=(dp, lax.rem(me + o, space)), device_id_type=MESH))
        loop(1, near, lambda o: pl.semaphore_signal(barrier, inc=1, device_id=near_id(o)[1], device_id_type=MESH))

    for c in first:
        c.wait()
    win_t[...] = win[...].T
    half_out[...] = wout[...] * 0.5
    for h in range(2):
        win_h[h] = win[:, h * hh:(h + 1) * hh]
        wout_t[h] = (wout[h * hh:(h + 1) * hh, :] * 0.5).T
    grads[...] = jnp.zeros_like(grads)
    sums[...] = jnp.zeros_like(sums)
    bsum[...] = jnp.zeros_like(bsum)
    act_b[...] = jnp.zeros_like(act_b)
    dpre_b[...] = jnp.zeros_like(dpre_b)

    def pick_code(k, nbr, turn):
        side = k & 3
        edge = (turn + (side + 2)) & 3
        flip = ((turn + (side & 1)) >> 1) & 1
        return flip * picks + 4 * (nbr & (slots - 1)) + edge

    if COMM:
        def scan(o):
            peer = lax.rem(me + o, space)
            hit = jnp.int32(0)
            for k in range(picks):
                nbr = nbrs[k & 3, peer * slots + (k >> 2)]
                hit = jnp.where((nbr >> shift) == me, k, hit)
            slot = peer * slots + (hit >> 2)
            codes[o] = pick_code(hit, nbrs[hit & 3, slot], turns[hit & 3, slot])

        loop(0, space, scan)

    def clear(t):
        frame[t, 0:PITCH, :] = jnp.zeros((PITCH, chans), F32)
        frame[t, pl.ds((width + 1) * PITCH, PITCH + 8), :] = jnp.zeros((PITCH + 8, chans), F32)

        def side(r):
            frame[t, pl.ds(pl.multiple_of((r + 1) * PITCH, 8), 8), :] = jnp.zeros((8, chans), F32)
            frame[t, pl.ds(pl.multiple_of((r + 1) * PITCH + 8 + width, 8), 8), :] = jnp.zeros((8, chans), F32)
            frame[t, pl.ds(pl.multiple_of((r + 1) * PITCH + 8, 8), width), :] = tile[t, r].astype(F32)

        loop(0, width, side, 4)

    def edge_of(k, q):
        t = k
        if q == 0:
            return frame[t, pl.ds(PITCH + 8, width), :]
        if q == 1:
            return frame[t, pl.ds(PITCH + 7 + width, width, stride=PITCH), :]
        if q == 2:
            return frame[t, pl.ds(width * PITCH + 8, width), :]
        return frame[t, pl.ds(PITCH + 8, width, stride=PITCH), :]

    for t in range(slots):
        loads[t][0].wait()
        clear(t)
    i = lax.broadcasted_iota(jnp.int32, (width, width), 0)
    j = lax.broadcasted_iota(jnp.int32, (width, width), 1)
    mirror = (i + j == width - 1).astype(BF16)

    def candidates(t):
        for q in range(4):
            line = edge_of(t, q).astype(BF16)
            cand[4 * t + q] = line
            cand[picks + 4 * t + q] = jnp.dot(mirror, line, preferred_element_type=F32).astype(BF16)

    loop(0, slots, candidates)

    if COMM:
        def gather(o):
            outgo[o] = cand[codes[o]]

        loop(0, space, gather, 4)
        income[me] = outgo[0]
        pl.semaphore_wait(barrier, space + near - 2)

        loop(1, space, lambda o: remote(
            outgo.at[o], income.at[me], halo_send.at[o], halo_recv.at[me], (dp, lax.rem(me + o, space))).start())

    for t in range(slots):
        loads[t][1].wait()

    count = counts[me]
    px = lax.broadcasted_iota(jnp.int32, (width, chans), 0)
    inner = ((px > 0) & (px < width - 1)).astype(F32)

    def norm_rows(conv, at):
        x = conv - jnp.mean(conv, axis=-1, keepdims=True)
        iv = lax.rsqrt(jnp.mean(x * x, axis=-1, keepdims=True) + 1e-06)
        nhat = x * iv
        sl = pl.ds(pl.multiple_of(at, 16), width)
        inv_s[sl, :] = jnp.broadcast_to(iv, (width, chans))
        nhat_s[sl, :] = nhat
        normed_s[sl, :] = (nhat * gain[...] + nbias[...]).astype(BF16)

    per = width // CONV_ROWS

    def conv_chunk(step):
        t = step // per
        top = (step - t * per) * CONV_ROWS
        live = jnp.where(t < count, 1.0, 0.0)
        kern = [[taps_w[x, y:y + 1, :] for y in range(3)] for x in range(3)]
        bias = dbias[...]
        weigh = scale[...] * inner * live
        s_g = jnp.zeros((8, chans), F32)
        conv = {}
        for fr in range(CONV_ROWS + 2):
            base = (top + fr) * PITCH + 7
            win3 = [frame[t, pl.ds(base + b, width), :] for b in range(3)]
            for x in range(3):
                r = fr - x
                if 0 <= r < CONV_ROWS:
                    acc = conv.get(r, bias)
                    for b in range(3):
                        acc = acc + win3[b] * kern[x][b]
                    conv[r] = acc
            r = fr - 2
            if r >= 0:
                if r in (0, CONV_ROWS - 1):
                    ends = weigh * jnp.where((top + r > 0) & (top + r < width - 1), 1.0, 0.0)
                at = t * area + (top + r) * width
                norm_rows(conv.pop(r), at)
                g = cotan[t, top + r].astype(F32)
                s_g = s_g + over_rows(g)
                branch_s[pl.ds(pl.multiple_of(at, 16), width), :] = (g * (ends if r in (0, CONV_ROWS - 1) else weigh)).astype(BF16)
        sums[12] += s_g * live

    loop(0, slots * per, conv_chunk)

    def border(t):
        live = jnp.where(t < count, 1.0, 0.0)
        kern = [[taps_w[x, y:y + 1, :] for y in range(3)] for x in range(3)]
        for s in range(4):
            if COMM:
                line = income[nbrs[s, me * slots + t] >> shift]
            else:
                line = cand[pick_code(s, nbrs[s, t], turns[s, t])]
            line = line.astype(F32)
            if s == 0:
                frame[t, pl.ds(8, width), :] = line
            elif s == 1:
                frame[t, pl.ds(PITCH + 8 + width, width, stride=PITCH), :] = line
            elif s == 2:
                frame[t, pl.ds((width + 1) * PITCH + 8, width), :] = line
            else:
                frame[t, pl.ds(PITCH + 7, width, stride=PITCH), :] = line

        def cots(r):
            cot_s[pl.ds(pl.multiple_of(r * 16, 8), 8), :] = cotan[t, r, 0:16, :].astype(F32)[0:8]
            cot_s[pl.ds(pl.multiple_of(r * 16 + 8, 8), 8), :] = cotan[t, r, width - 16:width, :].astype(F32)[8:16]

        loop(0, width, cots, 4)
        for s in range(4):
            acc = dbias[...]
            for x in range(3):
                for b in range(3):
                    if s == 0:
                        w = frame[t, pl.ds(x * PITCH + 7 + b, width), :]
                    elif s == 1:
                        w = frame[t, pl.ds(x * PITCH + 6 + width + b, width, stride=PITCH), :]
                    elif s == 2:
                        w = frame[t, pl.ds((width - 1 + x) * PITCH + 7 + b, width), :]
                    else:
                        w = frame[t, pl.ds(x * PITCH + 7 + b, width, stride=PITCH), :]
                    acc = acc + w * taps_w[x, b:b + 1, :]
            at = main + (t * 4 + s) * width
            norm_rows(acc, at)
            if s == 0:
                g = cotan[t, 0].astype(F32)
            elif s == 1:
                g = cot_s[pl.ds(15, width, stride=16), :] * inner
            elif s == 2:
                g = cotan[t, width - 1].astype(F32)
            else:
                g = cot_s[pl.ds(0, width, stride=16), :] * inner
            branch_s[pl.ds(pl.multiple_of(at, 16), width), :] = (g * live * scale[...]).astype(BF16)

    steps = (main + slots * 4 * width) // m
    total = 2 * steps

    def place(k):
        h = k // steps
        return h, pl.ds(pl.multiple_of((k - h * steps) * m, 16), m)

    def ahead(k, pre_s, dact_s):
        h, rows = place(k)
        pre_s[...] = jnp.dot(normed_s[rows, :], win_h[h], preferred_element_type=F32)
        dact_s[...] = jnp.dot(branch_s[rows, :], wout_t[h], preferred_element_type=F32)

    def behind(k, act_s, dpre_s):
        h, rows = place(k)
        act = act_s[...]
        dpre = dpre_s[...]
        act_all[h, rows, :] = act
        dpre_all[h, rows, :] = dpre
        grads[h, 0:chans, :] += contract_rows(normed_s[rows, :], dpre)
        grads[h, chans:2 * chans, :] += contract_rows(branch_s[rows, :], act)

    def hidden(k, pre_s, dact_s, act_s, dpre_s):
        h, _ = place(k)
        bias = bin_[h]
        bs = jnp.zeros((8, hh), F32)
        for q in range(0, m, GROUP):
            sl = pl.ds(q, GROUP)
            pre = pre_s[sl, :] + bias
            twice = lax.erf(pre * (1.0 / math.sqrt(2.0))) + 1.0
            act_s[sl, :] = (pre * twice).astype(BF16)
            bell = jnp.exp2((pre * (-0.5 * math.log2(math.e))) * pre + math.log2(2.0 / math.sqrt(2.0 * math.pi)))
            dpre = dact_s[sl, :] * (twice + pre * bell)
            bs = bs + over_rows(dpre)
            dpre_s[sl, :] = dpre.astype(BF16)
        bsum[h] += bs

    def send_near(h):
        prows = 2 * chans // near
        for p in range(near):
            part = grads[h, p * prows:(p + 1) * prows, :]
            halves[h, p] = (part if p < near // 2 else 0.5 * part).astype(BF16)
        got[h, a] = halves[h, a]

        def go(o):
            p, device = near_id(o)
            remote(halves.at[h, p], got.at[h, a], near_sem.at[h, 0, o], near_sem.at[h, 1, a], device).start()

        loop(1, near, go)

    def pass_far(h):
        def wait(o):
            p, device = near_id(near - o)
            remote(halves.at[h, p], got.at[h, p], near_sem.at[h, 0, o], near_sem.at[h, 1, p], device).wait()

        loop(1, near, wait)
        tot = got[h, 0].astype(F32)
        for p in range(1, near):
            tot = tot + got[h, p].astype(F32)
        mid[h] = tot.astype(BF16)
        far_got[h, plane] = mid[h]

        def go(o):
            p, device = far_id(o)
            remote(mid.at[h], far_got.at[h, plane], far_sem.at[h, 0, o], far_sem.at[h, 1, plane], device).start()

        loop(1, far, go)

    def pass_back(h):
        def wait(o):
            p, device = far_id(far - o)
            remote(mid.at[h], far_got.at[h, p], far_sem.at[h, 0, o], far_sem.at[h, 1, p], device).wait()

        loop(1, far, wait)
        tot = far_got[h, 0].astype(F32)
        for p in range(1, far):
            tot = tot + far_got[h, p].astype(F32)
        spread[h] = tot.astype(BF16)
        whole[h, a] = spread[h]

        def go(o):
            p, device = near_id(o)
            remote(spread.at[h], whole.at[h, a], back_sem.at[h, 0, o], back_sem.at[h, 1, a], device).start()

        loop(1, near, go)

    def finish(h):
        def wait(o):
            p, device = near_id(near - o)
            remote(spread.at[h], whole.at[h, p], back_sem.at[h, 0, o], back_sem.at[h, 1, p], device).wait()

        loop(1, near, wait)
        prows = 2 * chans // near
        hs = slice(h * hh, (h + 1) * hh)
        full = whole[h].reshape(2 * chans, hh).astype(F32)
        grad_win[:, hs] = full[:chans]
        grad_wout[hs, :] = full[chans:].T

    def halo_wait(o):
        src = lax.rem(me + space - o, space)
        remote(outgo.at[o], income.at[src], halo_send.at[o], halo_recv.at[src], (dp, src)).wait()

    def pair(k):
        behind(jnp.maximum(k - 1, 0), act_b, dpre_b)
        ahead(k + 1, pre_b, dact_b)
        hidden(k, pre_a, dact_a, act_a, dpre_a)
        behind(k, act_a, dpre_a)
        ahead(jnp.minimum(k + 2, total - 1), pre_a, dact_a)
        hidden(k + 1, pre_b, dact_b, act_b, dpre_b)

    def stage(i):
        @pl.when(i == (steps - 3) // (2 * UNROLL))
        def _():
            if COMM:
                loop(1, space, halo_wait)
            loop(0, slots, border)

        if COMM:
            @pl.when(i == (steps - 3) // (2 * UNROLL) + 1)
            def _():
                send_near(0)

            @pl.when(i == (steps - 1) // UNROLL - 1)
            def _():
                pass_far(0)

        for n in range(UNROLL):
            pair(2 + 2 * UNROLL * i + 2 * n)

    ahead(0, pre_a, dact_a)
    pair(0)
    loop(0, (steps - 1) // UNROLL, stage)
    behind(total - 1, act_b, dpre_b)
    if COMM:
        send_near(1)
    edge_rows = pl.ds(main, m)
    g_proj = jnp.zeros((8, chans), F32)
    for h in range(2):
        g_proj = g_proj + over_rows(grads[h, chans:2 * chans, :].T * half_out[h * hh:(h + 1) * hh, :].astype(F32))
    parts[...] = jnp.zeros_like(parts)
    parts[13:14, :] = jnp.sum(g_proj, axis=0, keepdims=True) / scale[...]
    b = jnp.sum(bsum[...], axis=1)
    per_h = hh // chans
    for h in range(2):
        for n in range(per_h):
            k = 14 + h * per_h + n
            parts[k:k + 1, :] = b[h:h + 1, n * chans:(n + 1) * chans]
    dnorm_b[...] = jnp.dot(jnp.concatenate([dpre_all[0, edge_rows, :], dpre_all[1, edge_rows, :]], axis=1), win_t[...],
                           preferred_element_type=F32)

    def merge(t):
        for ref in (nhat_s, inv_s):
            for s in (1, 3, 0, 2):
                v = ref[pl.ds(pl.multiple_of(main + (t * 4 + s) * width, 8), width), :]
                if s == 1:
                    ref[pl.ds(t * area + width - 1, width, stride=width), :] = v
                elif s == 3:
                    ref[pl.ds(t * area, width, stride=width), :] = v
                elif s == 0:
                    ref[pl.ds(pl.multiple_of(t * area, 8), width), :] = v
                else:
                    ref[pl.ds(pl.multiple_of(t * area + area - width, 8), width), :] = v

    loop(0, slots, merge)

    lper = width // LAST_ROWS
    lrows = LAST_ROWS * width

    def product(step, both, weight, rows_s):
        rows = pl.ds(pl.multiple_of(step * lrows, 16), lrows)
        rows_s[...] = jnp.dot(jnp.concatenate([both[0, rows, :], both[1, rows, :]], axis=1), weight[...],
                              preferred_element_type=F32)

    def piped(lo, hi, both, weight, use, hook=None):
        product(lo, both, weight, rows_a)

        def pair(j):
            k = lo + 2 * j
            if hook is not None:
                hook(j)
            product(k + 1, both, weight, rows_b)
            use(k, rows_a)
            product(jnp.minimum(k + 2, hi - 1), both, weight, rows_a)
            use(k + 1, rows_b)

        loop(0, (hi - lo) // 2, pair)

    def with_border(t, top, rows_s, edges):
        at = t * 4 * width
        rows_s[pl.ds(width - 1, LAST_ROWS, stride=width), :] = edges[pl.ds(pl.multiple_of(at + width + top, 8), LAST_ROWS), :]
        rows_s[pl.ds(0, LAST_ROWS, stride=width), :] = edges[pl.ds(pl.multiple_of(at + 3 * width + top, 8), LAST_ROWS), :]
        out = []
        for r in range(LAST_ROWS):
            v = rows_s[pl.ds(r * width, width), :]
            if r == 0:
                v = jnp.where(top == 0, edges[pl.ds(pl.multiple_of(at, 8), width), :], v)
            if r == LAST_ROWS - 1:
                v = jnp.where(top == width - LAST_ROWS, edges[pl.ds(pl.multiple_of(at + 2 * width, 8), width), :], v)
            out.append(v)
        return out

    def last(step, rows_s):
        t = step // lper
        top = pl.multiple_of((step - t * lper) * LAST_ROWS, 8)
        start = pl.multiple_of(t * area + top * width, 16)
        dn = with_border(t, top, rows_s, dnorm_b)
        taps = [[jnp.zeros((8, chans), F32)] * 3 for _ in range(3)]
        s_dn = s_dnh = s_dc = jnp.zeros((8, chans), F32)
        dconv = {}
        for fr in range(LAST_ROWS + 2):
            r = fr
            if r < LAST_ROWS:
                sl = pl.ds(pl.multiple_of(start + r * width, 16), width)
                dnorm = dn[r] * gain[...]
                nhat = nhat_s[sl, :]
                dnh = dnorm * nhat
                s_dn = s_dn + over_rows(dnorm)
                s_dnh = s_dnh + over_rows(dnh)
                m1 = jnp.mean(dnorm, axis=-1, keepdims=True)
                m2 = jnp.mean(dnh, axis=-1, keepdims=True)
                dc = inv_s[sl, :] * (dnorm - m1 - nhat * m2)
                s_dc = s_dc + over_rows(dc)
                dconv[r] = dc
            base = (top + fr) * PITCH + 7
            win3 = [frame[t, pl.ds(base + b, width), :] for b in range(3)]
            for x in range(3):
                r = fr - x
                if 0 <= r < LAST_ROWS:
                    for b in range(3):
                        taps[x][b] = taps[x][b] + over_rows(dconv[r] * win3[b])
            dconv.pop(fr - 2, None)
        for n, s in enumerate([taps[x][b] for x in range(3) for b in range(3)] + [s_dc, s_dnh, s_dn]):
            sums[n] += s
    def finalize(step, rows_s):
        t = step // lper
        top = pl.multiple_of((step - t * lper) * LAST_ROWS, 8)
        live = jnp.where(t < count, 1.0, 0.0)
        start = pl.multiple_of(t * area + top * width, 16)
        proj = with_border(t, top, rows_s, proj_b)
        for r in range(LAST_ROWS):
            x = tile[t, top + r].astype(F32)
            tile[t, top + r] = ((x + scale[...] * (proj[r] + bout[...])) * live).astype(BF16)

        @pl.when(top == width - LAST_ROWS)
        def _():
            pltpu.make_async_copy(tile.at[t], out.at[t], out_sem.at[t]).start()

    def small_near(o):
        p, device = near_id(o)
        remote(small, small_got.at[a], sn_sem.at[0, o], sn_sem.at[1, a], device).start()

    def finalize_all(lo, hi):
        piped(lo, hi, act_all, half_out, finalize)

    def between(j):
        if COMM:
            @pl.when(j == slots * lper // 2 * 2 // 3)
            def _():
                pass_far(1)
                pass_back(0)

    piped(0, slots * lper, dpre_all, win_t, last, between)

    tot = jnp.sum(sums[...], axis=1)
    parts[0:10, :] = tot[0:10]
    parts[10:12, :] = tot[10:12] / gain[...]
    parts[12:13, :] = tot[12:13] * scale[...]
    parts[13:14, :] += tot[12:13] * bout[...]
    small[...] = parts[...].astype(BF16)
    if COMM:
        small_got[a] = small[...]
        loop(1, near, small_near)

    def write_small(v):
        channel_out[...] = v[0:14]
        for n in range(hid // chans):
            bias_out[:, n * chans:(n + 1) * chans] = v[14 + n:15 + n]

    proj_b[...] = jnp.dot(jnp.concatenate([act_all[0, edge_rows, :], act_all[1, edge_rows, :]], axis=1), half_out[...],
                          preferred_element_type=F32)
    if not COMM:
        write_small(parts[...])
        for h in range(2):
            grad_win[:, h * hh:(h + 1) * hh] = grads[h, 0:chans, :]
            grad_wout[h * hh:(h + 1) * hh, :] = 0.5 * grads[h, chans:2 * chans, :].T
        finalize_all(0, slots * lper)
        for c in final_copies:
            c.start()
        for t in range(slots):
            pltpu.make_async_copy(tile.at[t], out.at[t], out_sem.at[t]).wait()
        for c in final_copies:
            c.wait()
        return

    def small_near_wait(o):
        p, device = near_id(near - o)
        remote(small, small_got.at[p], sn_sem.at[0, o], sn_sem.at[1, p], device).wait()

    def small_far_go(o):
        p, device = far_id(o)
        remote(small_mid, small_far.at[plane], sf_sem.at[0, o], sf_sem.at[1, plane], device).start()

    def small_far_wait(o):
        p, device = far_id(far - o)
        remote(small_mid, small_far.at[p], sf_sem.at[0, o], sf_sem.at[1, p], device).wait()

    finalize_all(0, slots * lper // 2)
    loop(1, near, small_near_wait)
    s = small_got[0].astype(F32)
    for p in range(1, near):
        s = s + small_got[p].astype(F32)
    small_mid[...] = s.astype(BF16)
    small_far[plane] = small_mid[...]
    loop(1, far, small_far_go)
    pass_back(1)
    finalize_all(slots * lper // 2, slots * lper)
    finish(0)
    for t in range(slots):
        pltpu.make_async_copy(tile.at[t], out.at[t], out_sem.at[t]).wait()
    finish(1)
    for c in final_copies[:2]:
        c.start()
    loop(1, far, small_far_wait)
    s = small_far[0].astype(F32)
    for p in range(1, far):
        s = s + small_far[p].astype(F32)
    write_small(s)
    for c in final_copies[2:]:
        c.start()
    for c in final_copies:
        c.wait()


def publish_kernel(*refs):
    n = (len(refs) - 1) // 3
    srcs, dsts, held, sems = refs[:n], refs[n:2 * n], refs[2 * n:3 * n], refs[3 * n]
    parts = [(srcs[0].at[t], held[0].at[t], dsts[0].at[t]) for t in range(srcs[0].shape[0])]
    parts += list(zip(srcs[1:], held[1:], dsts[1:]))
    ins = [pltpu.make_async_copy(src, mid, sems.at[0, i]) for i, (src, mid, _) in enumerate(parts)]
    outs = [pltpu.make_async_copy(mid, dst, sems.at[1, i]) for i, (_, mid, dst) in enumerate(parts)]
    for c in ins:
        c.start()
    for c, d in zip(ins, outs):
        c.wait()
        d.start()
    for d in outs:
        d.wait()


def publish(*arrays):
    anyw = pl.BlockSpec(memory_space=pl.ANY)
    return pl.pallas_call(
        publish_kernel,
        in_specs=[anyw] * len(arrays),
        out_specs=[anyw] * len(arrays),
        out_shape=[jax.ShapeDtypeStruct(v.shape, v.dtype) for v in arrays],
        scratch_shapes=[pltpu.VMEM(v.shape, v.dtype) for v in arrays]
        + [pltpu.SemaphoreType.DMA((2, arrays[0].shape[0] + len(arrays) - 1))],
        compiler_params=pltpu.CompilerParams(vmem_limit_bytes=60 * 2**20),
    )(*arrays)


def block(space, near, nbrs, turns, counts, fields, cotan, kern, dbias, gain, nbias, win, bin_, wout, bout, scale):
    slots, width, _, chans = fields.shape
    hid = win.shape[1]
    hh = hid // 2
    far = space // 2
    main, edge = slots * width * width, slots * 4 * width
    row = lambda v: v.reshape(1, -1)
    anyw = pl.BlockSpec(memory_space=pl.ANY)
    ints = lambda *s: pltpu.SMEM(s, jnp.int32)
    dma = lambda *s: pltpu.SemaphoreType.DMA(s)
    v = lambda dt, *s: pltpu.VMEM(s, dt)
    piece = (2 * chans // near, hh)
    line = (width, chans)
    return pl.pallas_call(
        functools.partial(block_kernel, space, near),
        in_specs=[anyw] * 14,
        out_specs=[anyw] * 5,
        out_shape=[jax.ShapeDtypeStruct(fields.shape, BF16), jax.ShapeDtypeStruct((chans, hid), F32),
                   jax.ShapeDtypeStruct((hid, chans), F32), jax.ShapeDtypeStruct((14, chans), F32),
                   jax.ShapeDtypeStruct((1, hid), F32)],
        scratch_shapes=[
            ints(*nbrs.shape), ints(*turns.shape), ints(*counts.shape), v(F32, 3, 3, chans), v(F32, 1, chans),
            v(F32, 1, chans), v(F32, 1, chans), v(F32, 2, 1, hh), v(F32, 1, chans), v(BF16, chans, hid),
            v(F32, 1, chans), v(BF16, hid, chans),
            v(F32, chans, hid), v(F32, hid, chans), v(F32, 14, chans), v(F32, 1, hid), dma(12), dma(4),
            v(BF16, *fields.shape), v(BF16, *fields.shape), v(F32, slots, (width + 2) * PITCH + 8, chans),
            v(BF16, hid, chans), v(BF16, hid, chans), v(BF16, 2, chans, hh), v(BF16, 2, chans, hh),
            v(F32, main + edge, chans), v(F32, main + edge, chans),
            v(BF16, main + edge, chans), v(BF16, main + edge, chans),
            v(BF16, 2, main + edge, hh), v(BF16, 2, main + edge, hh),
            v(F32, edge, hh), v(F32, edge, hh), v(F32, edge, hh), v(F32, edge, hh),
            v(BF16, edge, hh), v(BF16, edge, hh), v(BF16, edge, hh), v(BF16, edge, hh),
            v(F32, edge, chans), v(F32, edge, chans), v(F32, LAST_ROWS * width, chans), v(F32, LAST_ROWS * width, chans),
            v(F32, width * 16, chans), pltpu.SMEM((space,), jnp.int32),
            v(F32, 2, 2 * chans, hh), v(F32, 13, 8, chans), v(F32, 2, 8, hh), v(BF16, 32, chans),
            v(BF16, 8 * slots, *line), v(BF16, space, *line), v(BF16, space, *line),
            v(BF16, 2, near, *piece), v(BF16, 2, near, *piece), v(BF16, 2, *piece), v(BF16, 2, far, *piece),
            v(BF16, 2, *piece), v(BF16, 2, near, *piece),
            v(BF16, near, 32, chans), v(BF16, 32, chans), v(BF16, far, 32, chans), v(F32, 32, chans),
            dma(2, slots), dma(slots), dma(space), dma(space), dma(2, 2, near), dma(2, 2, far), dma(2, 2, near),
            dma(2, near), dma(2, far)],
        compiler_params=pltpu.CompilerParams(
            vmem_limit_bytes=60 * 2**20, **(dict(collective_id=0, has_side_effects=True) if COMM else {})),
    )(fields, cotan, nbrs, turns, counts, kern, row(dbias), row(gain), row(nbias), bin_.reshape(2, 1, hh), row(scale),
      win, row(bout), wout)


def local(fields, cotangent, neighbours, rotations, tile_counts, depth_kernel, depth_bias, norm_gain, norm_bias,
          weight_in, bias_in, weight_out, bias_out, layer_scale, shape):
    result, grad_win, grad_wout, channel, bias = publish(*block(
        shape["space"], 2 * shape["dp"], neighbours.T, rotations.T, tile_counts, fields[0], cotangent[0], depth_kernel,
        depth_bias, norm_gain, norm_bias, weight_in, bias_in, weight_out, bias_out, layer_scale))
    return result[None], grad_win, grad_wout, bias.reshape(-1), channel


def solution(mesh):
    placed = P("dp", "space", None, None, None)
    return jax.shard_map(
        functools.partial(local, shape=dict(mesh.shape)),
        mesh=mesh,
        in_specs=(placed, placed) + (P(),) * 12,
        out_specs=(placed, P(), P(), P(), P()),
        check_vma=False,
    )
```

```python
import functools
import math

import jax
import jax.numpy as jnp
from jax import lax
from jax.experimental import pallas as pl
from jax.experimental.pallas import tpu as pltpu
from jax.sharding import PartitionSpec as P

F32, BF16 = jnp.float32, jnp.bfloat16
MESH = pl.DeviceIdType.MESH
PITCH = 64
CONV_ROWS = 16
LAST_ROWS = 16
GROUP = 64
UNROLL = 2
COMM = True


def settle(pieces, sems, device):
    copy = remote(pieces, pieces, sems.at[0], sems.at[1], device)
    copy.wait_send()
    copy.wait_recv()


def over_rows(a):
    return jnp.sum(a.reshape(-1, 8, a.shape[-1]), axis=0)


def contract_rows(a, b):
    return lax.dot_general(a, b, (((0,), (0,)), ((), ())), preferred_element_type=F32)


def remote(src, dst, send_sem, recv_sem, device):
    return pltpu.make_async_remote_copy(
        src_ref=src, dst_ref=dst, send_sem=send_sem, recv_sem=recv_sem, device_id=device, device_id_type=MESH
    )


def loop(lo, hi, body, unroll=1):
    def step(i, c):
        body(i)
        return c

    lax.fori_loop(lo, hi, step, 0, unroll=unroll)


def block_kernel(space, near, fields, cotangent, *refs):
    slots, width, _, chans = fields.shape
    held, outs, scratch = refs[:12], refs[12:17], refs[17:]
    kept, made, rest = scratch[:12], scratch[12:16], scratch[16:]
    in_sem, out_sem = rest[:2]
    first = [pltpu.make_async_copy(held[n], kept[n], in_sem.at[n]) for n in range(12)]
    for n in (9, 11, 0, 1, 2, 3, 4, 5, 6, 7, 8, 10):
        first[n].start()
    last = [pltpu.make_async_copy(made[n], outs[n + 1], out_sem.at[n]) for n in range(4)]
    body(space, near, fields, cotangent, *kept, outs[0], *made, first, last, *rest[2:])


def body(space, near, fields, cotangent, nbrs, turns, counts, taps_w, dbias, gain, nbias, bin_, scale, win, bout, wout,
         out, grad_win, grad_wout, channel_out, bias_out, first, final_copies,
                 tile, cotan, frame, win_t, half_out, wout_t, win_h, nhat_s, inv_s, normed_s, branch_s, act_all, dpre_all,
                 pre_a, pre_b, dact_a, dact_b, act_a, act_b, dpre_a, dpre_b, proj_b, dnorm_b, rows_a, rows_b,
                 cot_s, codes, grads, sums, bsum, small, cand, outgo, income, halves, got, mid, far_got, spread, whole,
                 small_got, small_mid, small_far, parts,
                 load_sem, out_sem, halo_sem, near_sem, far_sem, back_sem, sn_sem, sf_sem):
    slots, width, _, chans = tile.shape
    hid = win.shape[1]
    hh = hid // 2
    area = width * width
    main = slots * area
    m = act_a.shape[0]
    shift = slots.bit_length() - 1
    picks = 4 * slots
    far = space // 2
    if COMM:
        dp, me = lax.axis_index("dp"), lax.axis_index("space")
        core, plane = lax.rem(me, 2), me // 2
        a = dp * 2 + core
    else:
        me = 0
    loads = []
    for t in range(slots):
        loads.append((pltpu.make_async_copy(fields.at[t], tile.at[t], load_sem.at[0, t]),
                      pltpu.make_async_copy(cotangent.at[t], cotan.at[t], load_sem.at[1, t])))
    for t in range(slots):
        loads[t][0].start()
    for t in range(slots):
        loads[t][1].start()

    def near_id(o):
        p = lax.rem(a + o, near)
        return p, (p // 2, plane * 2 + lax.rem(p, 2))

    def far_id(o):
        p = lax.rem(plane + o, far)
        return p, (dp, p * 2 + core)

    if COMM:
        barrier = pltpu.get_barrier_semaphore()
        loop(1, space, lambda o: pl.semaphore_signal(
            barrier, inc=1, device_id=(dp, lax.rem(me + o, space)), device_id_type=MESH))
        loop(1, near, lambda o: pl.semaphore_signal(barrier, inc=1, device_id=near_id(o)[1], device_id_type=MESH))

    for c in first:
        c.wait()
    win_t[...] = win[...].T
    half_out[...] = wout[...] * 0.5
    for h in range(2):
        win_h[h] = win[:, h * hh:(h + 1) * hh]
        wout_t[h] = (wout[h * hh:(h + 1) * hh, :] * 0.5).T
    grads[...] = jnp.zeros_like(grads)
    sums[...] = jnp.zeros_like(sums)
    bsum[...] = jnp.zeros_like(bsum)
    act_b[...] = jnp.zeros_like(act_b)
    dpre_b[...] = jnp.zeros_like(dpre_b)

    def pick_code(k, nbr, turn):
        side = k & 3
        edge = (turn + (side + 2)) & 3
        flip = ((turn + (side & 1)) >> 1) & 1
        return flip * picks + 4 * (nbr & (slots - 1)) + edge

    def scan(o):
        peer = lax.rem(me + o, space)
        hit = jnp.int32(0)
        for k in range(picks):
            nbr = nbrs[k & 3, peer * slots + (k >> 2)]
            hit = jnp.where((nbr >> shift) == me, k, hit)
        slot = peer * slots + (hit >> 2)
        codes[o] = pick_code(hit, nbrs[hit & 3, slot], turns[hit & 3, slot])

    def clear(t):
        frame[t, 0:PITCH, :] = jnp.zeros((PITCH, chans), F32)
        frame[t, pl.ds((width + 1) * PITCH, PITCH + 8), :] = jnp.zeros((PITCH + 8, chans), F32)

        def side(r):
            frame[t, pl.ds(pl.multiple_of((r + 1) * PITCH, 8), 8), :] = jnp.zeros((8, chans), F32)
            frame[t, pl.ds(pl.multiple_of((r + 1) * PITCH + 8 + width, 8), 8), :] = jnp.zeros((8, chans), F32)
            frame[t, pl.ds(pl.multiple_of((r + 1) * PITCH + 8, 8), width), :] = tile[t, r].astype(F32)

        each = space // slots

        def fill(n):
            if COMM:
                scan(t * each + n)
            for r in range(width // each):
                side(n * (width // each) + r)

        loop(0, each, fill)

    def edge_of(k, q):
        t = k
        if q == 0:
            return frame[t, pl.ds(PITCH + 8, width), :]
        if q == 1:
            return frame[t, pl.ds(PITCH + 7 + width, width, stride=PITCH), :]
        if q == 2:
            return frame[t, pl.ds(width * PITCH + 8, width), :]
        return frame[t, pl.ds(PITCH + 8, width, stride=PITCH), :]

    for t in range(slots):
        loads[t][0].wait()
        clear(t)
    i = lax.broadcasted_iota(jnp.int32, (width, width), 0)
    j = lax.broadcasted_iota(jnp.int32, (width, width), 1)
    mirror = (i + j == width - 1).astype(BF16)

    def candidates(t):
        for q in range(4):
            line = edge_of(t, q).astype(BF16)
            cand[4 * t + q] = line
            cand[picks + 4 * t + q] = jnp.dot(mirror, line, preferred_element_type=F32).astype(BF16)

    loop(0, slots, candidates)

    if COMM:
        def gather(o):
            outgo[o] = cand[codes[o]]

        loop(0, space, gather, 4)
        income[me] = outgo[0]
        pl.semaphore_wait(barrier, space + near - 2)

        loop(1, space, lambda o: remote(
            outgo.at[o], income.at[me], halo_sem.at[0], halo_sem.at[1], (dp, lax.rem(me + o, space))).start())

    for t in range(slots):
        loads[t][1].wait()

    count = counts[me]
    px = lax.broadcasted_iota(jnp.int32, (width, chans), 0)
    inner = ((px > 0) & (px < width - 1)).astype(F32)

    def norm_rows(conv, at):
        x = conv - jnp.mean(conv, axis=-1, keepdims=True)
        iv = lax.rsqrt(jnp.mean(x * x, axis=-1, keepdims=True) + 1e-06)
        nhat = x * iv
        sl = pl.ds(pl.multiple_of(at, 16), width)
        inv_s[sl, :] = jnp.broadcast_to(iv, (width, chans))
        nhat_s[sl, :] = nhat
        normed_s[sl, :] = (nhat * gain[...] + nbias[...]).astype(BF16)

    per = width // CONV_ROWS

    def conv_chunk(step):
        t = step // per
        top = (step - t * per) * CONV_ROWS
        live = jnp.where(t < count, 1.0, 0.0)
        kern = [[taps_w[x, y:y + 1, :] for y in range(3)] for x in range(3)]
        bias = dbias[...]
        weigh = scale[...] * inner * live
        s_g = jnp.zeros((8, chans), F32)
        conv = {}
        for fr in range(CONV_ROWS + 2):
            base = (top + fr) * PITCH + 7
            win3 = [frame[t, pl.ds(base + b, width), :] for b in range(3)]
            for x in range(3):
                r = fr - x
                if 0 <= r < CONV_ROWS:
                    acc = conv.get(r, bias)
                    for b in range(3):
                        acc = acc + win3[b] * kern[x][b]
                    conv[r] = acc
            r = fr - 2
            if r >= 0:
                if r in (0, CONV_ROWS - 1):
                    ends = weigh * jnp.where((top + r > 0) & (top + r < width - 1), 1.0, 0.0)
                at = t * area + (top + r) * width
                norm_rows(conv.pop(r), at)
                g = cotan[t, top + r].astype(F32)
                s_g = s_g + over_rows(g)
                sides = (t * width + top + r) * 8
                cot_s[pl.ds(pl.multiple_of(sides, 8), 8), :] = jnp.where(px[0:8] == 0, g[0:8], g[width - 8:width])
                branch_s[pl.ds(pl.multiple_of(at, 16), width), :] = (g * (ends if r in (0, CONV_ROWS - 1) else weigh)).astype(BF16)
        sums[12] += s_g * live

    loop(0, slots * per, conv_chunk)

    def border(t):
        live = jnp.where(t < count, 1.0, 0.0)
        kern = [[taps_w[x, y:y + 1, :] for y in range(3)] for x in range(3)]
        for s in range(4):
            if COMM:
                line = income[nbrs[s, me * slots + t] >> shift]
            else:
                line = cand[pick_code(s, nbrs[s, t], turns[s, t])]
            line = line.astype(F32)
            if s == 0:
                frame[t, pl.ds(8, width), :] = line
            elif s == 1:
                frame[t, pl.ds(PITCH + 8 + width, width, stride=PITCH), :] = line
            elif s == 2:
                frame[t, pl.ds((width + 1) * PITCH + 8, width), :] = line
            else:
                frame[t, pl.ds(PITCH + 7, width, stride=PITCH), :] = line

        for s in range(4):
            acc = dbias[...]
            for x in range(3):
                for b in range(3):
                    if s == 0:
                        w = frame[t, pl.ds(x * PITCH + 7 + b, width), :]
                    elif s == 1:
                        w = frame[t, pl.ds(x * PITCH + 6 + width + b, width, stride=PITCH), :]
                    elif s == 2:
                        w = frame[t, pl.ds((width - 1 + x) * PITCH + 7 + b, width), :]
                    else:
                        w = frame[t, pl.ds(x * PITCH + 7 + b, width, stride=PITCH), :]
                    acc = acc + w * taps_w[x, b:b + 1, :]
            at = main + (t * 4 + s) * width
            norm_rows(acc, at)
            if s == 0:
                g = cotan[t, 0].astype(F32)
            elif s == 1:
                g = cot_s[pl.ds(t * width * 8 + 7, width, stride=8), :] * inner
            elif s == 2:
                g = cotan[t, width - 1].astype(F32)
            else:
                g = cot_s[pl.ds(t * width * 8, width, stride=8), :] * inner
            branch_s[pl.ds(pl.multiple_of(at, 16), width), :] = (g * live * scale[...]).astype(BF16)

    steps = (main + slots * 4 * width) // m
    total = 2 * steps

    def place(k):
        h = k // steps
        return h, pl.ds(pl.multiple_of((k - h * steps) * m, 16), m)

    def ahead(k, pre_s, dact_s):
        h, rows = place(k)
        pre_s[...] = jnp.dot(normed_s[rows, :], win_h[h], preferred_element_type=F32)
        dact_s[...] = jnp.dot(branch_s[rows, :], wout_t[h], preferred_element_type=F32)

    def behind(k, act_s, dpre_s):
        h, rows = place(k)
        act = act_s[...]
        dpre = dpre_s[...]
        act_all[h, rows, :] = act
        dpre_all[h, rows, :] = dpre
        grads[h, 0:chans, :] += contract_rows(normed_s[rows, :], dpre)
        grads[h, chans:2 * chans, :] += contract_rows(branch_s[rows, :], act)

    def hidden(k, pre_s, dact_s, act_s, dpre_s):
        h, _ = place(k)
        bias = bin_[h]
        bs = jnp.zeros((8, hh), F32)
        for q in range(0, m, GROUP):
            sl = pl.ds(q, GROUP)
            pre = pre_s[sl, :] + bias
            twice = lax.erf(pre * (1.0 / math.sqrt(2.0))) + 1.0
            act_s[sl, :] = (pre * twice).astype(BF16)
            bell = jnp.exp2((pre * (-0.5 * math.log2(math.e))) * pre + math.log2(2.0 / math.sqrt(2.0 * math.pi)))
            dpre = dact_s[sl, :] * (twice + pre * bell)
            bs = bs + over_rows(dpre)
            dpre_s[sl, :] = dpre.astype(BF16)
        bsum[h] += bs

    def send_near(h):
        prows = 2 * chans // near
        for p in range(near):
            part = grads[h, p * prows:(p + 1) * prows, :]
            halves[h, p] = (part if p < near // 2 else 0.5 * part).astype(BF16)
        got[h, a] = halves[h, a]

        def go(o):
            p, device = near_id(o)
            remote(halves.at[h, p], got.at[h, a], near_sem.at[h, 0], near_sem.at[h, 1], device).start()

        loop(1, near, go)

    def pass_far(h):
        settle(got.at[h, pl.ds(0, near - 1)], near_sem.at[h], near_id(1)[1])
        tot = got[h, 0].astype(F32)
        for p in range(1, near):
            tot = tot + got[h, p].astype(F32)
        mid[h] = tot.astype(BF16)
        far_got[h, plane] = mid[h]

        def go(o):
            p, device = far_id(o)
            remote(mid.at[h], far_got.at[h, plane], far_sem.at[h, 0], far_sem.at[h, 1], device).start()

        loop(1, far, go)

    def pass_back(h):
        settle(far_got.at[h, pl.ds(0, far - 1)], far_sem.at[h], far_id(1)[1])
        tot = far_got[h, 0].astype(F32)
        for p in range(1, far):
            tot = tot + far_got[h, p].astype(F32)
        spread[h] = tot.astype(BF16)
        whole[h, a] = spread[h]

        def go(o):
            p, device = near_id(o)
            remote(spread.at[h], whole.at[h, a], back_sem.at[h, 0], back_sem.at[h, 1], device).start()

        loop(1, near, go)

    def finish(h):
        settle(whole.at[h, pl.ds(0, near - 1)], back_sem.at[h], near_id(1)[1])
        prows = 2 * chans // near
        hs = slice(h * hh, (h + 1) * hh)
        full = whole[h].reshape(2 * chans, hh).astype(F32)
        grad_win[:, hs] = full[:chans]
        grad_wout[hs, :] = full[chans:].T

    def pair(k):
        behind(jnp.maximum(k - 1, 0), act_b, dpre_b)
        ahead(k + 1, pre_b, dact_b)
        hidden(k, pre_a, dact_a, act_a, dpre_a)
        behind(k, act_a, dpre_a)
        ahead(jnp.minimum(k + 2, total - 1), pre_a, dact_a)
        hidden(k + 1, pre_b, dact_b, act_b, dpre_b)

    def stage(i):
        @pl.when(i == (steps - 3) // (2 * UNROLL))
        def _():
            if COMM:
                settle(income.at[pl.ds(0, space - 1)], halo_sem, (dp, lax.rem(me + 1, space)))
            loop(0, slots, border)

        if COMM:
            @pl.when(i == (steps - 3) // (2 * UNROLL) + 1)
            def _():
                send_near(0)

            @pl.when(i == (steps - 1) // UNROLL - 1)
            def _():
                pass_far(0)

        for n in range(UNROLL):
            pair(2 + 2 * UNROLL * i + 2 * n)

    ahead(0, pre_a, dact_a)
    pair(0)
    loop(0, (steps - 1) // UNROLL, stage)
    behind(total - 1, act_b, dpre_b)
    if COMM:
        send_near(1)
    edge_rows = pl.ds(main, m)
    g_proj = jnp.zeros((8, chans), F32)
    for h in range(2):
        g_proj = g_proj + over_rows(grads[h, chans:2 * chans, :].T * half_out[h * hh:(h + 1) * hh, :].astype(F32))
    parts[...] = jnp.zeros_like(parts)
    parts[13:14, :] = jnp.sum(g_proj, axis=0, keepdims=True) / scale[...]
    b = jnp.sum(bsum[...], axis=1)
    per_h = hh // chans
    for h in range(2):
        for n in range(per_h):
            k = 14 + h * per_h + n
            parts[k:k + 1, :] = b[h:h + 1, n * chans:(n + 1) * chans]
    dnorm_b[...] = jnp.dot(jnp.concatenate([dpre_all[0, edge_rows, :], dpre_all[1, edge_rows, :]], axis=1), win_t[...],
                           preferred_element_type=F32)

    def merge(t):
        for ref in (nhat_s, inv_s):
            for s in (1, 3, 0, 2):
                v = ref[pl.ds(pl.multiple_of(main + (t * 4 + s) * width, 8), width), :]
                if s == 1:
                    ref[pl.ds(t * area + width - 1, width, stride=width), :] = v
                elif s == 3:
                    ref[pl.ds(t * area, width, stride=width), :] = v
                elif s == 0:
                    ref[pl.ds(pl.multiple_of(t * area, 8), width), :] = v
                else:
                    ref[pl.ds(pl.multiple_of(t * area + area - width, 8), width), :] = v

    loop(0, slots, merge)

    lper = width // LAST_ROWS
    lrows = LAST_ROWS * width

    def product(step, both, weight, rows_s):
        rows = pl.ds(pl.multiple_of(step * lrows, 16), lrows)
        rows_s[...] = jnp.dot(jnp.concatenate([both[0, rows, :], both[1, rows, :]], axis=1), weight[...],
                              preferred_element_type=F32)

    def piped(lo, hi, both, weight, use, hook=None):
        product(lo, both, weight, rows_a)

        def pair(j):
            k = lo + 2 * j
            if hook is not None:
                hook(j)
            product(k + 1, both, weight, rows_b)
            use(k, rows_a)
            product(jnp.minimum(k + 2, hi - 1), both, weight, rows_a)
            use(k + 1, rows_b)

        loop(0, (hi - lo) // 2, pair)

    def with_border(t, top, rows_s, edges):
        at = t * 4 * width
        rows_s[pl.ds(width - 1, LAST_ROWS, stride=width), :] = edges[pl.ds(pl.multiple_of(at + width + top, 8), LAST_ROWS), :]
        rows_s[pl.ds(0, LAST_ROWS, stride=width), :] = edges[pl.ds(pl.multiple_of(at + 3 * width + top, 8), LAST_ROWS), :]
        out = []
        for r in range(LAST_ROWS):
            v = rows_s[pl.ds(r * width, width), :]
            if r == 0:
                v = jnp.where(top == 0, edges[pl.ds(pl.multiple_of(at, 8), width), :], v)
            if r == LAST_ROWS - 1:
                v = jnp.where(top == width - LAST_ROWS, edges[pl.ds(pl.multiple_of(at + 2 * width, 8), width), :], v)
            out.append(v)
        return out

    def last(step, rows_s):
        t = step // lper
        top = pl.multiple_of((step - t * lper) * LAST_ROWS, 8)
        start = pl.multiple_of(t * area + top * width, 16)
        dn = with_border(t, top, rows_s, dnorm_b)
        taps = [[jnp.zeros((8, chans), F32)] * 3 for _ in range(3)]
        s_dn = s_dnh = s_dc = jnp.zeros((8, chans), F32)
        dconv = {}
        for fr in range(LAST_ROWS + 2):
            r = fr
            if r < LAST_ROWS:
                sl = pl.ds(pl.multiple_of(start + r * width, 16), width)
                dnorm = dn[r] * gain[...]
                nhat = nhat_s[sl, :]
                dnh = dnorm * nhat
                s_dn = s_dn + over_rows(dnorm)
                s_dnh = s_dnh + over_rows(dnh)
                m1 = jnp.mean(dnorm, axis=-1, keepdims=True)
                m2 = jnp.mean(dnh, axis=-1, keepdims=True)
                dc = inv_s[sl, :] * (dnorm - m1 - nhat * m2)
                s_dc = s_dc + over_rows(dc)
                dconv[r] = dc
            base = (top + fr) * PITCH + 7
            win3 = [frame[t, pl.ds(base + b, width), :] for b in range(3)]
            for x in range(3):
                r = fr - x
                if 0 <= r < LAST_ROWS:
                    for b in range(3):
                        taps[x][b] = taps[x][b] + over_rows(dconv[r] * win3[b])
            dconv.pop(fr - 2, None)
        for n, s in enumerate([taps[x][b] for x in range(3) for b in range(3)] + [s_dc, s_dnh, s_dn]):
            sums[n] += s
    def finalize(step, rows_s):
        t = step // lper
        top = pl.multiple_of((step - t * lper) * LAST_ROWS, 8)
        live = jnp.where(t < count, 1.0, 0.0)
        start = pl.multiple_of(t * area + top * width, 16)
        proj = with_border(t, top, rows_s, proj_b)
        for r in range(LAST_ROWS):
            x = tile[t, top + r].astype(F32)
            tile[t, top + r] = ((x + scale[...] * (proj[r] + bout[...])) * live).astype(BF16)

        @pl.when(top == width - LAST_ROWS)
        def _():
            pltpu.make_async_copy(tile.at[t], out.at[t], out_sem.at[t]).start()

    def small_near(o):
        p, device = near_id(o)
        remote(small, small_got.at[a], sn_sem.at[0], sn_sem.at[1], device).start()

    def finalize_all(lo, hi):
        piped(lo, hi, act_all, half_out, finalize)

    def between(j):
        if COMM:
            @pl.when(j == slots * lper // 2 * 2 // 3)
            def _():
                pass_far(1)
                pass_back(0)

    piped(0, slots * lper, dpre_all, win_t, last, between)

    tot = jnp.sum(sums[...], axis=1)
    parts[0:10, :] = tot[0:10]
    parts[10:12, :] = tot[10:12] / gain[...]
    parts[12:13, :] = tot[12:13] * scale[...]
    parts[13:14, :] += tot[12:13] * bout[...]
    small[...] = parts[...].astype(BF16)
    if COMM:
        small_got[a] = small[...]
        loop(1, near, small_near)

    def write_small(v):
        channel_out[...] = v[0:14]
        for n in range(hid // chans):
            bias_out[:, n * chans:(n + 1) * chans] = v[14 + n:15 + n]

    proj_b[...] = jnp.dot(jnp.concatenate([act_all[0, edge_rows, :], act_all[1, edge_rows, :]], axis=1), half_out[...],
                          preferred_element_type=F32)
    if not COMM:
        write_small(parts[...])
        for h in range(2):
            grad_win[:, h * hh:(h + 1) * hh] = grads[h, 0:chans, :]
            grad_wout[h * hh:(h + 1) * hh, :] = 0.5 * grads[h, chans:2 * chans, :].T
        finalize_all(0, slots * lper)
        for c in final_copies:
            c.start()
        for t in range(slots):
            pltpu.make_async_copy(tile.at[t], out.at[t], out_sem.at[t]).wait()
        for c in final_copies:
            c.wait()
        return

    def small_far_go(o):
        p, device = far_id(o)
        remote(small_mid, small_far.at[plane], sf_sem.at[0], sf_sem.at[1], device).start()

    finalize_all(0, slots * lper // 2)
    settle(small_got.at[pl.ds(0, near - 1)], sn_sem, near_id(1)[1])
    s = small_got[0].astype(F32)
    for p in range(1, near):
        s = s + small_got[p].astype(F32)
    small_mid[...] = s.astype(BF16)
    small_far[plane] = small_mid[...]
    loop(1, far, small_far_go)
    pass_back(1)
    finalize_all(slots * lper // 2, slots * lper)
    finish(0)
    for t in range(slots):
        pltpu.make_async_copy(tile.at[t], out.at[t], out_sem.at[t]).wait()
    finish(1)
    for c in final_copies[:2]:
        c.start()
    settle(small_far.at[pl.ds(0, far - 1)], sf_sem, far_id(1)[1])
    s = small_far[0].astype(F32)
    for p in range(1, far):
        s = s + small_far[p].astype(F32)
    write_small(s)
    for c in final_copies[2:]:
        c.start()
    for c in final_copies:
        c.wait()


def publish_kernel(*refs):
    n = (len(refs) - 1) // 3
    srcs, dsts, held, sems = refs[:n], refs[n:2 * n], refs[2 * n:3 * n], refs[3 * n]
    parts = [(srcs[0].at[t], held[0].at[t], dsts[0].at[t]) for t in range(srcs[0].shape[0])]
    parts += list(zip(srcs[1:], held[1:], dsts[1:]))
    ins = [pltpu.make_async_copy(src, mid, sems.at[0, i]) for i, (src, mid, _) in enumerate(parts)]
    outs = [pltpu.make_async_copy(mid, dst, sems.at[1, i]) for i, (_, mid, dst) in enumerate(parts)]
    for c in ins:
        c.start()
    for c, d in zip(ins, outs):
        c.wait()
        d.start()
    for d in outs:
        d.wait()


def publish(*arrays):
    anyw = pl.BlockSpec(memory_space=pl.ANY)
    return pl.pallas_call(
        publish_kernel,
        in_specs=[anyw] * len(arrays),
        out_specs=[anyw] * len(arrays),
        out_shape=[jax.ShapeDtypeStruct(v.shape, v.dtype) for v in arrays],
        scratch_shapes=[pltpu.VMEM(v.shape, v.dtype) for v in arrays]
        + [pltpu.SemaphoreType.DMA((2, arrays[0].shape[0] + len(arrays) - 1))],
        compiler_params=pltpu.CompilerParams(vmem_limit_bytes=60 * 2**20),
    )(*arrays)


def block(space, near, nbrs, turns, counts, fields, cotan, kern, dbias, gain, nbias, win, bin_, wout, bout, scale):
    slots, width, _, chans = fields.shape
    hid = win.shape[1]
    hh = hid // 2
    far = space // 2
    main, edge = slots * width * width, slots * 4 * width
    row = lambda v: v.reshape(1, -1)
    anyw = pl.BlockSpec(memory_space=pl.ANY)
    ints = lambda *s: pltpu.SMEM(s, jnp.int32)
    dma = lambda *s: pltpu.SemaphoreType.DMA(s)
    v = lambda dt, *s: pltpu.VMEM(s, dt)
    piece = (2 * chans // near, hh)
    line = (width, chans)
    return pl.pallas_call(
        functools.partial(block_kernel, space, near),
        in_specs=[anyw] * 14,
        out_specs=[anyw] * 5,
        out_shape=[jax.ShapeDtypeStruct(fields.shape, BF16), jax.ShapeDtypeStruct((chans, hid), F32),
                   jax.ShapeDtypeStruct((hid, chans), F32), jax.ShapeDtypeStruct((14, chans), F32),
                   jax.ShapeDtypeStruct((1, hid), F32)],
        scratch_shapes=[
            ints(*nbrs.shape), ints(*turns.shape), ints(*counts.shape), v(F32, 3, 3, chans), v(F32, 1, chans),
            v(F32, 1, chans), v(F32, 1, chans), v(F32, 2, 1, hh), v(F32, 1, chans), v(BF16, chans, hid),
            v(F32, 1, chans), v(BF16, hid, chans),
            v(F32, chans, hid), v(F32, hid, chans), v(F32, 14, chans), v(F32, 1, hid), dma(12), dma(4),
            v(BF16, *fields.shape), v(BF16, *fields.shape), v(F32, slots, (width + 2) * PITCH + 8, chans),
            v(BF16, hid, chans), v(BF16, hid, chans), v(BF16, 2, chans, hh), v(BF16, 2, chans, hh),
            v(F32, main + edge, chans), v(F32, main + edge, chans),
            v(BF16, main + edge, chans), v(BF16, main + edge, chans),
            v(BF16, 2, main + edge, hh), v(BF16, 2, main + edge, hh),
            v(F32, edge, hh), v(F32, edge, hh), v(F32, edge, hh), v(F32, edge, hh),
            v(BF16, edge, hh), v(BF16, edge, hh), v(BF16, edge, hh), v(BF16, edge, hh),
            v(F32, edge, chans), v(F32, edge, chans), v(F32, LAST_ROWS * width, chans), v(F32, LAST_ROWS * width, chans),
            v(F32, slots * width * 8, chans), pltpu.SMEM((space,), jnp.int32),
            v(F32, 2, 2 * chans, hh), v(F32, 13, 8, chans), v(F32, 2, 8, hh), v(BF16, 32, chans),
            v(BF16, 8 * slots, *line), v(BF16, space, *line), v(BF16, space, *line),
            v(BF16, 2, near, *piece), v(BF16, 2, near, *piece), v(BF16, 2, *piece), v(BF16, 2, far, *piece),
            v(BF16, 2, *piece), v(BF16, 2, near, *piece),
            v(BF16, near, 32, chans), v(BF16, 32, chans), v(BF16, far, 32, chans), v(F32, 32, chans),
            dma(2, slots), dma(slots), dma(2), dma(2, 2), dma(2, 2), dma(2, 2), dma(2), dma(2)],
        compiler_params=pltpu.CompilerParams(
            vmem_limit_bytes=61 * 2**20, **(dict(collective_id=0, has_side_effects=True) if COMM else {})),
    )(fields, cotan, nbrs, turns, counts, kern, row(dbias), row(gain), row(nbias), bin_.reshape(2, 1, hh), row(scale),
      win, row(bout), wout)


def local(fields, cotangent, neighbours, rotations, tile_counts, depth_kernel, depth_bias, norm_gain, norm_bias,
          weight_in, bias_in, weight_out, bias_out, layer_scale, shape):
    result, grad_win, grad_wout, channel, bias = publish(*block(
        shape["space"], 2 * shape["dp"], neighbours.T, rotations.T, tile_counts, fields[0], cotangent[0], depth_kernel,
        depth_bias, norm_gain, norm_bias, weight_in, bias_in, weight_out, bias_out, layer_scale))
    return result[None], grad_win, grad_wout, bias.reshape(-1), channel


def solution(mesh):
    placed = P("dp", "space", None, None, None)
    return jax.shard_map(
        functools.partial(local, shape=dict(mesh.shape)),
        mesh=mesh,
        in_specs=(placed, placed) + (P(),) * 12,
        out_specs=(placed, P(), P(), P(), P()),
        check_vma=False,
    )
```

```python
import functools
import math

import jax
import jax.numpy as jnp
from jax import lax
from jax.experimental import pallas as pl
from jax.experimental.pallas import tpu as pltpu
from jax.sharding import PartitionSpec as P

F32, BF16 = jnp.float32, jnp.bfloat16
MESH = pl.DeviceIdType.MESH
PITCH = 64
CONV_ROWS = 12
LAST_ROWS = 16
GROUP = 64
UNROLL = 2
COMM = True


def settle(pieces, sems, device):
    copy = remote(pieces, pieces, sems.at[0], sems.at[1], device)
    copy.wait_send()
    copy.wait_recv()


def over_rows(a):
    return jnp.sum(a.reshape(-1, 8, a.shape[-1]), axis=0)


def contract_rows(a, b):
    return lax.dot_general(a, b, (((0,), (0,)), ((), ())), preferred_element_type=F32)


def remote(src, dst, send_sem, recv_sem, device):
    return pltpu.make_async_remote_copy(
        src_ref=src, dst_ref=dst, send_sem=send_sem, recv_sem=recv_sem, device_id=device, device_id_type=MESH
    )


def loop(lo, hi, body, unroll=1):
    def step(i, c):
        body(i)
        return c

    lax.fori_loop(lo, hi, step, 0, unroll=unroll)


def block_kernel(space, near, fields, cotangent, *refs):
    slots, width, _, chans = fields.shape
    held, outs, scratch = refs[:12], refs[12:17], refs[17:]
    kept, made, rest = scratch[:12], scratch[12:16], scratch[16:]
    in_sem, out_sem = rest[:2]
    first = [pltpu.make_async_copy(held[n], kept[n], in_sem.at[n]) for n in range(12)]
    for n in (9, 11, 0, 1, 2, 3, 4, 5, 6, 7, 8, 10):
        first[n].start()
    last = [pltpu.make_async_copy(made[n], outs[n + 1], out_sem.at[n]) for n in range(4)]
    body(space, near, fields, cotangent, *kept, outs[0], *made, first, last, *rest[2:])


def body(space, near, fields, cotangent, nbrs, turns, counts, taps_w, dbias, gain, nbias, bin_, scale, win, bout, wout,
         out, grad_win, grad_wout, channel_out, bias_out, first, final_copies,
                 tile, cotan, frame, win_t, half_out, wout_t, win_h, nhat_s, inv_s, normed_s, branch_s, act_all, dpre_all,
                 pre_a, pre_b, dact_a, dact_b, act_a, act_b, dpre_a, dpre_b, proj_b, dnorm_b, rows_a, rows_b,
                 cot_s, codes, grads, sums, bsum, small, cand, outgo, income, halves, got, mid, far_got, spread, whole,
                 small_got, small_mid, small_far, parts,
                 load_sem, out_sem, halo_sem, near_sem, far_sem, back_sem, sn_sem, sf_sem):
    slots, width, _, chans = tile.shape
    hid = win.shape[1]
    hh = hid // 2
    area = width * width
    main = slots * area
    m = act_a.shape[0]
    shift = slots.bit_length() - 1
    picks = 4 * slots
    far = space // 2
    if COMM:
        dp, me = lax.axis_index("dp"), lax.axis_index("space")
        core, plane = lax.rem(me, 2), me // 2
        a = dp * 2 + core
    else:
        me = 0
    loads = []
    for t in range(slots):
        loads.append((pltpu.make_async_copy(fields.at[t], tile.at[t], load_sem.at[0, t]),
                      pltpu.make_async_copy(cotangent.at[t], cotan.at[t], load_sem.at[1, t])))
    for t in range(slots):
        loads[t][0].start()
    for t in range(slots):
        loads[t][1].start()

    def near_id(o):
        p = lax.rem(a + o, near)
        return p, (p // 2, plane * 2 + lax.rem(p, 2))

    def far_id(o):
        p = lax.rem(plane + o, far)
        return p, (dp, p * 2 + core)

    if COMM:
        barrier = pltpu.get_barrier_semaphore()
        loop(1, space, lambda o: pl.semaphore_signal(
            barrier, inc=1, device_id=(dp, lax.rem(me + o, space)), device_id_type=MESH))
        loop(1, near, lambda o: pl.semaphore_signal(barrier, inc=1, device_id=near_id(o)[1], device_id_type=MESH))

    for c in first:
        c.wait()
    win_t[...] = win[...].T
    half_out[...] = wout[...] * 0.5
    for h in range(2):
        win_h[h] = win[:, h * hh:(h + 1) * hh]
        wout_t[h] = (wout[h * hh:(h + 1) * hh, :] * 0.5).T
    grads[...] = jnp.zeros_like(grads)
    sums[...] = jnp.zeros_like(sums)
    bsum[...] = jnp.zeros_like(bsum)
    act_b[...] = jnp.zeros_like(act_b)
    dpre_b[...] = jnp.zeros_like(dpre_b)

    def pick_code(k, nbr, turn):
        side = k & 3
        edge = (turn + (side + 2)) & 3
        flip = ((turn + (side & 1)) >> 1) & 1
        return flip * picks + 4 * (nbr & (slots - 1)) + edge

    def scan(o):
        peer = lax.rem(me + o, space)
        hit = jnp.int32(0)
        for k in range(picks):
            nbr = nbrs[k & 3, peer * slots + (k >> 2)]
            hit = jnp.where((nbr >> shift) == me, k, hit)
        slot = peer * slots + (hit >> 2)
        codes[o] = pick_code(hit, nbrs[hit & 3, slot], turns[hit & 3, slot])

    def clear(t):
        frame[t, 0:PITCH, :] = jnp.zeros((PITCH, chans), F32)
        frame[t, pl.ds((width + 1) * PITCH, PITCH + 8), :] = jnp.zeros((PITCH + 8, chans), F32)

        def side(r):
            frame[t, pl.ds(pl.multiple_of((r + 1) * PITCH, 8), 8), :] = jnp.zeros((8, chans), F32)
            frame[t, pl.ds(pl.multiple_of((r + 1) * PITCH + 8 + width, 8), 8), :] = jnp.zeros((8, chans), F32)
            frame[t, pl.ds(pl.multiple_of((r + 1) * PITCH + 8, 8), width), :] = tile[t, r].astype(F32)

        each = space // slots

        def fill(n):
            if COMM:
                scan(t * each + n)
            for r in range(width // each):
                side(n * (width // each) + r)

        loop(0, each, fill)

    def edge_of(k, q):
        t = k
        if q == 0:
            return frame[t, pl.ds(PITCH + 8, width), :]
        if q == 1:
            return frame[t, pl.ds(PITCH + 7 + width, width, stride=PITCH), :]
        if q == 2:
            return frame[t, pl.ds(width * PITCH + 8, width), :]
        return frame[t, pl.ds(PITCH + 8, width, stride=PITCH), :]

    for t in range(slots):
        loads[t][0].wait()
        clear(t)
    i = lax.broadcasted_iota(jnp.int32, (width, width), 0)
    j = lax.broadcasted_iota(jnp.int32, (width, width), 1)
    mirror = (i + j == width - 1).astype(BF16)

    def candidates(t):
        for q in range(4):
            line = edge_of(t, q).astype(BF16)
            cand[4 * t + q] = line
            cand[picks + 4 * t + q] = jnp.dot(mirror, line, preferred_element_type=F32).astype(BF16)

    loop(0, slots, candidates)

    if COMM:
        def gather(o):
            outgo[o] = cand[codes[o]]

        loop(0, space, gather, 4)
        income[me] = outgo[0]
        pl.semaphore_wait(barrier, space + near - 2)

        loop(1, space, lambda o: remote(
            outgo.at[o], income.at[me], halo_sem.at[0], halo_sem.at[1], (dp, lax.rem(me + o, space))).start())

    for t in range(slots):
        loads[t][1].wait()

    count = counts[me]
    px = lax.broadcasted_iota(jnp.int32, (width, chans), 0)
    inner = ((px > 0) & (px < width - 1)).astype(F32)

    def norm_rows(conv, at):
        x = conv - jnp.mean(conv, axis=-1, keepdims=True)
        iv = lax.rsqrt(jnp.mean(x * x, axis=-1, keepdims=True) + 1e-06)
        nhat = x * iv
        sl = pl.ds(pl.multiple_of(at, 16), width)
        inv_s[sl, :] = jnp.broadcast_to(iv, (width, chans))
        nhat_s[sl, :] = nhat
        normed_s[sl, :] = (nhat * gain[...] + nbias[...]).astype(BF16)

    per = width // CONV_ROWS

    def conv_chunk(step):
        t = step // per
        top = (step - t * per) * CONV_ROWS
        live = jnp.where(t < count, 1.0, 0.0)
        kern = [[taps_w[x, y:y + 1, :] for y in range(3)] for x in range(3)]
        bias = dbias[...]
        weigh = scale[...] * inner * live
        s_g = jnp.zeros((8, chans), F32)
        conv = {}
        for fr in range(CONV_ROWS + 2):
            base = (top + fr) * PITCH + 7
            win3 = [frame[t, pl.ds(base + b, width), :] for b in range(3)]
            for x in range(3):
                r = fr - x
                if 0 <= r < CONV_ROWS:
                    acc = conv.get(r, bias)
                    for b in range(3):
                        acc = acc + win3[b] * kern[x][b]
                    conv[r] = acc
            r = fr - 2
            if r >= 0:
                if r in (0, CONV_ROWS - 1):
                    ends = weigh * jnp.where((top + r > 0) & (top + r < width - 1), 1.0, 0.0)
                at = t * area + (top + r) * width
                norm_rows(conv.pop(r), at)
                g = cotan[t, top + r].astype(F32)
                s_g = s_g + over_rows(g)
                sides = (t * width + top + r) * 8
                cot_s[pl.ds(pl.multiple_of(sides, 8), 8), :] = jnp.where(px[0:8] == 0, g[0:8], g[width - 8:width])
                branch_s[pl.ds(pl.multiple_of(at, 16), width), :] = (g * (ends if r in (0, CONV_ROWS - 1) else weigh)).astype(BF16)
        sums[12] += s_g * live

    loop(0, slots * per, conv_chunk)

    def border(t):
        live = jnp.where(t < count, 1.0, 0.0)
        kern = [[taps_w[x, y:y + 1, :] for y in range(3)] for x in range(3)]
        for s in range(4):
            if COMM:
                line = income[nbrs[s, me * slots + t] >> shift]
            else:
                line = cand[pick_code(s, nbrs[s, t], turns[s, t])]
            line = line.astype(F32)
            if s == 0:
                frame[t, pl.ds(8, width), :] = line
            elif s == 1:
                frame[t, pl.ds(PITCH + 8 + width, width, stride=PITCH), :] = line
            elif s == 2:
                frame[t, pl.ds((width + 1) * PITCH + 8, width), :] = line
            else:
                frame[t, pl.ds(PITCH + 7, width, stride=PITCH), :] = line

        for s in range(4):
            acc = dbias[...]
            for x in range(3):
                for b in range(3):
                    if s == 0:
                        w = frame[t, pl.ds(x * PITCH + 7 + b, width), :]
                    elif s == 1:
                        w = frame[t, pl.ds(x * PITCH + 6 + width + b, width, stride=PITCH), :]
                    elif s == 2:
                        w = frame[t, pl.ds((width - 1 + x) * PITCH + 7 + b, width), :]
                    else:
                        w = frame[t, pl.ds(x * PITCH + 7 + b, width, stride=PITCH), :]
                    acc = acc + w * taps_w[x, b:b + 1, :]
            at = main + (t * 4 + s) * width
            norm_rows(acc, at)
            if s == 0:
                g = cotan[t, 0].astype(F32)
            elif s == 1:
                g = cot_s[pl.ds(t * width * 8 + 7, width, stride=8), :] * inner
            elif s == 2:
                g = cotan[t, width - 1].astype(F32)
            else:
                g = cot_s[pl.ds(t * width * 8, width, stride=8), :] * inner
            branch_s[pl.ds(pl.multiple_of(at, 16), width), :] = (g * live * scale[...]).astype(BF16)

    steps = (main + slots * 4 * width) // m
    total = 2 * steps

    def place(k):
        h = k // steps
        return h, pl.ds(pl.multiple_of((k - h * steps) * m, 16), m)

    def ahead(k, pre_s, dact_s):
        h, rows = place(k)
        pre_s[...] = jnp.dot(normed_s[rows, :], win_h[h], preferred_element_type=F32)
        dact_s[...] = jnp.dot(branch_s[rows, :], wout_t[h], preferred_element_type=F32)

    def behind(k, act_s, dpre_s):
        h, rows = place(k)
        act = act_s[...]
        dpre = dpre_s[...]
        act_all[h, rows, :] = act
        dpre_all[h, rows, :] = dpre
        grads[h, 0:chans, :] += contract_rows(normed_s[rows, :], dpre)
        grads[h, chans:2 * chans, :] += contract_rows(branch_s[rows, :], act)

    def hidden(k, pre_s, dact_s, act_s, dpre_s):
        h, _ = place(k)
        bias = bin_[h]
        bs = jnp.zeros((8, hh), F32)
        for q in range(0, m, GROUP):
            sl = pl.ds(q, GROUP)
            pre = pre_s[sl, :] + bias
            twice = lax.erf(pre * (1.0 / math.sqrt(2.0))) + 1.0
            act_s[sl, :] = (pre * twice).astype(BF16)
            bell = jnp.exp2((pre * (-0.5 * math.log2(math.e))) * pre + math.log2(2.0 / math.sqrt(2.0 * math.pi)))
            dpre = dact_s[sl, :] * (twice + pre * bell)
            bs = bs + over_rows(dpre)
            dpre_s[sl, :] = dpre.astype(BF16)
        bsum[h] += bs

    def send_near(h):
        prows = 2 * chans // near
        for p in range(near):
            part = grads[h, p * prows:(p + 1) * prows, :]
            halves[h, p] = (part if p < near // 2 else 0.5 * part).astype(BF16)
        got[h, a] = halves[h, a]

        def go(o):
            p, device = near_id(o)
            remote(halves.at[h, p], got.at[h, a], near_sem.at[h, 0], near_sem.at[h, 1], device).start()

        loop(1, near, go)

    def pass_far(h):
        settle(got.at[h, pl.ds(0, near - 1)], near_sem.at[h], near_id(1)[1])
        tot = got[h, 0].astype(F32)
        for p in range(1, near):
            tot = tot + got[h, p].astype(F32)
        mid[h] = tot.astype(BF16)
        far_got[h, plane] = mid[h]

        def go(o):
            p, device = far_id(o)
            remote(mid.at[h], far_got.at[h, plane], far_sem.at[h, 0], far_sem.at[h, 1], device).start()

        loop(1, far, go)

    def pass_back(h):
        settle(far_got.at[h, pl.ds(0, far - 1)], far_sem.at[h], far_id(1)[1])
        tot = far_got[h, 0].astype(F32)
        for p in range(1, far):
            tot = tot + far_got[h, p].astype(F32)
        spread[h] = tot.astype(BF16)
        whole[h, a] = spread[h]

        def go(o):
            p, device = near_id(o)
            remote(spread.at[h], whole.at[h, a], back_sem.at[h, 0], back_sem.at[h, 1], device).start()

        loop(1, near, go)

    def finish(h):
        settle(whole.at[h, pl.ds(0, near - 1)], back_sem.at[h], near_id(1)[1])
        prows = 2 * chans // near
        hs = slice(h * hh, (h + 1) * hh)
        full = whole[h].reshape(2 * chans, hh).astype(F32)
        grad_win[:, hs] = full[:chans]
        grad_wout[hs, :] = full[chans:].T

    def pair(k):
        behind(jnp.maximum(k - 1, 0), act_b, dpre_b)
        ahead(k + 1, pre_b, dact_b)
        hidden(k, pre_a, dact_a, act_a, dpre_a)
        behind(k, act_a, dpre_a)
        ahead(jnp.minimum(k + 2, total - 1), pre_a, dact_a)
        hidden(k + 1, pre_b, dact_b, act_b, dpre_b)

    def stage(i):
        @pl.when(i == (steps - 3) // (2 * UNROLL))
        def _():
            if COMM:
                settle(income.at[pl.ds(0, space - 1)], halo_sem, (dp, lax.rem(me + 1, space)))
            loop(0, slots, border)

        if COMM:
            @pl.when(i == (steps - 3) // (2 * UNROLL) + 1)
            def _():
                send_near(0)

            @pl.when(i == (steps - 1) // UNROLL - 1)
            def _():
                pass_far(0)

        for n in range(UNROLL):
            pair(2 + 2 * UNROLL * i + 2 * n)

    ahead(0, pre_a, dact_a)
    pair(0)
    loop(0, (steps - 1) // UNROLL, stage)
    behind(total - 1, act_b, dpre_b)
    if COMM:
        send_near(1)
    edge_rows = pl.ds(main, m)
    g_proj = jnp.zeros((8, chans), F32)
    for h in range(2):
        g_proj = g_proj + over_rows(grads[h, chans:2 * chans, :].T * half_out[h * hh:(h + 1) * hh, :].astype(F32))
    parts[...] = jnp.zeros_like(parts)
    parts[13:14, :] = jnp.sum(g_proj, axis=0, keepdims=True) / scale[...]
    b = jnp.sum(bsum[...], axis=1)
    per_h = hh // chans
    for h in range(2):
        for n in range(per_h):
            k = 14 + h * per_h + n
            parts[k:k + 1, :] = b[h:h + 1, n * chans:(n + 1) * chans]
    dnorm_b[...] = jnp.dot(jnp.concatenate([dpre_all[0, edge_rows, :], dpre_all[1, edge_rows, :]], axis=1), win_t[...],
                           preferred_element_type=F32)

    def merge(t):
        for ref in (nhat_s, inv_s):
            for s in (1, 3, 0, 2):
                v = ref[pl.ds(pl.multiple_of(main + (t * 4 + s) * width, 8), width), :]
                if s == 1:
                    ref[pl.ds(t * area + width - 1, width, stride=width), :] = v
                elif s == 3:
                    ref[pl.ds(t * area, width, stride=width), :] = v
                elif s == 0:
                    ref[pl.ds(pl.multiple_of(t * area, 8), width), :] = v
                else:
                    ref[pl.ds(pl.multiple_of(t * area + area - width, 8), width), :] = v

    loop(0, slots, merge)

    lper = width // LAST_ROWS
    lrows = LAST_ROWS * width

    def product(step, both, weight, rows_s):
        rows = pl.ds(pl.multiple_of(step * lrows, 16), lrows)
        rows_s[...] = jnp.dot(jnp.concatenate([both[0, rows, :], both[1, rows, :]], axis=1), weight[...],
                              preferred_element_type=F32)

    def piped(lo, hi, both, weight, use, hook=None):
        product(lo, both, weight, rows_a)

        def pair(j):
            k = lo + 2 * j
            if hook is not None:
                hook(j)
            product(k + 1, both, weight, rows_b)
            use(k, rows_a)
            product(jnp.minimum(k + 2, hi - 1), both, weight, rows_a)
            use(k + 1, rows_b)

        loop(0, (hi - lo) // 2, pair)

    def with_border(t, top, rows_s, edges):
        at = t * 4 * width
        rows_s[pl.ds(width - 1, LAST_ROWS, stride=width), :] = edges[pl.ds(pl.multiple_of(at + width + top, 8), LAST_ROWS), :]
        rows_s[pl.ds(0, LAST_ROWS, stride=width), :] = edges[pl.ds(pl.multiple_of(at + 3 * width + top, 8), LAST_ROWS), :]
        out = []
        for r in range(LAST_ROWS):
            v = rows_s[pl.ds(r * width, width), :]
            if r == 0:
                v = jnp.where(top == 0, edges[pl.ds(pl.multiple_of(at, 8), width), :], v)
            if r == LAST_ROWS - 1:
                v = jnp.where(top == width - LAST_ROWS, edges[pl.ds(pl.multiple_of(at + 2 * width, 8), width), :], v)
            out.append(v)
        return out

    def last(step, rows_s):
        t = step // lper
        top = pl.multiple_of((step - t * lper) * LAST_ROWS, 8)
        start = pl.multiple_of(t * area + top * width, 16)
        dn = with_border(t, top, rows_s, dnorm_b)
        taps = [[jnp.zeros((8, chans), F32)] * 3 for _ in range(3)]
        s_dn = s_dnh = s_dc = jnp.zeros((8, chans), F32)
        dconv = {}
        for fr in range(LAST_ROWS + 2):
            r = fr
            if r < LAST_ROWS:
                sl = pl.ds(pl.multiple_of(start + r * width, 16), width)
                dnorm = dn[r] * gain[...]
                nhat = nhat_s[sl, :]
                dnh = dnorm * nhat
                s_dn = s_dn + over_rows(dnorm)
                s_dnh = s_dnh + over_rows(dnh)
                m1 = jnp.mean(dnorm, axis=-1, keepdims=True)
                m2 = jnp.mean(dnh, axis=-1, keepdims=True)
                dc = inv_s[sl, :] * (dnorm - m1 - nhat * m2)
                s_dc = s_dc + over_rows(dc)
                dconv[r] = dc
            base = (top + fr) * PITCH + 7
            win3 = [frame[t, pl.ds(base + b, width), :] for b in range(3)]
            for x in range(3):
                r = fr - x
                if 0 <= r < LAST_ROWS:
                    for b in range(3):
                        taps[x][b] = taps[x][b] + over_rows(dconv[r] * win3[b])
            dconv.pop(fr - 2, None)
        for n, s in enumerate([taps[x][b] for x in range(3) for b in range(3)] + [s_dc, s_dnh, s_dn]):
            sums[n] += s
    def finalize(step, rows_s):
        t = step // lper
        top = pl.multiple_of((step - t * lper) * LAST_ROWS, 8)
        live = jnp.where(t < count, 1.0, 0.0)
        start = pl.multiple_of(t * area + top * width, 16)
        proj = with_border(t, top, rows_s, proj_b)
        for r in range(LAST_ROWS):
            x = tile[t, top + r].astype(F32)
            tile[t, top + r] = ((x + scale[...] * (proj[r] + bout[...])) * live).astype(BF16)

        @pl.when(top == width - LAST_ROWS)
        def _():
            pltpu.make_async_copy(tile.at[t], out.at[t], out_sem.at[t]).start()

    def small_near(o):
        p, device = near_id(o)
        remote(small, small_got.at[a], sn_sem.at[0], sn_sem.at[1], device).start()

    def finalize_all(lo, hi):
        piped(lo, hi, act_all, half_out, finalize)

    def between(j):
        if COMM:
            @pl.when(j == slots * lper // 2 * 2 // 3)
            def _():
                pass_far(1)
                pass_back(0)

    piped(0, slots * lper, dpre_all, win_t, last, between)

    tot = jnp.sum(sums[...], axis=1)
    parts[0:10, :] = tot[0:10]
    parts[10:12, :] = tot[10:12] / gain[...]
    parts[12:13, :] = tot[12:13] * scale[...]
    parts[13:14, :] += tot[12:13] * bout[...]
    small[...] = parts[...].astype(BF16)
    if COMM:
        small_got[a] = small[...]
        loop(1, near, small_near)

    def write_small(v):
        channel_out[...] = v[0:14]
        for n in range(hid // chans):
            bias_out[:, n * chans:(n + 1) * chans] = v[14 + n:15 + n]

    proj_b[...] = jnp.dot(jnp.concatenate([act_all[0, edge_rows, :], act_all[1, edge_rows, :]], axis=1), half_out[...],
                          preferred_element_type=F32)
    if not COMM:
        write_small(parts[...])
        for h in range(2):
            grad_win[:, h * hh:(h + 1) * hh] = grads[h, 0:chans, :]
            grad_wout[h * hh:(h + 1) * hh, :] = 0.5 * grads[h, chans:2 * chans, :].T
        finalize_all(0, slots * lper)
        for c in final_copies:
            c.start()
        for t in range(slots):
            pltpu.make_async_copy(tile.at[t], out.at[t], out_sem.at[t]).wait()
        for c in final_copies:
            c.wait()
        return

    def small_far_go(o):
        p, device = far_id(o)
        remote(small_mid, small_far.at[plane], sf_sem.at[0], sf_sem.at[1], device).start()

    finalize_all(0, slots * lper // 2)
    settle(small_got.at[pl.ds(0, near - 1)], sn_sem, near_id(1)[1])
    s = small_got[0].astype(F32)
    for p in range(1, near):
        s = s + small_got[p].astype(F32)
    small_mid[...] = s.astype(BF16)
    small_far[plane] = small_mid[...]
    loop(1, far, small_far_go)
    pass_back(1)
    finalize_all(slots * lper // 2, slots * lper)
    finish(0)
    for t in range(slots):
        pltpu.make_async_copy(tile.at[t], out.at[t], out_sem.at[t]).wait()
    finish(1)
    for c in final_copies[:2]:
        c.start()
    settle(small_far.at[pl.ds(0, far - 1)], sf_sem, far_id(1)[1])
    s = small_far[0].astype(F32)
    for p in range(1, far):
        s = s + small_far[p].astype(F32)
    write_small(s)
    for c in final_copies[2:]:
        c.start()
    for c in final_copies:
        c.wait()


def publish_kernel(*refs):
    n = (len(refs) - 1) // 3
    srcs, dsts, held, sems = refs[:n], refs[n:2 * n], refs[2 * n:3 * n], refs[3 * n]
    slots, width = srcs[0].shape[:2]
    third = width // 3
    cuts = [(t, pl.ds(r, third)) for t in range(slots) for r in range(0, width, third)]
    parts = [tuple(ref.at[t, r] for ref in (srcs[0], held[0], dsts[0])) for t, r in cuts]
    parts += list(zip(srcs[1:], held[1:], dsts[1:]))
    ins = [pltpu.make_async_copy(src, mid, sems.at[0, i]) for i, (src, mid, _) in enumerate(parts)]
    outs = [pltpu.make_async_copy(mid, dst, sems.at[1, i]) for i, (_, mid, dst) in enumerate(parts)]
    for c in ins:
        c.start()
    for c, d in zip(ins, outs):
        c.wait()
        d.start()
    for d in outs:
        d.wait()


def publish(*arrays):
    anyw = pl.BlockSpec(memory_space=pl.ANY)
    return pl.pallas_call(
        publish_kernel,
        in_specs=[anyw] * len(arrays),
        out_specs=[anyw] * len(arrays),
        out_shape=[jax.ShapeDtypeStruct(v.shape, v.dtype) for v in arrays],
        scratch_shapes=[pltpu.VMEM(v.shape, v.dtype) for v in arrays]
        + [pltpu.SemaphoreType.DMA((2, 3 * arrays[0].shape[0] + len(arrays) - 1))],
        compiler_params=pltpu.CompilerParams(vmem_limit_bytes=60 * 2**20),
    )(*arrays)


def block(space, near, nbrs, turns, counts, fields, cotan, kern, dbias, gain, nbias, win, bin_, wout, bout, scale):
    slots, width, _, chans = fields.shape
    hid = win.shape[1]
    hh = hid // 2
    far = space // 2
    main, edge = slots * width * width, slots * 4 * width
    row = lambda v: v.reshape(1, -1)
    anyw = pl.BlockSpec(memory_space=pl.ANY)
    ints = lambda *s: pltpu.SMEM(s, jnp.int32)
    dma = lambda *s: pltpu.SemaphoreType.DMA(s)
    v = lambda dt, *s: pltpu.VMEM(s, dt)
    piece = (2 * chans // near, hh)
    line = (width, chans)
    return pl.pallas_call(
        functools.partial(block_kernel, space, near),
        in_specs=[anyw] * 14,
        out_specs=[anyw] * 5,
        out_shape=[jax.ShapeDtypeStruct(fields.shape, BF16), jax.ShapeDtypeStruct((chans, hid), F32),
                   jax.ShapeDtypeStruct((hid, chans), F32), jax.ShapeDtypeStruct((14, chans), F32),
                   jax.ShapeDtypeStruct((1, hid), F32)],
        scratch_shapes=[
            ints(*nbrs.shape), ints(*turns.shape), ints(*counts.shape), v(F32, 3, 3, chans), v(F32, 1, chans),
            v(F32, 1, chans), v(F32, 1, chans), v(F32, 2, 1, hh), v(F32, 1, chans), v(BF16, chans, hid),
            v(F32, 1, chans), v(BF16, hid, chans),
            v(F32, chans, hid), v(F32, hid, chans), v(F32, 14, chans), v(F32, 1, hid), dma(12), dma(4),
            v(BF16, *fields.shape), v(BF16, *fields.shape), v(F32, slots, (width + 2) * PITCH + 8, chans),
            v(BF16, hid, chans), v(BF16, hid, chans), v(BF16, 2, chans, hh), v(BF16, 2, chans, hh),
            v(F32, main + edge, chans), v(F32, main + edge, chans),
            v(BF16, main + edge, chans), v(BF16, main + edge, chans),
            v(BF16, 2, main + edge, hh), v(BF16, 2, main + edge, hh),
            v(F32, edge, hh), v(F32, edge, hh), v(F32, edge, hh), v(F32, edge, hh),
            v(BF16, edge, hh), v(BF16, edge, hh), v(BF16, edge, hh), v(BF16, edge, hh),
            v(F32, edge, chans), v(F32, edge, chans), v(F32, LAST_ROWS * width, chans), v(F32, LAST_ROWS * width, chans),
            v(F32, slots * width * 8, chans), pltpu.SMEM((space,), jnp.int32),
            v(F32, 2, 2 * chans, hh), v(F32, 13, 8, chans), v(F32, 2, 8, hh), v(BF16, 32, chans),
            v(BF16, 8 * slots, *line), v(BF16, space, *line), v(BF16, space, *line),
            v(BF16, 2, near, *piece), v(BF16, 2, near, *piece), v(BF16, 2, *piece), v(BF16, 2, far, *piece),
            v(BF16, 2, *piece), v(BF16, 2, near, *piece),
            v(BF16, near, 32, chans), v(BF16, 32, chans), v(BF16, far, 32, chans), v(F32, 32, chans),
            dma(2, slots), dma(slots), dma(2), dma(2, 2), dma(2, 2), dma(2, 2), dma(2), dma(2)],
        compiler_params=pltpu.CompilerParams(
            vmem_limit_bytes=61 * 2**20, **(dict(collective_id=0, has_side_effects=True) if COMM else {})),
    )(fields, cotan, nbrs, turns, counts, kern, row(dbias), row(gain), row(nbias), bin_.reshape(2, 1, hh), row(scale),
      win, row(bout), wout)


def local(fields, cotangent, neighbours, rotations, tile_counts, depth_kernel, depth_bias, norm_gain, norm_bias,
          weight_in, bias_in, weight_out, bias_out, layer_scale, shape):
    result, grad_win, grad_wout, channel, bias = publish(*block(
        shape["space"], 2 * shape["dp"], neighbours.T, rotations.T, tile_counts, fields[0], cotangent[0], depth_kernel,
        depth_bias, norm_gain, norm_bias, weight_in, bias_in, weight_out, bias_out, layer_scale))
    return result[None], grad_win, grad_wout, bias.reshape(-1), channel


def solution(mesh):
    placed = P("dp", "space", None, None, None)
    return jax.shard_map(
        functools.partial(local, shape=dict(mesh.shape)),
        mesh=mesh,
        in_specs=(placed, placed) + (P(),) * 12,
        out_specs=(placed, P(), P(), P(), P()),
        check_vma=False,
    )
```
